128 devices in a mesh: dp: 16 (over y, x_lo, core), expert: 8 (over z, x_hi).
Axes of the slice: x: 4 (x_hi: 2, x_lo: 2; x = x_hi * 2 + x_lo), y: 4, z: 4, core: 2. Of those that a mesh axis runs over, the one named last changes fastest.
Arguments:
- tokens: bfloat16 [2, 16, 1024, 1024], P(None, 'dp', 'expert'), may hold values from -6 to 6
- cotangent: bfloat16 [2, 16, 1024, 1024], P(None, 'dp', 'expert'), may hold values from -6 to 6
- routes: int32 [2, 16, 1024, 8], P(None, 'dp', 'expert'), may hold values from 0 to 31, all different within a row; in each aligned block of 128 rows (0 to 127, 128 to 255, ..., all dimensions but the last counted through in order) at most 48 rows name the same one
- doc_lengths: int32 [2, 16, 6], P(None, 'dp'), may hold values from 1 to 512, 1024 in all within a row
- valid: int32 [2, 16, 1024], P(None, 'dp', 'expert'), may hold values 0 or 1
- attn_gain: bfloat16 [1024], P(('dp', 'expert')), may hold values from 0.25 to 1.75
- w_query: bfloat16 [1024, 1024], P(('dp', 'expert')), may hold values from -0.1875 to 0.1875
- w_key: bfloat16 [1024, 512], P(('dp', 'expert')), may hold values from -0.1875 to 0.1875
- w_value: bfloat16 [1024, 512], P(('dp', 'expert')), may hold values from -0.1875 to 0.1875
- query_gain: bfloat16 [64], replicated, may hold values from 0.25 to 1.75
- key_gain: bfloat16 [64], replicated, may hold values from 0.25 to 1.75
- w_out: bfloat16 [1024, 1024], P(('dp', 'expert')), may hold values from -1.5 to 1.5
- ffn_gain: bfloat16 [1024], P(('dp', 'expert')), may hold values from 0.25 to 1.75
- w_router: bfloat16 [1024, 32], P(('dp', 'expert')), may hold values from -0.09375 to 0.09375
- w_gate: bfloat16 [32, 1024, 512], P('expert', 'dp'), may hold values from -0.1875 to 0.1875
- w_up: bfloat16 [32, 1024, 512], P('expert', 'dp'), may hold values from -0.1875 to 0.1875
- w_down: bfloat16 [32, 512, 1024], P('expert', 'dp'), may hold values from -1 to 1
Outputs:
- output: bfloat16 [2, 16, 1024, 1024], P(None, 'dp', 'expert')
- tokens_grad: bfloat16 [2, 16, 1024, 1024], P(None, 'dp', 'expert')
- attn_gain_grad: float32 [1024], P(('dp', 'expert'))
- w_query_grad: float32 [1024, 1024], P(('dp', 'expert'))
- w_key_grad: float32 [1024, 512], P(('dp', 'expert'))
- w_value_grad: float32 [1024, 512], P(('dp', 'expert'))
- query_gain_grad: float32 [64], replicated
- key_gain_grad: float32 [64], replicated
- w_out_grad: float32 [1024, 1024], P(('dp', 'expert'))
- ffn_gain_grad: float32 [1024], P(('dp', 'expert'))
- w_router_grad: float32 [1024, 32], P(('dp', 'expert'))
- w_gate_grad: float32 [32, 1024, 512], P('expert', 'dp')
- w_up_grad: float32 [32, 1024, 512], P('expert', 'dp')
- w_down_grad: float32 [32, 512, 1024], P('expert', 'dp')
The draws below stay inside these ranges and needn't reach their ends.
Inputs may be any that keep to these rules, and one draw needn't show every extreme that they name: `routes`: in each aligned block of 128 positions of a sequence, no expert is named more than 48 times; the 8 experts of a token differ. `doc_lengths`: the 6 lengths of a sequence sum to 1024; the largest is exactly half of 1024.
All inputs are finite; a program needn't handle non-finite values. No bound on the sum of `valid` on one device may be relied on, other than what follows from the above.
Results may differ from the reference program's by a relative error of at most 0.02.
Values may be sent and summed in bfloat16 or wider, within the bound.
No kernel may reach another device: no remote copies, remote signals or barrier semaphores. Data moves between devices by JAX's collectives and lax.ppermute only.
A program may use at most 192 MiB of HBM per device.

```python
import math
import jax
import jax.numpy as jnp
import numpy as np
from jax import lax

D = 1024
HQ = 16
KVH = 8
HD = 64
FFE = 512
EXPERTS = 32
TOP = 8
WINDOW = 256
DOCS = 6
MICRO = 2
SEQ_LEN = 1024
SEQS = 16
TOK_MB = 128
CAP = 48
N_EXPERT = 8


def with_ends(values, own_key, low, largest):
    longest = values.shape.index(max(values.shape))
    spots = []
    for shift in (0, 1):
        where = [jax.random.randint(jax.random.fold_in(own_key, axis), (), 0, length) for axis, length in enumerate(values.shape)]
        where[longest] = (where[longest] + shift) % values.shape[longest]
        spots.append(tuple(where))
    return values.at[spots[0]].set(low).at[spots[1]].set(largest)


def steps_of(own_key, extent, split, low, largest):
    def one(position, blocks):
        draws = jax.random.uniform(jax.random.fold_in(jax.random.fold_in(own_key, 6), position), (blocks,), jnp.float32, low / len(split), largest / len(split))
        return jnp.repeat(jnp.exp(draws), extent[position] // blocks).reshape((-1,) + (1,) * (len(extent) - position - 1))

    level = one(*split[0])
    for cut in split[1:]:
        level = level * one(*cut)
    return level


def split_up(amount, total, most, slope):
    weights = [(1 << 20) // math.isqrt(grade ** slope) + 1 for grade in range(2, amount + 1)]
    rest, counts = total - most - (amount - 1), [1] * (amount - 1)
    while rest > 0:
        candidates = [i for i in range(amount - 1) if counts[i] < most]
        pool, left = sum([weights[i] for i in candidates]), rest
        for i in candidates:
            more = min(most - counts[i], max(1, left * weights[i] // pool), rest)
            counts[i] = counts[i] + more
            rest = rest - more
    return np.array([most] + counts)


def ragged_sizes(own_key, amount, total, bound, lean):
    if amount == 2:
        one = jax.random.randint(own_key, (), max(1, total - bound), min(bound, total - 1) + 1)
        return jnp.stack([one, total - one])
    tallies = jnp.asarray(split_up(amount, total, bound, lean), jnp.int32)
    couples = (amount - 1) // 2
    source_of, receiver = tallies[1:1 + 2 * couples:2], tallies[2:2 + 2 * couples:2]
    slack = jnp.minimum(source_of - 1, bound - receiver)
    moved = jax.random.randint(jax.random.fold_in(own_key, 1), (couples,), 0, 1 << 20) % (slack + 1)
    tallies = tallies.at[1:1 + 2 * couples:2].set(source_of - moved).at[2:2 + 2 * couples:2].set(receiver + moved)
    return tallies[jax.random.permutation(jax.random.fold_in(own_key, 2), amount)]


def routed_block(rng, own, number, rows, count, top, reach, lean):
    order = jax.random.permutation(rng, count)
    packed, usual = shares(count, rows * top, reach, lean, True), shares(count, rows * top, reach, lean, False)
    places = jnp.arange(count)

    def named(sizes, turn):
        used = int((sizes > 0).sum())
        fixed = max(1, used // 4)
        passed = fixed + (places - fixed + turn * (used - fixed)) % max(1, count - fixed)
        return jnp.zeros((count,), jnp.int32).at[order[jnp.where(places < fixed, places, passed)]].set(jnp.asarray(sizes, jnp.int32))

    sizes = jnp.where(number % 4 == 0, named(packed, number // 4), named(usual, number - number // 4 - 1))
    mixed = jax.random.permutation(jax.random.fold_in(own, 3), count)
    donor, sink = mixed[0:count // 2 * 2:2], mixed[1:count // 2 * 2:2]
    margin = jnp.minimum(sizes[donor] - 1, reach - sizes[sink]) // 2
    margin = jnp.where((donor == order[0]) | (sink == order[0]) | (sizes[sink] == 0), 0, jnp.maximum(margin, 0))
    passed = jax.random.randint(jax.random.fold_in(own, 4), (count // 2,), 0, 1 << 20) % (margin + 1)
    sizes = sizes.at[donor].add(-passed).at[sink].add(passed)
    labels = jnp.searchsorted(jnp.cumsum(sizes), jnp.arange(rows * top), side="right").astype(jnp.int32)
    table = labels.reshape(top, rows).T
    table = table[jax.random.permutation(jax.random.fold_in(own, 1), rows)]
    turn = jax.random.randint(jax.random.fold_in(own, 2), (rows, 1), 0, top)
    return jnp.take_along_axis(table, (jnp.arange(top)[None, :] + turn) % top, axis=1)


def shares(count, total, limit, skew, full):
    loads = [(1 << 20) // math.isqrt(rank ** skew) + 1 for rank in range(1, count + 1)]
    largest = limit if full else min(limit, max(-(-total // count), total * loads[0] // sum(loads)))
    least = 1 if total - largest >= count - 1 else 0
    holding, rest = [largest] + [least] * (count - 1), total - largest - least * (count - 1)
    while rest > 0:
        free = [i for i in range(1, count) if holding[i] < largest] or [i for i in range(1, count) if holding[i] < limit]
        whole, remaining = sum([loads[i] for i in free]), rest
        for i in free:
            extra = min(limit - holding[i], max(1, remaining * loads[i] // whole), rest)
            holding[i] = holding[i] + extra
            rest = rest - extra
    return np.array(holding)


def noise(rng, shape, width, most, pieces=(), kind=jnp.bfloat16):
    values = width * jax.random.normal(rng, shape, jnp.float32)
    if pieces:
        values = values * steps_of(rng, shape, pieces, -0.22, 0.18)
    return jnp.clip(values, -most, most).astype(kind)


def setup_inputs(seed: int = 0) -> dict:
    key_list = jax.random.split(jax.random.key(seed), 18)
    tokens = noise(key_list[0], (MICRO, SEQS, SEQ_LEN, D), 1.0, 6.0, ((1, 16), (2, 8)))
    cotangent = noise(key_list[1], (MICRO, SEQS, SEQ_LEN, D), 1.0, 6.0, ((1, 16), (2, 8)))
    routes_keys = jax.random.split(jax.random.fold_in(key_list[2], 1), MICRO * SEQS * SEQ_LEN // TOK_MB)
    routes_turns = jax.random.permutation(jax.random.fold_in(key_list[2], 3), MICRO * SEQS * SEQ_LEN // TOK_MB)
    routes = jax.vmap(lambda own, number: routed_block(jax.random.fold_in(key_list[2], 2), own, number, TOK_MB, EXPERTS, TOP, CAP, 1))(routes_keys, routes_turns).reshape((MICRO, SEQS, SEQ_LEN, TOP))
    doc_lengths = jax.vmap(lambda own: ragged_sizes(own, DOCS, SEQ_LEN, SEQ_LEN // 2, 1))(jax.random.split(key_list[3], MICRO * SEQS)).reshape((MICRO, SEQS, DOCS)).astype(jnp.int32)
    valid = with_ends((jax.random.randint(key_list[4], (MICRO, SEQS, SEQ_LEN), 0, 8) < 7).astype(jnp.int32), jax.random.fold_in(key_list[4], 1), 0, 1)
    attn_gain = jnp.clip(1.0 + 0.15 * jax.random.normal(key_list[5], (D,), jnp.float32), 0.25, 1.75).astype(jnp.bfloat16)
    w_query = noise(key_list[6], (D, HQ * HD), D ** -0.5, 0.1875, ((0, 128),))
    w_key = noise(key_list[7], (D, KVH * HD), D ** -0.5, 0.1875, ((0, 128),))
    w_value = noise(key_list[8], (D, KVH * HD), D ** -0.5, 0.1875, ((0, 128),))
    query_gain = jnp.clip(1.0 + 0.15 * jax.random.normal(key_list[9], (HD,), jnp.float32), 0.25, 1.75).astype(jnp.bfloat16)
    key_gain = jnp.clip(1.0 + 0.15 * jax.random.normal(key_list[10], (HD,), jnp.float32), 0.25, 1.75).astype(jnp.bfloat16)
    w_out = noise(key_list[11], (HQ * HD, D), (HQ * HD // 64) ** -0.5, 1.5, ((0, 128),))
    ffn_gain = jnp.clip(1.0 + 0.15 * jax.random.normal(key_list[12], (D,), jnp.float32), 0.25, 1.75).astype(jnp.bfloat16)
    w_router = noise(key_list[13], (D, EXPERTS), (4 * D) ** -0.5, 0.09375, ((0, 128),))
    w_gate = noise(key_list[14], (EXPERTS, D, FFE), D ** -0.5, 0.1875, ((0, 8), (1, 16)))
    w_up = noise(key_list[15], (EXPERTS, D, FFE), D ** -0.5, 0.1875, ((0, 8), (1, 16)))
    w_down = noise(key_list[16], (EXPERTS, FFE, D), (FFE // 16) ** -0.5, 1.0, ((0, 8), (1, 16)))
    return dict(tokens=tokens, cotangent=cotangent, routes=routes, doc_lengths=doc_lengths, valid=valid, attn_gain=attn_gain, w_query=w_query, w_key=w_key, w_value=w_value, query_gain=query_gain, key_gain=key_gain, w_out=w_out, ffn_gain=ffn_gain, w_router=w_router, w_gate=w_gate, w_up=w_up, w_down=w_down)


EPSILON = 1e-06
ROPE_BASE = 10000.0
HIGHEST = lax.Precision.HIGHEST

@jax.custom_vjp
def low(v):
    return lax.optimization_barrier(v.astype(jnp.bfloat16)).astype(jnp.float32)

@jax.custom_vjp
def low_back(v):
    return v

def low_keep(v):
    return (low(v), None)

def low_pass(kept, grad):
    return (grad,)

def back_keep(v):
    return (v, None)

def back_low(kept, grad):
    return (low(grad),)
low.defvjp(low_keep, low_pass)
low_back.defvjp(back_keep, back_low)

def rms_scale(values):
    return lax.rsqrt(lax.optimization_barrier(jnp.mean(values * values, axis=-1, keepdims=True)) + EPSILON)

def rope_tables(positions, head_size):
    half_size = head_size // 2
    frequency = jnp.exp(-math.log(ROPE_BASE) * (2.0 * jnp.arange(half_size, dtype=jnp.float32) / head_size))
    angles = positions.astype(jnp.float32)[:, None] * frequency[None, :]
    angles = jnp.concatenate([angles, angles], axis=-1)
    return (jnp.cos(angles), jnp.sin(angles))

def rotate(values, cosine, sine):
    half_size = values.shape[-1] // 2
    turned = jnp.concatenate([-values[..., half_size:], values[..., :half_size]], axis=-1)
    return values * cosine[:, None, :] + turned * sine[:, None, :]

def hi_dot(left_side, right_side):
    return jnp.dot(left_side, right_side, precision=HIGHEST)

def attention(query_rot, key_rot, value_all, doc_ids):
    seq_rows = query_rot.shape[0]
    block_rows = min(512, seq_rows)
    group_size = HQ // KVH
    score_scale = 1.0 / math.sqrt(HD)
    query_blocks = query_rot.reshape(seq_rows // block_rows, block_rows, KVH, group_size, HD)
    key_pad = jnp.concatenate([jnp.zeros((WINDOW, KVH, HD), jnp.float32), key_rot], axis=0)
    value_pad = jnp.concatenate([jnp.zeros((WINDOW, KVH, HD), jnp.float32), value_all], axis=0)
    doc_pad = jnp.concatenate([-jnp.ones((WINDOW,), jnp.int32), doc_ids], axis=0)

    def one_block(element):
        query_block, first_row = element
        key_block = lax.dynamic_slice_in_dim(key_pad, first_row, block_rows + WINDOW, 0)
        value_block = lax.dynamic_slice_in_dim(value_pad, first_row, block_rows + WINDOW, 0)
        key_docs = lax.dynamic_slice_in_dim(doc_pad, first_row, block_rows + WINDOW, 0)
        query_docs = lax.dynamic_slice_in_dim(doc_ids, first_row, block_rows, 0)
        q_pos = first_row + jnp.arange(block_rows, dtype=jnp.int32)
        k_pos = first_row - WINDOW + jnp.arange(block_rows + WINDOW, dtype=jnp.int32)
        offset = q_pos[:, None] - k_pos[None, :]
        visible = (query_docs[:, None] == key_docs[None, :]) & (offset >= 0) & (offset < WINDOW)
        scores = low_back(jnp.einsum('tkgd,skd->kgts', query_block, key_block, precision=HIGHEST)) * score_scale
        scores = jnp.where(visible[None, None], scores, -1e+30)
        attn_probs = jax.nn.softmax(scores, axis=-1)
        mixed = jnp.einsum('kgts,skd->tkgd', low(attn_probs), value_block, precision=HIGHEST)
        return mixed.reshape(block_rows, HQ * HD)
    starts = jnp.arange(seq_rows // block_rows, dtype=jnp.int32) * block_rows
    result = lax.map(jax.checkpoint(one_block), (query_blocks, starts))
    return result.reshape(seq_rows, HQ * HD)

def sequence_forward(tokens_seq, route_seq, length_seq, weights):
    attn_gain, w_query, w_key, w_value, query_gain, key_gain, w_out, ffn_gain, w_router, w_gate, w_up, w_down = weights
    seq_rows = tokens_seq.shape[0]
    positions = jnp.arange(seq_rows, dtype=jnp.int32)
    bounds = jnp.cumsum(length_seq)
    doc_ids = lax.optimization_barrier(jnp.sum((positions[:, None] >= bounds[None, :]).astype(jnp.int32), axis=1))
    cosine, sine = rope_tables(positions, HD)
    normed = low(tokens_seq * rms_scale(tokens_seq) * attn_gain)
    query = low_back(hi_dot(normed, w_query)).reshape(seq_rows, HQ, HD)
    key_pre = low_back(hi_dot(normed, w_key)).reshape(seq_rows, KVH, HD)
    value_all = low_back(low(hi_dot(normed, w_value))).reshape(seq_rows, KVH, HD)
    query_rot = low(rotate(query * rms_scale(query) * query_gain, cosine, sine))
    key_rot = low(rotate(key_pre * rms_scale(key_pre) * key_gain, cosine, sine))
    attended = low_back(low(attention(query_rot, key_rot, value_all, doc_ids)))
    middle = tokens_seq + low_back(hi_dot(attended, w_out))
    moe_in = low(middle * rms_scale(middle) * ffn_gain)
    logits = low_back(hi_dot(moe_in, w_router))
    chosen = jnp.take_along_axis(logits, route_seq, axis=1)
    gate_probs = jax.nn.softmax(chosen, axis=-1)
    one_hot = (route_seq[:, :, None] == jnp.arange(EXPERTS, dtype=jnp.int32)[None, None, :]).astype(jnp.int32)
    flat_hot = one_hot.reshape(seq_rows * TOP, EXPERTS)
    slot_rank = lax.optimization_barrier(jnp.sum((jnp.cumsum(flat_hot, axis=0) - 1) * flat_hot, axis=1))
    room_size = N_EXPERT * CAP
    slot_ids = (route_seq.reshape(-1) * room_size + slot_rank).astype(jnp.int32)
    outgoing = jnp.zeros((EXPERTS * room_size, D), jnp.float32).at[slot_ids].set(jnp.repeat(moe_in, TOP, axis=0))
    outgoing = outgoing.reshape(EXPERTS, room_size, D)
    gate_pre = low_back(jnp.einsum('ecd,edf->ecf', outgoing, w_gate, precision=HIGHEST))
    up_pre = low_back(jnp.einsum('ecd,edf->ecf', outgoing, w_up, precision=HIGHEST))
    hidden = low(jax.nn.silu(gate_pre) * up_pre)
    expert_out = low_back(low(jnp.einsum('ecf,efd->ecd', hidden, w_down, precision=HIGHEST)))
    picked = expert_out.reshape(EXPERTS * room_size, D)[slot_ids].reshape(seq_rows, TOP, D)
    return middle + lax.optimization_barrier(jnp.sum(gate_probs[:, :, None] * picked, axis=1))

def reference(tokens, cotangent, routes, doc_lengths, valid, attn_gain, w_query, w_key, w_value, query_gain, key_gain, w_out, ffn_gain, w_router, w_gate, w_up, w_down):
    weights = tuple((weight.astype(jnp.float32) for weight in (attn_gain, w_query, w_key, w_value, query_gain, key_gain, w_out, ffn_gain, w_router, w_gate, w_up, w_down)))
    seq_count = MICRO * SEQS
    inputs = tokens.astype(jnp.float32).reshape(seq_count, SEQ_LEN, D)
    route_all = routes.reshape(seq_count, SEQ_LEN, TOP)
    length_all = doc_lengths.reshape(seq_count, DOCS)

    def layer(layer_in, layer_weights):

        def one_step(running, element):
            return (running, jax.checkpoint(sequence_forward)(element[0], element[1], element[2], layer_weights))
        running, result = lax.scan(one_step, jnp.zeros((), jnp.float32), (layer_in, route_all, length_all))
        return result
    result, pullback = jax.vjp(layer, inputs, weights)
    out_seed = (cotangent.astype(jnp.float32) * valid.astype(jnp.float32)[..., None]).reshape(seq_count, SEQ_LEN, D)
    input_grad, weight_grads = pullback(out_seed)
    output = result.reshape(MICRO, SEQS, SEQ_LEN, D).astype(jnp.bfloat16)
    tokens_grad = input_grad.reshape(MICRO, SEQS, SEQ_LEN, D).astype(jnp.bfloat16)
    return (output, tokens_grad, weight_grads[0], weight_grads[1], weight_grads[2], weight_grads[3], weight_grads[4], weight_grads[5], weight_grads[6], weight_grads[7], weight_grads[8], weight_grads[9], weight_grads[10], weight_grads[11])
```

```python
import math

import jax
import jax.numpy as jnp
from jax import lax
from jax.sharding import PartitionSpec as P

WINDOW = 256
EPSILON = 1e-06
ROPE_BASE = 10000.0
CAP = 48

bf16 = jnp.bfloat16
f32 = jnp.float32


def rms_scale(values):
    return lax.rsqrt(jnp.mean(values * values, axis=-1, keepdims=True) + EPSILON)


def rope_tables(positions, head_size):
    half_size = head_size // 2
    frequency = jnp.exp(
        -math.log(ROPE_BASE) * (2.0 * jnp.arange(half_size, dtype=f32) / head_size)
    )
    angles = positions.astype(f32)[:, None] * frequency[None, :]
    angles = jnp.concatenate([angles, angles], axis=-1)
    return (jnp.cos(angles), jnp.sin(angles))


def rotate(values, cosine, sine):
    half_size = values.shape[-1] // 2
    turned = jnp.concatenate([-values[..., half_size:], values[..., :half_size]], axis=-1)
    return values * cosine[:, None, :] + turned * sine[:, None, :]


def rotate_back(upstream, cosine, sine):
    half_size = upstream.shape[-1] // 2
    scaled = upstream * sine[:, None, :]
    turned = jnp.concatenate([scaled[..., half_size:], -scaled[..., :half_size]], axis=-1)
    return upstream * cosine[:, None, :] + turned


def norm_back(upstream, values, scaling):
    return scaling * upstream - values * (scaling * scaling * scaling) * jnp.mean(
        upstream * values, axis=-1, keepdims=True
    )


def product(left_side, right_side):
    return jnp.dot(left_side, right_side, preferred_element_type=f32)


def product_tn(left_side, right_side):
    return lax.dot_general(
        left_side, right_side, (((0,), (0,)), ((), ())), preferred_element_type=f32
    )


def product_nt(left_side, right_side):
    return lax.dot_general(
        left_side, right_side, (((1,), (1,)), ((), ())), preferred_element_type=f32
    )


def einsum(spec, left_side, right_side):
    return jnp.einsum(spec, left_side, right_side, preferred_element_type=f32)


def spread(values, axis):
    count = lax.axis_size(axis)
    return lax.all_to_all(jnp.broadcast_to(values[None], (count,) + values.shape), axis, 0, 0)


def passed_along(value, axis, steps):
    count = lax.axis_size(axis)
    initial, last = (max(0, -steps), min(count, count - steps))
    return lax.ppermute(value, axis, [(source, source + steps) for source in range(initial, last)])


def sum_to_owner(parts):
    count = lax.axis_size("dp")
    half = count // 2
    core = lax.axis_index("dp") % 2
    pairs = parts.reshape((half, 2) + parts.shape[1:])
    kept = lax.dynamic_index_in_dim(pairs, core, 1, keepdims=False)
    sent = lax.dynamic_index_in_dim(pairs, 1 - core, 1, keepdims=False)
    received = lax.ppermute(sent, "dp", [(i, i ^ 1) for i in range(count)])
    both = (kept.astype(f32) + received.astype(f32)).astype(bf16)
    groups = [[2 * i + c for i in range(half)] for c in range(2)]
    arrived = lax.all_to_all(both, "dp", 0, 0, axis_index_groups=groups)
    return jnp.sum(arrived.astype(f32), axis=0)


def body(
    tokens,
    cotangent,
    routes,
    doc_lengths,
    valid,
    attn_gain,
    w_query,
    w_key,
    w_value,
    query_gain,
    key_gain,
    w_out,
    ffn_gain,
    w_router,
    w_gate,
    w_up,
    w_down,
):
    micro = tokens.shape[0]
    rows = tokens.shape[2]
    width = tokens.shape[3]
    head_size = query_gain.shape[0]
    q_width = w_query.shape[1]
    kv_width = w_key.shape[1]
    kv_heads = kv_width // head_size
    q_heads = q_width // head_size
    group_size = q_heads // kv_heads
    experts = w_router.shape[1]
    local = w_gate.shape[0]
    hidden_width = w_gate.shape[2]
    expert_devices = lax.axis_size("expert")
    dp_devices = lax.axis_size("dp")
    own_rows = w_query.shape[0]
    reach_back = (WINDOW + rows - 2) // rows
    key_rows = rows * (reach_back + 1)
    score_scale = 1.0 / math.sqrt(head_size)
    q_gain = query_gain.astype(f32)
    k_gain = key_gain.astype(f32)
    all_rows = micro * rows
    qkv_width = q_width + 2 * kv_width

    gains = jnp.concatenate([attn_gain[:, None], ffn_gain[:, None]], axis=1)
    tail = jnp.concatenate(
        [w_router, gains, jnp.zeros((own_rows, 128 - experts - 2), bf16)], axis=1
    )
    packed = jnp.concatenate([w_query, w_key, w_value, w_out, tail], axis=1)
    packed = spread(packed, "expert").reshape(expert_devices * own_rows, packed.shape[1])
    dense = lax.all_gather(packed, "dp", axis=0, tiled=True)
    qkv_full = dense[:, :qkv_width]
    out_full = dense[:, qkv_width : qkv_width + width]
    router_full = dense[:, qkv_width + width : qkv_width + width + experts]
    gain_attn = dense[:, qkv_width + width + experts].astype(f32)
    gain_ffn = dense[:, qkv_width + width + experts + 1].astype(f32)
    gate_up_full = lax.all_gather(
        jnp.concatenate([w_gate, w_up], axis=2), "dp", axis=1, tiled=True
    )
    down_full = lax.all_gather(w_down, "dp", axis=1, tiled=True)

    seed_low = cotangent[:, 0] * valid[:, 0][:, :, None].astype(bf16)
    out_seed = seed_low.astype(f32).reshape(all_rows, width)
    seed_all = spread(seed_low, "expert").reshape(expert_devices * micro, rows, width)
    routes_all = spread(routes[:, 0], "expert").reshape(expert_devices * micro, rows, -1)
    expert_ids = jnp.arange(experts, dtype=jnp.int32)
    member_all = jnp.any(routes_all[..., None] == expert_ids, axis=2)
    expert_index = lax.axis_index("expert")
    member = lax.dynamic_slice_in_dim(member_all, expert_index * local, local, 2)
    earlier = (
        jnp.arange(rows, dtype=jnp.int32)[:, None] > jnp.arange(rows, dtype=jnp.int32)[None, :]
    ).astype(bf16)
    rank = einsum("ut,btj->bju", earlier, member.astype(bf16)).astype(jnp.int32)
    slots = jnp.where(member.transpose(0, 2, 1), rank, -1)
    picks = slots[:, :, None, :] == jnp.arange(CAP, dtype=jnp.int32)[:, None]
    pick_low = picks.astype(bf16)

    q_pos = expert_index * rows + jnp.arange(rows, dtype=jnp.int32)
    k_pos = (expert_index - reach_back) * rows + jnp.arange(key_rows, dtype=jnp.int32)
    cosine, sine = rope_tables(q_pos, head_size)
    cosine = jnp.concatenate([cosine] * micro, axis=0)
    sine = jnp.concatenate([sine] * micro, axis=0)
    bounds = jnp.cumsum(doc_lengths[:, 0], axis=1)
    q_doc = jnp.sum((q_pos[None, :, None] >= bounds[:, None, :]).astype(jnp.int32), axis=2)
    k_doc = jnp.sum((k_pos[None, :, None] >= bounds[:, None, :]).astype(jnp.int32), axis=2)
    offset = q_pos[:, None] - k_pos[None, :]
    visible = (
        (k_pos[None, None, :] >= 0)
        & (q_doc[:, :, None] == k_doc[:, None, :])
        & (offset >= 0)[None]
        & (offset < WINDOW)[None]
    )[:, None, None]

    x_float = tokens[:, 0].reshape(all_rows, width).astype(f32)
    attn_scale = rms_scale(x_float)
    normed = (x_float * attn_scale * gain_attn).astype(bf16)
    qkv = product(normed, qkv_full)
    query = qkv[:, :q_width].reshape(all_rows, q_heads, head_size)
    key_pre = qkv[:, q_width : q_width + kv_width].reshape(all_rows, kv_heads, head_size)
    value_low = qkv[:, q_width + kv_width :].astype(bf16)
    query_scale = rms_scale(query)
    key_scale = rms_scale(key_pre)
    query_rot = rotate(query * query_scale * q_gain, cosine, sine).astype(bf16)
    key_rot = rotate(key_pre * key_scale * k_gain, cosine, sine).astype(bf16)
    key_value = jnp.concatenate([key_rot.reshape(all_rows, kv_width), value_low], axis=1)
    key_value = key_value.reshape(micro, rows, 2 * kv_width)
    parts = [key_value]
    for distance in range(1, reach_back + 1):
        parts = [passed_along(key_value, "expert", distance)] + parts
    key_value = jnp.concatenate(parts, axis=1)
    keys_all = key_value[..., :kv_width].reshape(micro, key_rows, kv_heads, head_size)
    values_all = key_value[..., kv_width:].reshape(micro, key_rows, kv_heads, head_size)
    query_group = query_rot.reshape(micro, rows, kv_heads, group_size, head_size)
    scores = einsum("mtkgd,mskd->mkgts", query_group, keys_all) * score_scale
    scores = jnp.where(visible, scores, -1e30)
    row_peak = jnp.max(scores, axis=-1, keepdims=True)
    exp_scores = jnp.exp(scores - row_peak)
    attn_probs = exp_scores / jnp.sum(exp_scores, axis=-1, keepdims=True)
    probs_low = attn_probs.astype(bf16)
    attended = einsum("mkgts,mskd->mtkgd", probs_low, values_all)
    attended = attended.reshape(all_rows, q_width).astype(bf16)
    middle = x_float + product(attended, out_full)
    ffn_scale = rms_scale(middle)
    moe_in = (middle * ffn_scale * gain_ffn).astype(bf16)

    moe_all = spread(moe_in.reshape(micro, rows, width), "expert")
    moe_all = moe_all.reshape(expert_devices * micro, rows, width)
    logits_all = einsum("btd,de->bte", moe_all, router_full)
    gates_all = jax.nn.softmax(jnp.where(member_all, logits_all, -1e30), axis=-1)
    gates_all = jnp.where(member_all, gates_all, 0.0)
    gates = lax.dynamic_slice_in_dim(gates_all, expert_index * local, local, 2)
    row_gates = jnp.sum(
        jnp.where(picks, gates.transpose(0, 2, 1)[:, :, None, :], 0.0), axis=-1
    ).transpose(1, 0, 2).reshape(local, -1)
    slot_rows = expert_devices * micro * CAP
    arrived = einsum("bjct,btd->jbcd", pick_low, moe_all).astype(bf16)
    arrived = arrived.reshape(local, slot_rows, width)
    seed_rows = einsum("bjct,btd->jbcd", pick_low, seed_all)
    seed_rows = seed_rows.reshape(local, slot_rows, width)
    out_rows = (row_gates[:, :, None] * seed_rows).astype(bf16)
    pre = einsum("ecd,edf->ecf", arrived, gate_up_full)
    gate_pre = pre[..., :hidden_width]
    up_pre = pre[..., hidden_width:]
    sigma = jax.nn.sigmoid(gate_pre)
    gate_act = gate_pre * sigma
    hidden = (gate_act * up_pre).astype(bf16)
    expert_out = einsum("ecf,efd->ecd", hidden, down_full).astype(bf16).astype(f32)
    row_grads = jnp.sum(expert_out * seed_rows, axis=-1)
    mixed_rows = (row_gates[:, :, None] * expert_out).astype(bf16)
    hidden_grad = einsum("ecd,efd->ecf", out_rows, down_full)
    down_grad = einsum("ecf,ecd->efd", hidden, out_rows).astype(bf16)
    gate_low = (hidden_grad * up_pre * sigma * (1.0 + gate_pre * (1.0 - sigma))).astype(bf16)
    up_low = (hidden_grad * gate_act).astype(bf16)
    pre_low = jnp.concatenate([gate_low, up_low], axis=2)
    gate_up_grad = einsum("ecd,ecf->edf", arrived, pre_low).astype(bf16)
    row_back = einsum("ecf,edf->ecd", pre_low, gate_up_full).astype(bf16)

    blocks = (local, expert_devices * micro, CAP)
    back_part = einsum("bjct,jbcd->btd", pick_low, row_back.reshape(blocks + (width,)))
    back_part = back_part.astype(bf16).reshape(expert_devices, micro, rows, width)
    out_part = einsum("bjct,jbcd->btd", pick_low, mixed_rows.reshape(blocks + (width,)))
    out_part = out_part.astype(bf16).reshape(expert_devices, micro, rows, width)
    row_grads = row_grads.reshape(blocks).transpose(1, 0, 2)
    gate_part = jnp.sum(jnp.where(picks, row_grads[..., None], 0.0), axis=2)
    gate_part = gate_part.reshape(expert_devices, micro, local, rows)
    gate_back = lax.all_to_all(gate_part, "expert", 0, 0)
    moe_back = lax.all_to_all(back_part, "expert", 0, 0)
    out_back = lax.all_to_all(out_part, "expert", 0, 0)

    own_gate_up = sum_to_owner(
        gate_up_grad.reshape(local, dp_devices, -1, 2 * hidden_width).transpose(1, 0, 2, 3)
    )
    own_down = sum_to_owner(down_grad.reshape(local, dp_devices, -1, width).transpose(1, 0, 2, 3))

    gate_grad = gate_back.transpose(1, 3, 0, 2).reshape(all_rows, experts)
    own_member = lax.dynamic_slice_in_dim(member_all, expert_index * micro, micro, 0)
    own_logits = product(moe_in, router_full)
    own_member = own_member.reshape(all_rows, experts)
    own_gates = jax.nn.softmax(jnp.where(own_member, own_logits, -1e30), axis=-1)
    own_gates = jnp.where(own_member, own_gates, 0.0)
    logit_grad = own_gates * (
        gate_grad - jnp.sum(own_gates * gate_grad, axis=-1, keepdims=True)
    )
    logit_grad = logit_grad.astype(bf16)
    router_grad = product_tn(moe_in, logit_grad)
    moe_grad = product_nt(logit_grad, router_full) + jnp.sum(
        moe_back.astype(f32), axis=0
    ).reshape(all_rows, width)
    ffn_gain_grad = jnp.sum(moe_grad * middle * ffn_scale, axis=0)
    mid_grad = out_seed + norm_back(moe_grad * gain_ffn, middle, ffn_scale)
    branch_low = mid_grad.astype(bf16)
    out_grad = product_tn(attended, branch_low)
    attended_grad = product_nt(branch_low, out_full).astype(bf16)
    attended_grad = attended_grad.reshape(micro, rows, kv_heads, group_size, head_size)
    first_sum = sum_to_owner(
        jnp.concatenate(
            [
                out_grad.astype(bf16),
                jnp.concatenate(
                    [router_grad, ffn_gain_grad[:, None], jnp.zeros((width, 128 - experts - 1), f32)],
                    axis=1,
                ).astype(bf16),
            ],
            axis=1,
        ).reshape(dp_devices, expert_devices * own_rows, width + 128)
    )

    prob_grad = einsum("mtkgd,mskd->mkgts", attended_grad, values_all)
    inner = jnp.sum(attn_probs * prob_grad, axis=-1, keepdims=True)
    score_low = (score_scale * attn_probs * (prob_grad - inner)).astype(bf16)
    value_grad = einsum("mkgts,mtkgd->mskd", probs_low, attended_grad)
    query_rot_grad = einsum("mkgts,mskd->mtkgd", score_low, keys_all)
    key_rot_grad = einsum("mkgts,mtkgd->mskd", score_low, query_group)
    both_grad = jnp.concatenate(
        [
            key_rot_grad.reshape(micro, key_rows, kv_width),
            value_grad.reshape(micro, key_rows, kv_width),
        ],
        axis=2,
    )
    start_local = reach_back * rows
    local_grad = both_grad[:, start_local:]
    for distance in range(1, reach_back + 1):
        first_row = (reach_back - distance) * rows
        local_grad = local_grad + passed_along(
            both_grad[:, first_row : first_row + rows].astype(bf16), "expert", -distance
        ).astype(f32)
    local_grad = local_grad.reshape(all_rows, 2 * kv_width)
    value_low_grad = local_grad[:, kv_width:].astype(bf16)
    key_norm_grad = rotate_back(
        local_grad[:, :kv_width].reshape(all_rows, kv_heads, head_size), cosine, sine
    )
    key_gain_grad = jnp.sum(key_norm_grad * key_pre * key_scale, axis=(0, 1))
    key_low = norm_back(key_norm_grad * k_gain, key_pre, key_scale).astype(bf16)
    query_norm_grad = rotate_back(
        query_rot_grad.reshape(all_rows, q_heads, head_size), cosine, sine
    )
    query_gain_grad = jnp.sum(query_norm_grad * query * query_scale, axis=(0, 1))
    query_low = norm_back(query_norm_grad * q_gain, query, query_scale).astype(bf16)
    qkv_low = jnp.concatenate(
        [query_low.reshape(all_rows, q_width), key_low.reshape(all_rows, kv_width), value_low_grad],
        axis=1,
    )
    qkv_grad = product_tn(normed, qkv_low)
    normed_grad = product_nt(qkv_low, qkv_full)
    attn_gain_grad = jnp.sum(normed_grad * x_float * attn_scale, axis=0)
    token_grad = mid_grad + norm_back(normed_grad * gain_attn, x_float, attn_scale)

    head_gains = jnp.concatenate([query_gain_grad, key_gain_grad])
    owners = width // own_rows
    extra = jnp.concatenate(
        [
            jnp.broadcast_to(head_gains[None, None], (owners, 1, 2 * head_size)),
            jnp.pad(
                attn_gain_grad.reshape(owners, 1, own_rows),
                ((0, 0), (0, own_rows - 2), (0, 2 * head_size - own_rows)),
            ),
        ],
        axis=1,
    ).reshape(width, 2 * head_size)
    last_sum = sum_to_owner(
        jnp.concatenate([qkv_grad.astype(bf16), extra.astype(bf16)], axis=1).reshape(
            dp_devices, expert_devices * own_rows, qkv_width + 2 * head_size
        )
    )
    dense_sum = jnp.concatenate([first_sum, last_sum], axis=1).astype(bf16)
    dense_sum = dense_sum.reshape(expert_devices, own_rows, -1)
    owned = jnp.sum(lax.all_to_all(dense_sum, "expert", 0, 0).astype(f32), axis=0)
    out_owned = owned[:, :width]
    router_owned = owned[:, width : width + experts]
    ffn_gain_owned = owned[:, width + experts]
    base = width + 128
    extra_owned = owned[:, base + qkv_width :]

    output = middle + jnp.sum(out_back.astype(f32), axis=0).reshape(all_rows, width)
    return (
        output.astype(bf16).reshape(micro, 1, rows, width),
        token_grad.astype(bf16).reshape(micro, 1, rows, width),
        extra_owned[1, :own_rows],
        owned[:, base : base + q_width],
        owned[:, base + q_width : base + q_width + kv_width],
        owned[:, base + q_width + kv_width : base + qkv_width],
        extra_owned[0, :head_size],
        extra_owned[0, head_size:],
        out_owned,
        ffn_gain_owned,
        router_owned,
        own_gate_up[..., :hidden_width],
        own_gate_up[..., hidden_width:],
        own_down,
    )


def solution(mesh):
    rows_spec = P(("dp", "expert"), None)
    gain_spec = P(("dp", "expert"))
    token_spec = P(None, "dp", "expert", None)
    expert_spec = P("expert", "dp", None)
    return jax.shard_map(
        body,
        mesh=mesh,
        in_specs=(
            token_spec,
            token_spec,
            token_spec,
            P(None, "dp", None),
            P(None, "dp", "expert"),
            gain_spec,
            rows_spec,
            rows_spec,
            rows_spec,
            P(),
            P(),
            rows_spec,
            gain_spec,
            rows_spec,
            expert_spec,
            expert_spec,
            expert_spec,
        ),
        out_specs=(
            token_spec,
            token_spec,
            gain_spec,
            rows_spec,
            rows_spec,
            rows_spec,
            P(),
            P(),
            rows_spec,
            gain_spec,
            rows_spec,
            expert_spec,
            expert_spec,
            expert_spec,
        ),
        check_vma=False,
    )
```

```python
import functools
import math

import jax
import jax.numpy as jnp
from jax import lax
from jax.experimental import pallas as pl
from jax.experimental.pallas import tpu as pltpu
from jax.sharding import PartitionSpec as P

WINDOW = 256
EPSILON = 1e-06
ROPE_BASE = 10000.0
CAP = 48
EXTRA = 16
VMEM = 60 << 20

bf16 = jnp.bfloat16
f32 = jnp.float32


def rms_scale(values):
    return lax.rsqrt(jnp.mean(values * values, axis=-1, keepdims=True) + EPSILON)


def rope_tables(positions, head_size):
    half_size = head_size // 2
    frequency = jnp.exp(
        -math.log(ROPE_BASE) * (2.0 * jnp.arange(half_size, dtype=f32) / head_size)
    )
    angles = positions.astype(f32)[:, None] * frequency[None, :]
    angles = jnp.concatenate([angles, angles], axis=-1)
    return (jnp.cos(angles), jnp.sin(angles))


def norm_back(upstream, values, scaling):
    return scaling * upstream - values * (scaling * scaling * scaling) * jnp.mean(
        upstream * values, axis=-1, keepdims=True
    )


def product(left_side, right_side):
    return jnp.dot(left_side, right_side, preferred_element_type=f32)


def product_tn(left_side, right_side):
    return lax.dot_general(
        left_side, right_side, (((0,), (0,)), ((), ())), preferred_element_type=f32
    )


def product_nt(left_side, right_side):
    return lax.dot_general(
        left_side, right_side, (((1,), (1,)), ((), ())), preferred_element_type=f32
    )


def einsum(spec, left_side, right_side):
    return jnp.einsum(spec, left_side, right_side, preferred_element_type=f32)


def spread(values, axis):
    count = lax.axis_size(axis)
    return lax.all_to_all(jnp.broadcast_to(values[None], (count,) + values.shape), axis, 0, 0)


def passed_along(value, axis, steps):
    count = lax.axis_size(axis)
    initial, last = (max(0, -steps), min(count, count - steps))
    return lax.ppermute(value, axis, [(source, source + steps) for source in range(initial, last)])


def whole(shape):
    return pl.BlockSpec(shape, lambda *_: (0,) * len(shape))


def once(shape):
    return pl.BlockSpec(shape, lambda *_: (0,) * len(shape), pipeline_mode=pl.Buffered(1))


def put_back(turned, pieces):
    column = lax.broadcasted_iota(jnp.int32, (turned.shape[0], CAP), 1)
    hot = [(turned[:, j : j + 1] == column).astype(f32) for j in range(len(pieces))]
    hot = jnp.concatenate(hot, axis=1).astype(bf16)
    return product(hot, jnp.concatenate(pieces, axis=0)).astype(bf16)


def experts_kernel(
    moe_ref,
    seed_ref,
    slots_ref,
    turned_ref,
    member_ref,
    router_ref,
    weights_ref,
    *refs,
):
    back_ref, arrived_ref, out_rows_ref, hidden_ref, pre_ref, mixed_ref = refs[-11:-5]
    taken, seeds, backs, row_gates, row_grads = refs[-5:]
    step = pl.program_id(0)
    blocks, rows, width = moe_ref.shape
    local = taken.shape[0]
    hidden_width = hidden_ref.shape[2]

    def picks(b, j):
        index = lax.broadcasted_iota(jnp.int32, (CAP, rows), 0)
        return slots_ref[b, j : j + 1, :] == index

    @pl.when(step == 0)
    def dispatch():
        for b in range(blocks):
            tokens = moe_ref[b]
            logits = product_nt(router_ref[...], tokens)
            member = member_ref[b] > 0.5
            shown = jnp.where(member, logits, -1e30)
            exps = jnp.where(member, jnp.exp(shown - jnp.max(shown, axis=0, keepdims=True)), 0.0)
            gates = exps / jnp.sum(exps, axis=0, keepdims=True)
            masks = [picks(b, j) for j in range(local)]
            pick = jnp.concatenate([m.astype(f32) for m in masks], axis=0).astype(bf16)
            arrived = product(pick, tokens).astype(bf16)
            seeded = product(pick, seed_ref[b // 2, b % 2, 0]).astype(bf16)
            for j in range(local):
                at = pl.ds(b * CAP, CAP)
                taken[j, at, :] = arrived[j * CAP : (j + 1) * CAP]
                seeds[j, at, :] = seeded[j * CAP : (j + 1) * CAP]
                row_gates[j, at, :] = jnp.sum(
                    jnp.where(masks[j], gates[j : j + 1, :], 0.0), axis=1, keepdims=True
                )

    upper = width // weights_ref.shape[1]
    gate_up_weights = weights_ref[0, :, :upper, :].reshape(width, 2 * hidden_width)
    down_weights = weights_ref[0, :, upper:, :].reshape(hidden_width, width)
    arrived_ref[0] = taken[step]
    pre = product(taken[step], gate_up_weights)
    gate_pre = pre[:, :hidden_width]
    up_pre = pre[:, hidden_width:]
    sigma = 1.0 / (1.0 + jnp.exp(-gate_pre))
    gate_act = gate_pre * sigma
    hidden = (gate_act * up_pre).astype(bf16)
    hidden_ref[0] = hidden
    expert_out = product(hidden, down_weights).astype(bf16).astype(f32)
    seed_rows = seeds[step].astype(f32)
    gate_column = row_gates[step]
    row_grads[step] = jnp.sum(expert_out * seed_rows, axis=1, keepdims=True)
    mixed_ref[0] = (gate_column * expert_out).astype(bf16)
    out_rows = (gate_column * seed_rows).astype(bf16)
    out_rows_ref[0] = out_rows
    hidden_grad = product_nt(out_rows, down_weights)
    gate_low = (hidden_grad * up_pre * sigma * (1.0 + gate_pre * (1.0 - sigma))).astype(bf16)
    up_low = (hidden_grad * gate_act).astype(bf16)
    pre_ref[0, :, :hidden_width] = gate_low
    pre_ref[0, :, hidden_width:] = up_low
    backs[step] = product_nt(pre_ref[0], gate_up_weights).astype(bf16)

    @pl.when(step == local - 1)
    def combine():
        for b in range(blocks):
            at = pl.ds(b * CAP, CAP)
            back_ref[b, :rows, :] = put_back(
                turned_ref[b], [backs[j, at, :] for j in range(local)]
            )
            gate_grads = [
                jnp.sum(jnp.where(picks(b, j), row_grads[j, at, :], 0.0), axis=0, keepdims=True)
                for j in range(local)
            ]
            gate_grads = jnp.concatenate(
                gate_grads + [jnp.zeros((1, width - local * rows), f32)], axis=1
            )
            high = gate_grads.astype(bf16).astype(f32)
            row = lax.broadcasted_iota(jnp.int32, (EXTRA, width), 0)
            back_ref[b, rows:, :] = jnp.where(
                row == 0, high, jnp.where(row == 1, gate_grads - high, 0.0)
            ).astype(bf16)


def run_experts(m, tokens, seeds, slots, turned, member, router, weights, after):
    blocks, rows, width = tokens.shape
    local, owners, each, wide = weights.shape
    hidden_width = wide // 2
    held = blocks * CAP
    shapes = [
        ((blocks, rows + EXTRA, width), bf16),
        ((local, held, width), bf16),
        ((local, held, width), bf16),
        ((local, held, hidden_width), bf16),
        ((local, held, wide), bf16),
        ((local, held, width), bf16),
    ]
    return pl.pallas_call(
        experts_kernel,
        grid=(local,),
        in_specs=[
            once(tokens.shape),
            pl.BlockSpec(
                seeds.shape[:2] + (1,) + seeds.shape[3:],
                lambda j: (0, 0, m, 0, 0),
                pipeline_mode=pl.Buffered(1),
            ),
            picked(slots, m),
            picked(turned, m),
            picked(member, m),
            once(router.shape),
            pl.BlockSpec((1, owners, each, wide), lambda j: (j, 0, 0, 0)),
        ]
        + [pl.BlockSpec(memory_space=pl.ANY)] * len(after),
        out_specs=[once(shapes[0][0])]
        + [pl.BlockSpec((1,) + shape[1:], lambda j: (j, 0, 0)) for shape, _ in shapes[1:]],
        out_shape=[jax.ShapeDtypeStruct(shape, kind) for shape, kind in shapes],
        scratch_shapes=[
            pltpu.VMEM((local, held, width), bf16),
            pltpu.VMEM((local, held, width), bf16),
            pltpu.VMEM((local, held, width), bf16),
            pltpu.VMEM((local, held, 1), f32),
            pltpu.VMEM((local, held, 1), f32),
        ],
        compiler_params=pltpu.CompilerParams(vmem_limit_bytes=VMEM),
        cost_estimate=pl.CostEstimate(
            flops=14 * local * held * width * wide // 4 * 2,
            bytes_accessed=40 << 20,
            transcendentals=local * held * hidden_width,
        ),
        name="experts",
    )(tokens, seeds, slots, turned, member, router, weights, *after)


def weight_grads_kernel(micro, core_ref, *refs):
    kept_ref, sent_ref = refs[-2:]
    parts = [refs[4 * m : 4 * m + 4] for m in range(micro)]
    gate_up = sum(product_tn(p[0][0], p[3][0]) for p in parts)
    down = sum(product_tn(p[2][0], p[1][0]) for p in parts)
    halves = kept_ref.shape[0]
    upper = gate_up.shape[0] // (2 * halves)
    lower = down.shape[0] // (2 * halves)
    gate_up = gate_up.reshape(halves, 2, upper, gate_up.shape[1]).astype(bf16)
    down = down.reshape(halves, 2, lower, down.shape[1]).astype(bf16)

    def place(kept, sent):
        kept_ref[:, 0, :upper, :] = gate_up[:, kept]
        kept_ref[:, 0, upper:, :] = down[:, kept]
        sent_ref[:, 0, :upper, :] = gate_up[:, sent]
        sent_ref[:, 0, upper:, :] = down[:, sent]

    @pl.when(core_ref[0] == 0)
    def even():
        place(0, 1)

    @pl.when(core_ref[0] == 1)
    def odd():
        place(1, 0)


def combine_kernel(m, depth_ref, mixed_ref, turned_ref, *refs):
    outs = refs[-4:]
    local = mixed_ref.shape[0]
    for ahead in range(len(outs)):
        target = lax.rem(depth_ref[0] + ahead, len(outs))
        for x in range(2):
            b = 2 * target + x
            at = pl.ds(pl.multiple_of(b * CAP, CAP), CAP)
            outs[ahead][x] = put_back(
                turned_ref[b], [mixed_ref[j, at, :] for j in range(local)]
            )


def run_combine(m, depth, mixed, turned, after):
    _, blocks, rows, _ = turned.shape
    width = mixed.shape[2]
    shape = (2, rows, width)
    count = blocks // 2
    return pl.pallas_call(
        functools.partial(combine_kernel, m),
        grid=(1,),
        in_specs=[pl.BlockSpec(memory_space=pltpu.SMEM), whole(mixed.shape), picked(turned, m)]
        + [pl.BlockSpec(memory_space=pl.ANY)] * len(after),
        out_specs=[whole(shape)] * count,
        out_shape=[jax.ShapeDtypeStruct(shape, bf16)] * count,
        compiler_params=pltpu.CompilerParams(vmem_limit_bytes=VMEM),
        cost_estimate=pl.CostEstimate(
            flops=2 * blocks * rows * mixed.shape[0] * CAP * width,
            bytes_accessed=5 << 20,
            transcendentals=0,
        ),
        name="combine",
    )(depth, mixed, turned, *after)


def fold_kernel(micro, across_ref, *refs):
    kept_ref, sent_ref = refs[-2:]
    middles, parts = refs[:micro], refs[micro : 5 * micro]

    def place(kept, sent):
        for m in range(micro):
            own = parts[4 * m : 4 * m + 4]
            total = middles[m][...]
            for part in own:
                total = total + part[kept].astype(f32)
            kept_ref[m] = total
            total = own[0][sent].astype(f32)
            for part in own[1:]:
                total = total + part[sent].astype(f32)
            sent_ref[m] = total.astype(bf16)

    @pl.when(across_ref[0] == 0)
    def low_x():
        place(0, 1)

    @pl.when(across_ref[0] == 1)
    def high_x():
        place(1, 0)


def run_fold(across, middles, parts, after):
    micro = len(middles)
    shape = (micro,) + middles[0].shape
    return pl.pallas_call(
        functools.partial(fold_kernel, micro),
        grid=(1,),
        in_specs=[pl.BlockSpec(memory_space=pltpu.SMEM)]
        + [whole(a.shape) for a in (*middles, *parts)]
        + [pl.BlockSpec(memory_space=pl.ANY)] * len(after),
        out_specs=[whole(shape)] * 2,
        out_shape=[jax.ShapeDtypeStruct(shape, f32), jax.ShapeDtypeStruct(shape, bf16)],
        compiler_params=pltpu.CompilerParams(vmem_limit_bytes=VMEM),
        cost_estimate=pl.CostEstimate(flops=4 << 20, bytes_accessed=8 << 20, transcendentals=0),
        name="fold",
    )(across, *middles, *parts, *after)


def pass_kernel(*refs):
    del refs


def pass_on(value, after):
    return pl.pallas_call(
        pass_kernel,
        in_specs=[pl.BlockSpec(memory_space=pl.ANY)] * (1 + len(after)),
        out_specs=pl.BlockSpec(memory_space=pl.ANY),
        out_shape=jax.ShapeDtypeStruct(value.shape, value.dtype),
        input_output_aliases={0: 0},
        compiler_params=pltpu.CompilerParams(vmem_limit_bytes=VMEM),
        cost_estimate=pl.CostEstimate(flops=0, bytes_accessed=0, transcendentals=0),
        name="pass_on",
    )(value, *after)


def weight_grads(core, halves, saved, after):
    local, held, width = saved[0][0].shape
    hidden_width = saved[0][2].shape[2]
    wide = 2 * hidden_width
    depth = (width + hidden_width) // (2 * halves)
    micro = len(saved)
    block = pl.BlockSpec((halves, 1, depth, width), lambda j: (0, j, 0, 0))
    out = jax.ShapeDtypeStruct((halves, local, depth, width), bf16)
    flat = [a for group in saved for a in group]
    return pl.pallas_call(
        functools.partial(weight_grads_kernel, micro),
        grid=(local,),
        in_specs=[pl.BlockSpec(memory_space=pltpu.SMEM)]
        + [pl.BlockSpec((1,) + a.shape[1:], lambda j: (j, 0, 0)) for a in flat]
        + [pl.BlockSpec(memory_space=pl.ANY)] * len(after),
        out_specs=[block, block],
        out_shape=[out, out],
        compiler_params=pltpu.CompilerParams(vmem_limit_bytes=VMEM),
        cost_estimate=pl.CostEstimate(
            flops=2 * len(saved) * local * held * width * (wide + hidden_width),
            bytes_accessed=35 << 20,
            transcendentals=0,
        ),
        name="weight_grads",
    )(core, *flat, *after)


def lanes_like(shape):
    return lax.broadcasted_iota(jnp.int32, shape, len(shape) - 1)


def head_sums(values):
    left = lax.broadcasted_iota(jnp.int32, (128, 128), 0) // 32
    right = lax.broadcasted_iota(jnp.int32, (128, 128), 1) // 32
    ones = (left == right).astype(f32).astype(bf16)
    high = values.astype(bf16)
    rest = (values - high.astype(f32)).astype(bf16)
    return product(high, ones) + product(rest, ones)


def columns(dense, start, size):
    return pl.BlockSpec((dense.shape[0], size), lambda *_: (0, start // size))


def pack_kernel(packed_ref, *refs):
    width = refs[-1].shape[1]
    for n in range(packed_ref.shape[0]):
        rows = packed_ref.shape[1]
        refs[-1][n * rows : (n + 1) * rows, :] = packed_ref[n, :, :width]


def run_pack(packed, width, after):
    count, rows, _ = packed.shape
    return pl.pallas_call(
        pack_kernel,
        grid=(1,),
        in_specs=[whole(packed.shape)] + [pl.BlockSpec(memory_space=pl.ANY)] * len(after),
        out_specs=whole((count * rows, width)),
        out_shape=jax.ShapeDtypeStruct((count * rows, width), packed.dtype),
        compiler_params=pltpu.CompilerParams(vmem_limit_bytes=VMEM),
        cost_estimate=pl.CostEstimate(flops=0, bytes_accessed=1 << 20, transcendentals=0),
        name="pack",
    )(packed, *after)


def group_stack(query_ref, g, q_half):
    lane = lanes_like((1, 256)) % 128 // 32
    pieces = []
    for i in range(4):
        for r in range(2):
            at = r * q_half + g * 256
            block = query_ref[:, at : at + 256]
            pieces.append(jnp.where(lane == i, block, jnp.zeros_like(block)))
    return jnp.concatenate(pieces, axis=0)


def doubled_values(values, h):
    block = values[:, h // 2 * 128 : h // 2 * 128 + 128]
    swapped = pltpu.roll(block, 64, 1)
    low_half = lanes_like(block.shape) < 64
    return jnp.where(low_half == (h % 2 == 0), block, swapped).astype(bf16)


def group_scores(keys, stack, bias, score_scale):
    scores = product_nt(keys, stack) * score_scale
    return scores + jnp.concatenate([bias] * 8, axis=1)


def rotated(u1, u2, cosine, sine, gain1, gain2, head_size):
    scale = lax.rsqrt(head_sums(u1 * u1 + u2 * u2) / head_size + EPSILON)
    u1 = u1 * scale * gain1
    u2 = u2 * scale * gain2
    return (
        (u1 * cosine - u2 * sine).astype(bf16),
        (u2 * cosine + u1 * sine).astype(bf16),
    )


def front_kernel(
    head_size,
    own_ref,
    one_ref,
    two_ref,
    weights_ref,
    out_weights_ref,
    tail_ref,
    cosine_ref,
    sine_ref,
    gains_ref,
    bias_ref,
    *refs,
):
    micro, rows, width = own_ref.shape
    first, rest = refs[-4 * micro - 5 : -4 * micro], refs[-4 * micro :]
    normed_ref, pre_ref, query_ref, key_value_ref, turned_ref = first
    q_width = query_ref.shape[2]
    kv_width = q_width // 2
    groups = kv_width // 256
    score_scale = 1.0 / math.sqrt(head_size)
    turned = tail_ref[...].astype(f32).T
    turned_ref[...] = turned
    gain = turned[33:34, :]
    low_half = lanes_like((rows, 128)) < 64
    head_gains = [gains_ref[n : n + 1, :] for n in range(4)]

    def norm(x):
        return (x * rms_scale(x) * gain).astype(bf16)

    for m in range(micro):
        attended_ref, middle_ref, moe_ref, peak_ref = rest[4 * m : 4 * m + 4]
        x = own_ref[m].astype(f32)
        normed = norm(x)
        normed_ref[m] = normed
        own = product(normed, weights_ref[...])
        pre_ref[m] = own[:, : q_width + kv_width]
        own_rows = pl.ds(2 * rows, rows)
        for at in range(0, q_width, 256):
            made = rotated(
                own[:, at : at + 128], own[:, at + 128 : at + 256],
                cosine_ref[own_rows, :], sine_ref[own_rows, :],
                head_gains[0], head_gains[1], head_size,
            )
            query_ref[m, :, at : at + 128] = made[0]
            query_ref[m, :, at + 128 : at + 256] = made[1]
        earlier = jnp.concatenate(
            [norm(two_ref[m].astype(f32)), norm(one_ref[m].astype(f32))], axis=0
        )
        earlier = product(earlier, weights_ref[:, q_width:])
        both = jnp.concatenate([earlier, own[:, q_width:]], axis=0)
        key_value_ref[m, :, kv_width:] = both[:, kv_width:].astype(bf16)
        for at in range(0, kv_width, 256):
            made = rotated(
                both[:, at : at + 128], both[:, at + 128 : at + 256],
                cosine_ref[...], sine_ref[...], head_gains[2], head_gains[3], head_size,
            )
            key_value_ref[m, :, at : at + 128] = made[0]
            key_value_ref[m, :, at + 128 : at + 256] = made[1]

        bias = bias_ref[m]
        values = key_value_ref[m, :, kv_width:].astype(f32)
        for g in range(groups):
            keys = key_value_ref[m, :, g * 256 : (g + 1) * 256]
            stack = group_stack(query_ref.at[m], g, q_width // 2)
            scores = group_scores(keys, stack, bias, score_scale)
            peak = jnp.max(scores, axis=0, keepdims=True)
            exps = jnp.exp(scores - peak)
            total = jnp.sum(exps, axis=0, keepdims=True)
            probs = (exps * (1.0 / total)).astype(bf16)
            peak_ref[g : g + 1, :] = peak + jnp.log(total)
            for i in range(4):
                h = 4 * g + i
                mixed = product_tn(probs[:, i * 256 : (i + 1) * 256], doubled_values(values, h))
                attended_ref[:, h * 128 : (h + 1) * 128] = jnp.where(
                    low_half, mixed[:rows], mixed[rows:]
                ).astype(bf16)
        middle = x + product(attended_ref[...], out_weights_ref[...])
        middle_ref[...] = middle
        moe_ref[...] = (middle * rms_scale(middle) * turned[32:33, :]).astype(bf16)


def picked(array, m):
    return pl.BlockSpec(
        (None,) + array.shape[1:], lambda *_: (m,) + (0,) * (len(array.shape) - 1)
    )


def run_front(own, one, two, dense, cosine, sine, gains, bias, head_size, q_width, after):
    micro, rows, width = own.shape
    kv_width = q_width // 2
    shapes = [
        ((micro, rows, width), bf16),
        ((micro, rows, q_width + kv_width), f32),
        ((micro, rows, q_width), bf16),
        ((micro, 3 * rows, 2 * kv_width), bf16),
        ((128, width), f32),
    ] + [
        ((rows, q_width), bf16),
        ((rows, width), f32),
        ((rows, width), bf16),
        ((8, 8 * rows), f32),
    ] * micro
    small = (cosine, sine, gains, bias)
    return pl.pallas_call(
        functools.partial(front_kernel, head_size),
        grid=(1,),
        in_specs=[whole(own.shape)] * 3
        + [
            columns(dense, 0, 2 * q_width),
            columns(dense, 2 * q_width, width),
            columns(dense, 2 * q_width + width, 128),
        ]
        + [whole(a.shape) for a in small]
        + [pl.BlockSpec(memory_space=pl.ANY)] * len(after),
        out_specs=[whole(shape) for shape, _ in shapes],
        out_shape=[jax.ShapeDtypeStruct(shape, kind) for shape, kind in shapes],
        compiler_params=pltpu.CompilerParams(vmem_limit_bytes=VMEM),
        cost_estimate=pl.CostEstimate(
            flops=2 * micro * rows * width * 5 * q_width
            + 4 * micro * rows * q_width * 3 * rows * 4,
            bytes_accessed=20 << 20,
            transcendentals=16 * micro * rows * 3 * rows,
        ),
        name="front",
    )(own, one, two, dense, dense, dense, *small, *after)


def add_kernel(left_ref, right_ref, *refs):
    refs[-1][...] = (left_ref[...].astype(f32) + right_ref[...].astype(f32)).astype(bf16)


def total_kernel(parts_ref, *refs):
    total = parts_ref[0].astype(f32)
    for n in range(1, parts_ref.shape[0]):
        total = total + parts_ref[n].astype(f32)
    refs[-1][...] = total


def run_total(parts, after):
    return pl.pallas_call(
        total_kernel,
        grid=(1,),
        in_specs=[whole(parts.shape)] + [pl.BlockSpec(memory_space=pl.ANY)] * len(after),
        out_specs=whole(parts.shape[1:]),
        out_shape=jax.ShapeDtypeStruct(parts.shape[1:], f32),
        compiler_params=pltpu.CompilerParams(vmem_limit_bytes=VMEM),
        cost_estimate=pl.CostEstimate(
            flops=parts.size, bytes_accessed=2 * parts.size, transcendentals=0
        ),
        name="total",
    )(parts, *after)


def add_low(left, right, each, after=()):
    block = pl.BlockSpec((each,) + left.shape[1:], lambda i: (i,) + (0,) * (left.ndim - 1))
    return pl.pallas_call(
        add_kernel,
        grid=(left.shape[0] // each,),
        in_specs=[block, block] + [pl.BlockSpec(memory_space=pl.ANY)] * len(after),
        out_specs=block,
        out_shape=jax.ShapeDtypeStruct(left.shape, bf16),
        compiler_params=pltpu.CompilerParams(vmem_limit_bytes=VMEM),
        cost_estimate=pl.CostEstimate(
            flops=left.size, bytes_accessed=6 * left.size, transcendentals=0
        ),
        name="add_low",
    )(left, right, *after)


def middle_back_kernel(
    score_scale,
    passing,
    parts_ref,
    member_ref,
    seed_ref,
    query_ref,
    key_value_ref,
    bias_ref,
    moe_ref,
    middle_ref,
    peak_ref,
    out_weights_ref,
    turned_ref,
    *refs,
):
    (
        mid_grad_ref,
        branch_ref,
        router_grad_ref,
        query_grad_ref,
        own_grad_ref,
        one_grad_ref,
        two_grad_ref,
    ) = refs[-8:-1] if passing else refs[-7:]
    rows, width = middle_ref.shape
    kv_width = key_value_ref.shape[1] // 2
    groups = kv_width // 256
    experts = member_ref.shape[0]
    senders = parts_ref.shape[0]
    router = turned_ref[:experts, :].astype(bf16)
    moe_in = moe_ref[...]
    member = member_ref[...] > 0.5
    shown = jnp.where(member, product_nt(router, moe_in), -1e30)
    exps = jnp.where(member, jnp.exp(shown - jnp.max(shown, axis=0, keepdims=True)), 0.0)
    gates = exps / jnp.sum(exps, axis=0, keepdims=True)
    gate_grad = []
    for s in range(senders):
        row = parts_ref[s, rows:, :].astype(f32)
        row = row[0:1] + row[1:2]
        for j in range(experts // senders):
            gate_grad.append(row[:, j * rows : (j + 1) * rows])
    gate_grad = jnp.concatenate(gate_grad, axis=0)
    logit_grad = gates * (gate_grad - jnp.sum(gates * gate_grad, axis=0, keepdims=True))
    logit_grad = logit_grad.astype(bf16)
    moe_grad = product_tn(logit_grad, router)
    for s in range(senders):
        moe_grad = moe_grad + parts_ref[s, :rows, :].astype(f32)
    middle = middle_ref[...]
    scale = rms_scale(middle)
    router_grad_ref[:experts, :] = product(logit_grad, moe_in)
    router_grad_ref[experts : experts + 1, :] = jnp.sum(
        moe_grad * middle * scale, axis=0, keepdims=True
    )
    mid_grad = seed_ref[...].astype(f32) + norm_back(
        moe_grad * turned_ref[32:33, :], middle, scale
    )
    mid_grad_ref[...] = mid_grad
    branch = mid_grad.astype(bf16)
    branch_ref[...] = branch
    attended_grad = product_nt(branch, out_weights_ref[...]).astype(bf16)

    bias = bias_ref[...]
    grads3 = (two_grad_ref, one_grad_ref, own_grad_ref)
    values = key_value_ref[:, kv_width:].astype(f32)
    low_half = lanes_like((rows, 128)) < 64
    low_rows = lanes_like((3 * rows, 128)) < 64
    lane = lanes_like((1, 256)) % 128 // 32
    q_half = query_ref.shape[1] // 2
    for g in range(groups):
        keys = key_value_ref[:, g * 256 : (g + 1) * 256]
        stack = group_stack(query_ref, g, q_half)
        scores = group_scores(keys, stack, bias, score_scale)
        probs = jnp.exp(scores - peak_ref[g : g + 1, :])
        probs_low = probs.astype(bf16)
        prob_grads, value_grads = [], []
        for i in range(4):
            h = 4 * g + i
            block = attended_grad[:, h * 128 : (h + 1) * 128]
            zero = jnp.zeros_like(block)
            masked = jnp.concatenate(
                [jnp.where(low_half, block, zero), jnp.where(low_half, zero, block)], axis=0
            )
            prob_grads.append(product_nt(doubled_values(values, h), masked))
            both = product(probs_low[:, i * 256 : (i + 1) * 256], masked)
            value_grads.append(both + pltpu.roll(both, 64, 1))
        prob_grad = jnp.concatenate(prob_grads, axis=1)
        inner = jnp.sum(probs * prob_grad, axis=0, keepdims=True)
        score_low = (score_scale * probs * (prob_grad - inner)).astype(bf16)
        for pair in range(2):
            merged = jnp.where(low_rows, value_grads[2 * pair], value_grads[2 * pair + 1])
            at = kv_width + (2 * g + pair) * 128
            for n in range(3):
                grads3[n][:, at : at + 128] = merged[n * rows : (n + 1) * rows].astype(
                    grads3[n].dtype
                )
        key_grad = product(score_low, stack)
        for n in range(3):
            grads3[n][:, g * 256 : (g + 1) * 256] = key_grad[n * rows : (n + 1) * rows].astype(
                grads3[n].dtype
            )
        spread_grad = product_tn(score_low, keys)
        for r in range(2):
            total = jnp.zeros((rows, 256), f32)
            for i in range(4):
                at = (2 * i + r) * rows
                total = jnp.where(lane == i, spread_grad[at : at + rows], total)
            at = r * q_half + g * 256
            query_grad_ref[:, at : at + 256] = total


def run_middle_back(
    m, parts, member, seeds, query, key_value, bias, moe_in, middle, peak, dense, turned,
    score_scale, after, passed,
):
    _, rows, width = seeds.shape
    q_width = query.shape[2]
    shapes = [
        ((rows, width), f32),
        ((rows, width), bf16),
        ((40, width), f32),
        ((rows, q_width), f32),
        ((rows, q_width), f32),
        ((rows, q_width), bf16),
        ((rows, q_width), bf16),
    ]
    first = (member, seeds, query, key_value, bias)
    second = (moe_in, middle, peak)
    return pl.pallas_call(
        functools.partial(middle_back_kernel, score_scale, bool(passed)),
        grid=(1,),
        in_specs=[whole(parts.shape)]
        + [picked(a, m) for a in first]
        + [whole(a.shape) for a in second]
        + [columns(dense, 2 * q_width, width), whole(turned.shape)]
        + [pl.BlockSpec(memory_space=pl.ANY)] * (len(after) + len(passed)),
        out_specs=[whole(shape) for shape, _ in shapes]
        + [pl.BlockSpec(memory_space=pl.ANY)] * len(passed),
        out_shape=[jax.ShapeDtypeStruct(shape, kind) for shape, kind in shapes]
        + [jax.ShapeDtypeStruct(a.shape, a.dtype) for a in passed],
        input_output_aliases={11 + len(after) + n: len(shapes) + n for n in range(len(passed))},
        compiler_params=pltpu.CompilerParams(vmem_limit_bytes=VMEM),
        cost_estimate=pl.CostEstimate(
            flops=2 * rows * q_width * width + 10 * 16 * rows * 3 * rows * 256,
            bytes_accessed=10 << 20,
            transcendentals=16 * rows * 3 * rows,
        ),
        name="middle_back",
    )(parts, *first, *second, dense, turned, *after, *passed)


def by_core(core_ref, values, kept_ref, sent_ref, at):
    halves, depth = kept_ref.shape[0], kept_ref.shape[1]
    pairs = values.reshape(halves, 2, depth, values.shape[1])
    columns = pl.ds(at, values.shape[1])

    @pl.when(core_ref[0] == 0)
    def even():
        kept_ref[:, :, columns] = pairs[:, 0]
        sent_ref[:, :, columns] = pairs[:, 1]

    @pl.when(core_ref[0] == 1)
    def odd():
        kept_ref[:, :, columns] = pairs[:, 1]
        sent_ref[:, :, columns] = pairs[:, 0]


def out_grads_kernel(micro, core_ref, *refs):
    kept_ref, sent_ref = refs[-2:]
    attended, branch, router = refs[:micro], refs[micro : 2 * micro], refs[2 * micro : 3 * micro]
    width = branch[0].shape[1]
    out_grad = sum(product_tn(a[...], b[...]) for a, b in zip(attended, branch))
    by_core(core_ref, out_grad.astype(bf16), kept_ref, sent_ref, 0)
    tail = sum(r[...] for r in router)
    tail = jnp.concatenate([tail, jnp.zeros((128 - tail.shape[0], width), f32)], axis=0)
    by_core(core_ref, tail.T.astype(bf16), kept_ref, sent_ref, width)


def run_out_grads(core, halves, attended, branch, router, after):
    width = branch[0].shape[1]
    micro = len(branch)
    out = jax.ShapeDtypeStruct((halves, width // (2 * halves), width + 128), bf16)
    return pl.pallas_call(
        functools.partial(out_grads_kernel, micro),
        grid=(1,),
        in_specs=[pl.BlockSpec(memory_space=pltpu.SMEM)]
        + [whole(a.shape) for a in (*attended, *branch, *router)]
        + [pl.BlockSpec(memory_space=pl.ANY)] * len(after),
        out_specs=[whole(out.shape)] * 2,
        out_shape=[out, out],
        compiler_params=pltpu.CompilerParams(vmem_limit_bytes=VMEM),
        cost_estimate=pl.CostEstimate(
            flops=2 * 256 * width * width, bytes_accessed=4 << 20, transcendentals=0
        ),
        name="out_grads",
    )(core, *attended, *branch, *router, *after)


def head_back(u1, u2, up1, up2, cosine, sine, gain1, gain2, head_size):
    back1 = up1 * cosine + up2 * sine
    back2 = up2 * cosine - up1 * sine
    scale = lax.rsqrt(head_sums(u1 * u1 + u2 * u2) / head_size + EPSILON)
    sum1 = jnp.sum(back1 * u1 * scale, axis=0, keepdims=True)
    sum2 = jnp.sum(back2 * u2 * scale, axis=0, keepdims=True)
    back1 = back1 * gain1
    back2 = back2 * gain2
    mean = head_sums(back1 * u1 + back2 * u2) / head_size
    cube = scale * scale * scale
    low1 = (scale * back1 - u1 * cube * mean).astype(bf16)
    low2 = (scale * back2 - u2 * cube * mean).astype(bf16)
    return low1, low2, sum1, sum2


def query_back_kernel(
    head_size, micro, core_ref, pre_ref, normed_ref, cosine_ref, sine_ref, gains_ref, weights_ref,
    out_kept_ref, out_sent_ref, *refs,
):
    query_grads = refs[:micro]
    kept_ref, sent_ref, normed_grad_ref, sums_ref, low = refs[-5:]
    _, rows, width = normed_ref.shape
    q_width = query_grads[0].shape[1]
    base = out_kept_ref.shape[2]
    kept_ref[:, :, :base] = out_kept_ref[...]
    sent_ref[:, :, :base] = out_sent_ref[...]
    sums = [jnp.zeros((1, 128), f32) for _ in range(2)]
    for m in range(micro):
        at_rows = pl.ds(m * rows, rows)
        for at in range(0, q_width, 256):
            low1, low2, sum1, sum2 = head_back(
                pre_ref[m, :, at : at + 128], pre_ref[m, :, at + 128 : at + 256],
                query_grads[m][:, at : at + 128], query_grads[m][:, at + 128 : at + 256],
                cosine_ref[...], sine_ref[...], gains_ref[0:1, :], gains_ref[1:2, :], head_size,
            )
            low[at_rows, at : at + 128] = low1
            low[at_rows, at + 128 : at + 256] = low2
            sums = [sums[0] + sum1, sums[1] + sum2]
    sums_ref[...] = jnp.concatenate(sums + [jnp.zeros((6, 128), f32)], axis=0)
    normed = jnp.concatenate([normed_ref[m] for m in range(micro)], axis=0)
    for at in range(0, q_width, 512):
        grad = product_tn(normed, low[:, at : at + 512]).astype(bf16)
        by_core(core_ref, grad, kept_ref, sent_ref, base + at)
    normed_grad_ref[...] = product_nt(low[...], weights_ref[...])


def run_query_back(
    core, pre, normed, cosine, sine, gains, dense, out_grads, query_grads, head_size, after
):
    micro, rows, width = normed.shape
    q_width = query_grads[0].shape[1]
    shape = out_grads[0].shape[:2] + (out_grads[0].shape[2] + q_width,)
    out = jax.ShapeDtypeStruct(shape, bf16)
    ins = (pre, normed, cosine, sine, gains)
    rest = (*out_grads, *query_grads)
    return pl.pallas_call(
        functools.partial(query_back_kernel, head_size, micro),
        grid=(1,),
        in_specs=[pl.BlockSpec(memory_space=pltpu.SMEM)]
        + [whole(a.shape) for a in ins]
        + [columns(dense, 0, q_width)]
        + [whole(a.shape) for a in rest]
        + [pl.BlockSpec(memory_space=pl.ANY)] * len(after),
        out_specs=[whole(shape), whole(shape), whole((micro * rows, width)), whole((8, 128))],
        out_shape=[
            out,
            out,
            jax.ShapeDtypeStruct((micro * rows, width), f32),
            jax.ShapeDtypeStruct((8, 128), f32),
        ],
        scratch_shapes=[pltpu.VMEM((micro * rows, q_width), bf16)],
        compiler_params=pltpu.CompilerParams(vmem_limit_bytes=VMEM),
        cost_estimate=pl.CostEstimate(
            flops=4 * micro * rows * width * q_width, bytes_accessed=15 << 20, transcendentals=0
        ),
        name="query_back",
    )(core, *ins, dense, *rest, *after)


def tokens_back_kernel(
    head_size, micro, core_ref, pre_ref, normed_ref, tokens_ref, cosine_ref, sine_ref, gains_ref,
    weights_ref, turned_ref, normed_grad_ref, sums_ref, *refs,
):
    kept_ref, sent_ref, tokens_grad_ref, low = refs[-4:]
    own_grads, mid_grads, ones, twos = [refs[n * micro : (n + 1) * micro] for n in range(4)]
    _, rows, width = normed_ref.shape
    kv_width = own_grads[0].shape[1] // 2
    q_width = pre_ref.shape[2] - kv_width
    sums = [jnp.zeros((1, 128), f32) for _ in range(2)]
    for m in range(micro):
        at_rows = pl.ds(m * rows, rows)

        def upstream(start, size):
            columns = pl.ds(start, size)
            return (
                own_grads[m][:, columns]
                + ones[m][:, columns].astype(f32)
                + twos[m][:, columns].astype(f32)
            )

        low[at_rows, kv_width:] = upstream(kv_width, kv_width).astype(bf16)
        for at in range(0, kv_width, 256):
            from_pre = q_width + at
            low1, low2, sum1, sum2 = head_back(
                pre_ref[m, :, from_pre : from_pre + 128],
                pre_ref[m, :, from_pre + 128 : from_pre + 256],
                upstream(at, 128), upstream(at + 128, 128),
                cosine_ref[...], sine_ref[...], gains_ref[2:3, :], gains_ref[3:4, :], head_size,
            )
            low[at_rows, at : at + 128] = low1
            low[at_rows, at + 128 : at + 256] = low2
            sums = [sums[0] + sum1, sums[1] + sum2]
    normed = jnp.concatenate([normed_ref[m] for m in range(micro)], axis=0)
    for at in range(0, low.shape[1], 512):
        grad = product_tn(normed, low[:, at : at + 512]).astype(bf16)
        by_core(core_ref, grad, kept_ref, sent_ref, at)
    normed_grad = normed_grad_ref[...] + product_nt(low[...], weights_ref[...])
    gain = turned_ref[33:34, :]
    gain_grad = jnp.zeros((1, width), f32)
    for m in range(micro):
        x = tokens_ref[m].astype(f32)
        scale = rms_scale(x)
        part = normed_grad[m * rows : (m + 1) * rows]
        gain_grad = gain_grad + jnp.sum(part * x * scale, axis=0, keepdims=True)
        tokens_grad_ref[m] = (mid_grads[m][...] + norm_back(part * gain, x, scale)).astype(bf16)
    folded = []
    for total in [sums_ref[0:1, :], sums_ref[1:2, :]] + sums:
        total = total + pltpu.roll(total, 64, 1)
        folded.append(total + pltpu.roll(total, 32, 1))
    lane = lanes_like((1, 128))
    query_row = jnp.where(lane < 96, folded[0], folded[1])
    key_row = jnp.where(lane < 96, folded[2], folded[3])
    column = jnp.concatenate([gain_grad, jnp.zeros((127, width), f32)], axis=0).T
    row = lax.broadcasted_iota(jnp.int32, (width, 128), 0)
    extra = jnp.where(
        lanes_like((width, 128)) < 64, column, jnp.where(row % 2 == 0, query_row, key_row)
    )
    by_core(core_ref, extra.astype(bf16), kept_ref, sent_ref, low.shape[1])


def run_tokens_back(
    core, pre, normed, tokens, cosine, sine, gains, dense, turned, normed_grad, sums,
    own_grads, mid_grads, ones, twos, owners, head_size, after,
):
    micro, rows, width = tokens.shape
    wide = own_grads[0].shape[1]
    shape = (owners // 2, width // owners, wide + 128)
    out = jax.ShapeDtypeStruct(shape, bf16)
    ins = (pre, normed, tokens, cosine, sine, gains)
    rest = (turned, normed_grad, sums, *own_grads, *mid_grads, *ones, *twos)
    return pl.pallas_call(
        functools.partial(tokens_back_kernel, head_size, micro),
        grid=(1,),
        in_specs=[pl.BlockSpec(memory_space=pltpu.SMEM)]
        + [whole(a.shape) for a in ins]
        + [columns(dense, 2 * wide - wide, wide)]
        + [whole(a.shape) for a in rest]
        + [pl.BlockSpec(memory_space=pl.ANY)] * len(after),
        out_specs=[whole(shape), whole(shape), whole(tokens.shape)],
        out_shape=[out, out, jax.ShapeDtypeStruct(tokens.shape, bf16)],
        scratch_shapes=[pltpu.VMEM((micro * rows, wide), bf16)],
        compiler_params=pltpu.CompilerParams(vmem_limit_bytes=VMEM),
        cost_estimate=pl.CostEstimate(
            flops=4 * micro * rows * width * wide, bytes_accessed=15 << 20, transcendentals=0
        ),
        name="tokens_back",
    )(core, *ins, dense, *rest, *after)


def totals_kernel(*refs):
    at = 0
    for ref in refs[:-1]:
        total = ref[0].astype(f32)
        for n in range(1, ref.shape[0]):
            total = total + ref[n].astype(f32)
        refs[-1][:, at : at + ref.shape[2]] = total.astype(bf16)
        at += ref.shape[2]


def run_totals(parts):
    shape = (parts[0].shape[1], sum(p.shape[2] for p in parts))
    return pl.pallas_call(
        totals_kernel,
        grid=(1,),
        in_specs=[whole(p.shape) for p in parts],
        out_specs=whole(shape),
        out_shape=jax.ShapeDtypeStruct(shape, bf16),
        compiler_params=pltpu.CompilerParams(vmem_limit_bytes=VMEM),
        cost_estimate=pl.CostEstimate(flops=2 << 20, bytes_accessed=4 << 20, transcendentals=0),
        name="totals",
    )(*parts)


def body(
    tokens,
    cotangent,
    routes,
    doc_lengths,
    valid,
    attn_gain,
    w_query,
    w_key,
    w_value,
    query_gain,
    key_gain,
    w_out,
    ffn_gain,
    w_router,
    w_gate,
    w_up,
    w_down,
):
    micro = tokens.shape[0]
    rows = tokens.shape[2]
    width = tokens.shape[3]
    head_size = query_gain.shape[0]
    q_width = w_query.shape[1]
    kv_width = w_key.shape[1]
    kv_heads = kv_width // head_size
    q_heads = q_width // head_size
    group_size = q_heads // kv_heads
    experts = w_router.shape[1]
    local = w_gate.shape[0]
    hidden_width = w_gate.shape[2]
    upper = w_gate.shape[1]
    expert_devices = lax.axis_size("expert")
    dp_devices = lax.axis_size("dp")
    own_rows = w_query.shape[0]
    reach_back = (WINDOW + rows - 2) // rows
    key_rows = rows * (reach_back + 1)
    score_scale = 1.0 / math.sqrt(head_size)
    q_gain = query_gain.astype(f32)
    k_gain = key_gain.astype(f32)
    all_rows = micro * rows
    qkv_width = q_width + 2 * kv_width

    tiles = 128 // (head_size // 2)
    halves = dp_devices // 2
    core = lax.axis_index("dp") % 2
    core_flag = core[None].astype(jnp.int32)
    expert_index = lax.axis_index("expert")
    across, depth = expert_index % 2, expert_index // 2
    other_core = [(i, i ^ 1) for i in range(dp_devices)]
    other_across = [(i, i ^ 1) for i in range(expert_devices)]
    along_depth = [[2 * z + x for z in range(expert_devices // 2)] for x in range(2)]

    groups = kv_heads // 4
    half_size = head_size // 2
    query_cols = w_query.reshape(own_rows, groups, 4, group_size, 2, half_size)
    query_cols = query_cols.transpose(0, 3, 1, 4, 2, 5).reshape(own_rows, q_width)
    key_cols = w_key.reshape(own_rows, groups, 4, 2, half_size)
    key_cols = key_cols.transpose(0, 1, 3, 2, 4).reshape(own_rows, kv_width)
    tail = jnp.concatenate(
        [
            w_router,
            ffn_gain[:, None],
            attn_gain[:, None],
            jnp.zeros((own_rows, 128 - experts - 2), bf16),
        ],
        axis=1,
    )
    route_cols = routes[:, 0].astype(bf16).reshape(own_rows, -1)
    packed = jnp.concatenate([query_cols, key_cols, w_value, w_out, tail, route_cols], axis=1)
    packed = spread(packed, "expert")
    dense_width = packed.shape[2] - route_cols.shape[1]
    routes_all = packed[:, :, dense_width:].astype(jnp.int32)
    routes_all = routes_all.reshape((expert_devices,) + routes.shape[:1] + routes.shape[2:])
    seed_low = cotangent[:, 0] * valid[:, 0][:, :, None].astype(bf16)
    seed_other = lax.ppermute(seed_low, "expert", other_across)
    x_low = tokens[:, 0]
    one = passed_along(x_low, "expert", 1)
    two = passed_along(x_low, "expert", 2)
    dense = run_pack(packed, dense_width, (one, two))
    dense = lax.all_gather(dense, "dp", axis=0, tiled=True)
    weights = jnp.concatenate([jnp.concatenate([w_gate, w_up], axis=2), w_down], axis=1)
    weights = lax.all_gather(weights, "dp", axis=1)

    def by_depth(values, other=None):
        if other is None:
            other = lax.ppermute(values, "expert", other_across)
        pair = jnp.where(
            across == 0, jnp.stack([values, other]), jnp.stack([other, values])
        )
        pair = jnp.broadcast_to(pair[None], (expert_devices // 2,) + pair.shape)
        return lax.all_to_all(pair, "expert", 0, 0, axis_index_groups=along_depth)

    seed_all = by_depth(seed_low, seed_other)
    expert_ids = jnp.arange(experts, dtype=jnp.int32)
    member_all = jnp.any(routes_all[..., None] == expert_ids, axis=3)
    member_turned = jnp.roll(member_all, -expert_index * local, axis=3).transpose(1, 0, 3, 2)
    member = member_turned[:, :, :local]
    earlier = (
        jnp.arange(rows, dtype=jnp.int32)[:, None] < jnp.arange(rows, dtype=jnp.int32)[None, :]
    ).astype(bf16)
    rank = einsum("mbjt,tu->mbju", member.astype(bf16), earlier).astype(jnp.int32)
    slots = jnp.where(member, rank, -1)
    turned_slots = slots.transpose(0, 1, 3, 2)
    member_turned = member_turned.astype(f32)
    own_member = jnp.any(routes[:, 0, :, :, None] == expert_ids, axis=2)
    own_member = own_member.transpose(0, 2, 1).astype(f32)

    q_pos = expert_index * rows + jnp.arange(rows, dtype=jnp.int32)
    k_pos = (expert_index - reach_back) * rows + jnp.arange(key_rows, dtype=jnp.int32)
    cosine, sine = rope_tables(k_pos, head_size)
    cosine = jnp.tile(cosine[:, :half_size], (1, tiles))
    sine = jnp.tile(sine[:, :half_size], (1, tiles))
    bounds = jnp.cumsum(doc_lengths[:, 0], axis=1)
    q_doc = jnp.sum((q_pos[None, :, None] >= bounds[:, None, :]).astype(jnp.int32), axis=2)
    k_doc = jnp.sum((k_pos[None, :, None] >= bounds[:, None, :]).astype(jnp.int32), axis=2)
    offset = q_pos[None, :] - k_pos[:, None]
    visible = (
        (k_pos[None, :, None] >= 0)
        & (q_doc[:, None, :] == k_doc[:, :, None])
        & (offset >= 0)[None]
        & (offset < WINDOW)[None]
    )
    bias = jnp.where(visible, 0.0, -1e30).astype(f32)
    head_gains = jnp.stack(
        [
            jnp.tile(part, tiles)
            for part in (
                q_gain[:half_size],
                q_gain[half_size:],
                k_gain[:half_size],
                k_gain[half_size:],
            )
        ]
        + [jnp.zeros((128,), f32)] * 4
    )

    result = run_front(
        x_low, one, two, dense, cosine, sine, head_gains, bias, head_size, q_width, ()
    )
    normed, pre, query, key_value, turned = result[:5]
    attended, middle, moe_in, peak = [result[5 + n :: 4] for n in range(4)]
    cosine, sine = cosine[-rows:], sine[-rows:]

    router_turned = jnp.roll(turned[:experts], -expert_index * local, axis=0).astype(bf16)
    saved, backs, mixed = [], [], []
    moe_all = [by_depth(moe_in[m]).reshape(expert_devices, rows, width) for m in range(micro)]
    for m in range(micro):
        back_part, arrived, out_rows, hidden, pre_low, mixed_rows = run_experts(
            m, moe_all[m], seed_all, slots, turned_slots, member_turned, router_turned, weights,
            tuple(mixed),
        )
        saved.append((arrived, out_rows, hidden, pre_low))
        backs.append(lax.all_to_all(back_part, "expert", 0, 0))
        mixed.append(mixed_rows)
    kept, sent = weight_grads(core_flag, halves, saved, (backs[0],))
    mid_grads, branches, router_grads, query_grads, own_grads, ones, twos = ([] for _ in range(7))
    for m in range(micro):
        result = run_middle_back(
            m, backs[m], own_member, seed_low, query, key_value, bias, moe_in[m], middle[m],
            peak[m], dense, turned, score_scale, (kept, backs[1]) if m == 0 else (),
            (sent,) if m == 0 else (),
        )
        if m == 0:
            sent = lax.ppermute(result[7], "dp", other_core)
        else:
            core_sum = add_low(kept, sent, 2, (result[0],))
        mid_grads.append(result[0])
        branches.append(result[1])
        router_grads.append(result[2])
        query_grads.append(result[3])
        own_grads.append(result[4])
        ones.append(passed_along(result[5], "expert", -1))
        twos.append(passed_along(result[6], "expert", -2))
    across_low = lax.axis_index("dp") // 2 % 2
    along_y = [[4 * y + place for y in range(dp_devices // 4)] for place in range(4)]
    summed = lax.psum_scatter(
        core_sum.reshape((dp_devices // 4, 2) + core_sum.shape[1:]),
        "dp",
        scatter_dimension=0,
        axis_index_groups=along_y,
    )
    own_expert = lax.dynamic_index_in_dim(summed, across_low, 0, keepdims=False)
    expert_other = lax.dynamic_index_in_dim(summed, 1 - across_low, 0, keepdims=False)
    expert_other = lax.ppermute(expert_other, "dp", [(i, i ^ 2) for i in range(dp_devices)])
    own_expert = own_expert.astype(f32) + expert_other.astype(f32)

    same_core = [[2 * i + c for i in range(halves)] for c in range(2)]

    def over_dp(kept, sent, each):
        both = add_low(kept, lax.ppermute(sent, "dp", other_core), each)
        return both, lax.all_to_all(both, "dp", 0, 0, axis_index_groups=same_core)

    out_grads = run_out_grads(core_flag, halves, attended, branches, router_grads, (core_sum,))
    kept_in, sent_in, normed_grad, gain_sums = run_query_back(
        core_flag, pre, normed, cosine, sine, head_gains, dense, out_grads, query_grads,
        head_size, (),
    )
    first_both, first_parts = over_dp(kept_in, sent_in, 4)

    out_parts = []
    for m in range(micro):
        made = run_combine(
            m, depth[None].astype(jnp.int32), mixed[m], turned_slots, (first_both,)
        )
        got = [made[0]]
        for ahead in range(1, expert_devices // 2):
            pairs = [(i, (i + 2 * ahead) % expert_devices) for i in range(expert_devices)]
            got.append(lax.ppermute(made[ahead], "expert", pairs))
        out_parts.append(got)

    kept_in, sent_in, token_grad = run_tokens_back(
        core_flag, pre, normed, x_low, cosine, sine, head_gains, dense, turned, normed_grad,
        gain_sums, own_grads, mid_grads, ones, twos, dp_devices, head_size, (),
    )
    sent_in = pass_on(sent_in, (first_parts, *out_parts[0][1:], *out_parts[1][1:]))
    both, last_parts = over_dp(kept_in, sent_in, 4)
    out_kept, out_sent = run_fold(
        across[None].astype(jnp.int32), middle, out_parts[0] + out_parts[1], (both,)
    )
    out_other = lax.ppermute(out_sent, "expert", other_across)
    dense_sum = run_totals((first_parts, last_parts)).reshape(expert_devices, own_rows, -1)
    owned = run_total(lax.all_to_all(dense_sum, "expert", 0, 0), (expert_other,))
    output = out_kept + out_other.astype(f32)

    base = width + 128
    query_owned = owned[:, base : base + q_width]
    query_owned = query_owned.reshape(own_rows, group_size, groups, 2, 4, half_size)
    query_owned = query_owned.transpose(0, 2, 4, 1, 3, 5).reshape(own_rows, q_width)
    key_owned = owned[:, base + q_width : base + q_width + kv_width]
    key_owned = key_owned.reshape(own_rows, groups, 2, 4, half_size)
    key_owned = key_owned.transpose(0, 1, 3, 2, 4).reshape(own_rows, kv_width)
    extra_owned = owned[:, base + qkv_width :]
    return (
        output.astype(bf16).reshape(micro, 1, rows, width),
        token_grad.reshape(micro, 1, rows, width),
        extra_owned[:, 0],
        query_owned,
        key_owned,
        owned[:, base + q_width + kv_width : base + qkv_width],
        extra_owned[0, head_size:],
        extra_owned[1, head_size:],
        owned[:, :width],
        owned[:, width + experts],
        owned[:, width : width + experts],
        own_expert[:, :upper, :hidden_width],
        own_expert[:, :upper, hidden_width:],
        own_expert[:, upper:],
    )


def solution(mesh):
    rows_spec = P(("dp", "expert"), None)
    gain_spec = P(("dp", "expert"))
    token_spec = P(None, "dp", "expert", None)
    expert_spec = P("expert", "dp", None)
    return jax.shard_map(
        body,
        mesh=mesh,
        in_specs=(
            token_spec,
            token_spec,
            token_spec,
            P(None, "dp", None),
            P(None, "dp", "expert"),
            gain_spec,
            rows_spec,
            rows_spec,
            rows_spec,
            P(),
            P(),
            rows_spec,
            gain_spec,
            rows_spec,
            expert_spec,
            expert_spec,
            expert_spec,
        ),
        out_specs=(
            token_spec,
            token_spec,
            gain_spec,
            rows_spec,
            rows_spec,
            rows_spec,
            P(),
            P(),
            rows_spec,
            gain_spec,
            rows_spec,
            expert_spec,
            expert_spec,
            expert_spec,
        ),
        check_vma=False,
    )
```

```python
import functools
import math

import jax
import jax.numpy as jnp
from jax import lax
from jax.experimental import pallas as pl
from jax.experimental.pallas import tpu as pltpu
from jax.sharding import PartitionSpec as P

WINDOW = 256
EPSILON = 1e-06
ROPE_BASE = 10000.0
CAP = 48
EXTRA = 16
VMEM = 60 << 20
PIECES = 2
LIGHT = pl.CostEstimate(flops=1, bytes_accessed=1, transcendentals=0)

bf16 = jnp.bfloat16
f32 = jnp.float32


def rms_scale(values):
    return lax.rsqrt(jnp.mean(values * values, axis=-1, keepdims=True) + EPSILON)


def rope_tables(positions, head_size):
    half_size = head_size // 2
    frequency = jnp.exp(
        -math.log(ROPE_BASE) * (2.0 * jnp.arange(half_size, dtype=f32) / head_size)
    )
    angles = positions.astype(f32)[:, None] * frequency[None, :]
    angles = jnp.concatenate([angles, angles], axis=-1)
    return (jnp.cos(angles), jnp.sin(angles))


def norm_back(upstream, values, scaling):
    return scaling * upstream - values * (scaling * scaling * scaling) * jnp.mean(
        upstream * values, axis=-1, keepdims=True
    )


def product(left_side, right_side):
    return jnp.dot(left_side, right_side, preferred_element_type=f32)


def product_tn(left_side, right_side):
    return lax.dot_general(
        left_side, right_side, (((0,), (0,)), ((), ())), preferred_element_type=f32
    )


def product_nt(left_side, right_side):
    return lax.dot_general(
        left_side, right_side, (((1,), (1,)), ((), ())), preferred_element_type=f32
    )


def einsum(spec, left_side, right_side):
    return jnp.einsum(spec, left_side, right_side, preferred_element_type=f32)


def spread(values, axis):
    count = lax.axis_size(axis)
    return lax.all_to_all(jnp.broadcast_to(values[None], (count,) + values.shape), axis, 0, 0)


def passed_along(value, axis, steps):
    count = lax.axis_size(axis)
    initial, last = (max(0, -steps), min(count, count - steps))
    return lax.ppermute(value, axis, [(source, source + steps) for source in range(initial, last)])


def whole(shape):
    return pl.BlockSpec(shape, lambda *_: (0,) * len(shape))


def once(shape):
    return pl.BlockSpec(shape, lambda *_: (0,) * len(shape), pipeline_mode=pl.Buffered(1))


def put_back(turned, pieces):
    column = lax.broadcasted_iota(jnp.int32, (turned.shape[0], CAP), 1)
    hot = [(turned[:, j : j + 1] == column).astype(f32) for j in range(len(pieces))]
    hot = jnp.concatenate(hot, axis=1).astype(bf16)
    return product(hot, jnp.concatenate(pieces, axis=0)).astype(bf16)


def experts_kernel(
    moe_ref,
    seed_ref,
    slots_ref,
    turned_ref,
    member_ref,
    router_ref,
    weights_ref,
    *refs,
):
    back_ref, arrived_ref, out_rows_ref, hidden_ref, pre_ref, mixed_ref = refs[-11:-5]
    taken, seeds, backs, row_gates, row_grads = refs[-5:]
    step = pl.program_id(0)
    blocks, rows, width = moe_ref.shape
    local = taken.shape[0]
    hidden_width = hidden_ref.shape[2]

    def picks(b, j):
        index = lax.broadcasted_iota(jnp.int32, (CAP, rows), 0)
        return slots_ref[b, j : j + 1, :] == index

    @pl.when(step == 0)
    def dispatch():
        for b in range(blocks):
            tokens = moe_ref[b]
            logits = product_nt(router_ref[...], tokens)
            member = member_ref[b] > 0.5
            shown = jnp.where(member, logits, -1e30)
            exps = jnp.where(member, jnp.exp(shown - jnp.max(shown, axis=0, keepdims=True)), 0.0)
            gates = exps / jnp.sum(exps, axis=0, keepdims=True)
            masks = [picks(b, j) for j in range(local)]
            pick = jnp.concatenate([m.astype(f32) for m in masks], axis=0).astype(bf16)
            arrived = product(pick, tokens).astype(bf16)
            seeded = product(pick, seed_ref[b // 2, b % 2, 0]).astype(bf16)
            for j in range(local):
                at = pl.ds(b * CAP, CAP)
                taken[j, at, :] = arrived[j * CAP : (j + 1) * CAP]
                seeds[j, at, :] = seeded[j * CAP : (j + 1) * CAP]
                row_gates[j, at, :] = jnp.sum(
                    jnp.where(masks[j], gates[j : j + 1, :], 0.0), axis=1, keepdims=True
                )

    def expert():
        upper = width // weights_ref.shape[1]
        gate_up_weights = weights_ref[0, :, :upper, :].reshape(width, 2 * hidden_width)
        down_weights = weights_ref[0, :, upper:, :].reshape(hidden_width, width)
        arrived_ref[0] = taken[step]
        pre = product(taken[step], gate_up_weights)
        gate_pre = pre[:, :hidden_width]
        up_pre = pre[:, hidden_width:]
        sigma = 1.0 / (1.0 + jnp.exp(-gate_pre))
        gate_act = gate_pre * sigma
        hidden = (gate_act * up_pre).astype(bf16)
        hidden_ref[0] = hidden
        expert_out = product(hidden, down_weights).astype(bf16).astype(f32)
        seed_rows = seeds[step].astype(f32)
        gate_column = row_gates[step]
        row_grads[step] = jnp.sum(expert_out * seed_rows, axis=1, keepdims=True)
        mixed_ref[0] = (gate_column * expert_out).astype(bf16)
        out_rows = (gate_column * seed_rows).astype(bf16)
        out_rows_ref[0] = out_rows
        hidden_grad = product_nt(out_rows, down_weights)
        gate_low = (hidden_grad * up_pre * sigma * (1.0 + gate_pre * (1.0 - sigma))).astype(bf16)
        up_low = (hidden_grad * gate_act).astype(bf16)
        pre_ref[0, :, :hidden_width] = gate_low
        pre_ref[0, :, hidden_width:] = up_low
        backs[step] = product_nt(pre_ref[0], gate_up_weights).astype(bf16)

    expert()

    @pl.when(step == local - 1)
    def combine():
        for b in range(blocks):
            at = pl.ds(b * CAP, CAP)
            back_ref[b, :rows, :] = put_back(
                turned_ref[b], [backs[j, at, :] for j in range(local)]
            )
            gate_grads = [
                jnp.sum(jnp.where(picks(b, j), row_grads[j, at, :], 0.0), axis=0, keepdims=True)
                for j in range(local)
            ]
            gate_grads = jnp.concatenate(
                gate_grads + [jnp.zeros((1, width - local * rows), f32)], axis=1
            )
            high = gate_grads.astype(bf16).astype(f32)
            row = lax.broadcasted_iota(jnp.int32, (EXTRA, width), 0)
            back_ref[b, rows:, :] = jnp.where(
                row == 0, high, jnp.where(row == 1, gate_grads - high, 0.0)
            ).astype(bf16)


def run_experts(m, tokens, seeds, slots, turned, member, router, weights, after):
    blocks, rows, width = tokens.shape
    local, owners, each, wide = weights.shape
    hidden_width = wide // 2
    held = blocks * CAP
    shapes = [
        ((blocks, rows + EXTRA, width), bf16),
        ((local, held, width), bf16),
        ((local, held, width), bf16),
        ((local, held, hidden_width), bf16),
        ((local, held, wide), bf16),
        ((local, held, width), bf16),
    ]
    return pl.pallas_call(
        experts_kernel,
        grid=(local,),
        in_specs=[
            once(tokens.shape),
            pl.BlockSpec(
                seeds.shape[:2] + (1,) + seeds.shape[3:],
                lambda j: (0, 0, m, 0, 0),
                pipeline_mode=pl.Buffered(1),
            ),
            picked(slots, m),
            picked(turned, m),
            picked(member, m),
            once(router.shape),
            pl.BlockSpec((1, owners, each, wide), lambda j: (j, 0, 0, 0)),
        ]
        + [pl.BlockSpec(memory_space=pl.ANY)] * len(after),
        out_specs=[once(shapes[0][0])]
        + [pl.BlockSpec((1,) + shape[1:], lambda j: (j, 0, 0)) for shape, _ in shapes[1:]],
        out_shape=[jax.ShapeDtypeStruct(shape, kind) for shape, kind in shapes],
        scratch_shapes=[
            pltpu.VMEM((local, held, width), bf16),
            pltpu.VMEM((local, held, width), bf16),
            pltpu.VMEM((local, held, width), bf16),
            pltpu.VMEM((local, held, 1), f32),
            pltpu.VMEM((local, held, 1), f32),
        ],
        compiler_params=pltpu.CompilerParams(vmem_limit_bytes=VMEM),
        cost_estimate=LIGHT,
        name="experts",
    )(tokens, seeds, slots, turned, member, router, weights, *after)


def weight_grads_kernel(micro, adding, core_ref, *refs):
    del core_ref
    parts = [refs[4 * m : 4 * m + 4] for m in range(micro)]
    gate_up = sum(product_tn(p[0][0], p[3][0]) for p in parts)
    down = sum(product_tn(p[2][0], p[1][0]) for p in parts)
    outs = refs[-1:] if adding else refs[-PIECES:]
    owners = sum(ref.shape[0] for ref in outs)
    upper = gate_up.shape[0] // owners
    gate_up = gate_up.reshape(owners, upper, gate_up.shape[1])
    down = down.reshape(owners, down.shape[0] // owners, down.shape[1])
    each = owners // PIECES
    for n in range(PIECES):
        part = slice(n * each, (n + 1) * each)
        above, below = gate_up[part], down[part]
        if adding:
            received_ref = refs[4 * micro + n]
            above = above + received_ref[:, 0, :upper, :].astype(f32)
            below = below + received_ref[:, 0, upper:, :].astype(f32)
            outs[0][part, 0, :upper, :] = above.astype(bf16)
            outs[0][part, 0, upper:, :] = below.astype(bf16)
        else:
            outs[n][:, 0, :upper, :] = above.astype(bf16)
            outs[n][:, 0, upper:, :] = below.astype(bf16)


def combine_kernel(micro, passing, depth_ref, *refs):
    mixed, turned = refs[:micro], refs[micro]
    outs = refs[-4 - passing : len(refs) - passing]
    local = mixed[0].shape[0]
    for ahead in range(len(outs)):
        target = lax.rem(depth_ref[0] + ahead, len(outs))
        for x in range(2):
            b = 2 * target + x
            at = pl.ds(pl.multiple_of(b * CAP, CAP), CAP)
            for m in range(micro):
                outs[ahead][x, m] = put_back(
                    turned[m, b], [mixed[m][j, at, :] for j in range(local)]
                )


def run_combine(depth, mixed, turned, after, passed):
    micro, blocks, rows, _ = turned.shape
    width = mixed[0].shape[2]
    shape = (2, micro, rows, width)
    count = blocks // 2
    return pl.pallas_call(
        functools.partial(combine_kernel, micro, len(passed)),
        grid=(1,),
        in_specs=[pl.BlockSpec(memory_space=pltpu.SMEM)]
        + [whole(a.shape) for a in (*mixed, turned)]
        + [pl.BlockSpec(memory_space=pl.ANY)] * (len(after) + len(passed)),
        out_specs=[whole(shape)] * count + [pl.BlockSpec(memory_space=pl.ANY)] * len(passed),
        out_shape=[jax.ShapeDtypeStruct(shape, bf16)] * count
        + [jax.ShapeDtypeStruct(a.shape, a.dtype) for a in passed],
        input_output_aliases={2 + micro + len(after) + n: count + n for n in range(len(passed))},
        compiler_params=pltpu.CompilerParams(vmem_limit_bytes=VMEM),
        cost_estimate=LIGHT,
        name="combine",
    )(depth, *mixed, turned, *after, *passed)


def fold_kernel(micro, across_ref, *refs):
    kept_ref, sent_ref = refs[-2:]
    middles, parts = refs[:micro], refs[micro : micro + 4]

    def place(kept, sent):
        for m in range(micro):
            total = middles[m][...]
            for part in parts:
                total = total + part[kept, m].astype(f32)
            kept_ref[m] = total
            total = parts[0][sent, m].astype(f32)
            for part in parts[1:]:
                total = total + part[sent, m].astype(f32)
            sent_ref[m] = total.astype(bf16)

    @pl.when(across_ref[0] == 0)
    def low_x():
        place(0, 1)

    @pl.when(across_ref[0] == 1)
    def high_x():
        place(1, 0)


def run_fold(across, middles, parts, after):
    micro = len(middles)
    shape = (micro,) + middles[0].shape
    return pl.pallas_call(
        functools.partial(fold_kernel, micro),
        grid=(1,),
        in_specs=[pl.BlockSpec(memory_space=pltpu.SMEM)]
        + [whole(a.shape) for a in (*middles, *parts)]
        + [pl.BlockSpec(memory_space=pl.ANY)] * len(after),
        out_specs=[whole(shape)] * 2,
        out_shape=[jax.ShapeDtypeStruct(shape, f32), jax.ShapeDtypeStruct(shape, bf16)],
        compiler_params=pltpu.CompilerParams(vmem_limit_bytes=VMEM),
        cost_estimate=LIGHT,
        name="fold",
    )(across, *middles, *parts, *after)


def weight_grads(core, owners, saved, received, after):
    local, held, width = saved[0][0].shape
    hidden_width = saved[0][2].shape[2]
    depth = (width + hidden_width) // owners
    micro, count = len(saved), local // 2
    own = bool(received)

    def expert(j, core_ref):
        side = core_ref[0] if own else 1 - core_ref[0]
        return (side * count + j, 0, 0)

    piece = (owners // PIECES, count, depth, width)
    each = (owners // PIECES, 1, depth, width)
    pieces = [pl.BlockSpec(each, lambda j, core_ref: (0, j, 0, 0))] * PIECES
    flat = [a for group in saved for a in group]
    return pl.pallas_call(
        functools.partial(weight_grads_kernel, micro, own),
        grid_spec=pltpu.PrefetchScalarGridSpec(
            num_scalar_prefetch=1,
            grid=(count,),
            in_specs=[pl.BlockSpec((1,) + a.shape[1:], expert) for a in flat]
            + pieces[: len(received)]
            + [pl.BlockSpec(memory_space=pl.ANY)] * len(after),
            out_specs=pl.BlockSpec((owners, 1, depth, width), lambda j, core_ref: (0, j, 0, 0))
            if own
            else pieces,
        ),
        out_shape=jax.ShapeDtypeStruct((owners, count, depth, width), bf16)
        if own
        else [jax.ShapeDtypeStruct(piece, bf16)] * PIECES,
        compiler_params=pltpu.CompilerParams(vmem_limit_bytes=VMEM),
        cost_estimate=LIGHT,
        name="weight_grads",
    )(core, *flat, *received, *after)


def pass_kernel(*refs):
    del refs


def pass_on(value, after):
    return pl.pallas_call(
        pass_kernel,
        in_specs=[pl.BlockSpec(memory_space=pl.ANY)] * (1 + len(after)),
        out_specs=pl.BlockSpec(memory_space=pl.ANY),
        out_shape=jax.ShapeDtypeStruct(value.shape, value.dtype),
        input_output_aliases={0: 0},
        compiler_params=pltpu.CompilerParams(vmem_limit_bytes=VMEM),
        cost_estimate=LIGHT,
        name="pass_on",
    )(value, *after)


def choose_kernel(place_ref, core_ref, parts_ref, *refs):
    place, core = place_ref[0], core_ref[0]
    refs[0][...] = parts_ref[1 - place, core]
    refs[1][...] = parts_ref[place, 1 - core]
    refs[2][...] = parts_ref[1 - place, 1 - core]


def run_choose(place, core, parts):
    shape = parts.shape[2:]
    return pl.pallas_call(
        choose_kernel,
        grid=(1,),
        in_specs=[pl.BlockSpec(memory_space=pltpu.SMEM)] * 2 + [whole(parts.shape)],
        out_specs=[whole(shape)] * 3,
        out_shape=[jax.ShapeDtypeStruct(shape, bf16)] * 3,
        compiler_params=pltpu.CompilerParams(vmem_limit_bytes=VMEM),
        cost_estimate=LIGHT,
        name="choose",
    )(place, core, parts)


def expert_owned_kernel(place_ref, core_ref, parts_ref, across_ref, other_ref, both_ref, *refs):
    gate_ref, up_ref, down_ref = refs
    upper, half = gate_ref.shape[1], gate_ref.shape[2]
    place, core = place_ref[0], core_ref[0]
    count = across_ref.shape[0]

    def put(at, total):
        gate_ref[at] = total[:upper, :half]
        up_ref[at] = total[:upper, half:]
        down_ref[at] = total[upper:]

    for n in range(count):
        own = parts_ref[place, core, n].astype(f32) + across_ref[n].astype(f32)
        put(core * count + n, own)
        put((1 - core) * count + n, other_ref[n].astype(f32) + both_ref[n].astype(f32))


def run_expert_owned(place, core, parts, received, upper, half):
    count, depth, width = received[0].shape
    count = 2 * count
    shapes = [(count, upper, half), (count, upper, half), (count, depth - upper, width)]
    return pl.pallas_call(
        expert_owned_kernel,
        grid=(1,),
        in_specs=[pl.BlockSpec(memory_space=pltpu.SMEM)] * 2
        + [whole(a.shape) for a in (parts, *received)],
        out_specs=[whole(shape) for shape in shapes],
        out_shape=[jax.ShapeDtypeStruct(shape, f32) for shape in shapes],
        compiler_params=pltpu.CompilerParams(vmem_limit_bytes=VMEM),
        cost_estimate=LIGHT,
        name="expert_owned",
    )(place, core, parts, *received)


def lanes_like(shape):
    return lax.broadcasted_iota(jnp.int32, shape, len(shape) - 1)


def head_sums(values):
    left = lax.broadcasted_iota(jnp.int32, (128, 128), 0) // 32
    right = lax.broadcasted_iota(jnp.int32, (128, 128), 1) // 32
    ones = (left == right).astype(f32).astype(bf16)
    high = values.astype(bf16)
    rest = (values - high.astype(f32)).astype(bf16)
    return product(high, ones) + product(rest, ones)


def columns(dense, start, size):
    return pl.BlockSpec((dense.shape[0], size), lambda *_: (0, start // size))


def pair_kernel(across_ref, own_ref, other_ref, *refs):
    out_ref = refs[-1]

    @pl.when(across_ref[0] == 0)
    def low_x():
        out_ref[0, 0] = own_ref[...]
        out_ref[0, 1] = other_ref[...]

    @pl.when(across_ref[0] == 1)
    def high_x():
        out_ref[0, 0] = other_ref[...]
        out_ref[0, 1] = own_ref[...]


def run_pair(across, own, other, count, after):
    shape = (count, 2) + own.shape
    zeros = (0,) * own.ndim
    return pl.pallas_call(
        pair_kernel,
        grid=(count,),
        in_specs=[pl.BlockSpec(memory_space=pltpu.SMEM), whole(own.shape), whole(other.shape)]
        + [pl.BlockSpec(memory_space=pl.ANY)] * len(after),
        out_specs=pl.BlockSpec((1, 2) + own.shape, lambda i: (i, 0) + zeros),
        out_shape=jax.ShapeDtypeStruct(shape, own.dtype),
        compiler_params=pltpu.CompilerParams(vmem_limit_bytes=VMEM),
        cost_estimate=LIGHT,
        name="pair",
    )(across, own, other, *after)


def pack_kernel(packed_ref, *refs):
    width = refs[-1].shape[1]
    for n in range(packed_ref.shape[0]):
        rows = packed_ref.shape[1]
        refs[-1][n * rows : (n + 1) * rows, :] = packed_ref[n, :, :width]


def run_pack(packed, width, after):
    count, rows, _ = packed.shape
    return pl.pallas_call(
        pack_kernel,
        grid=(1,),
        in_specs=[whole(packed.shape)] + [pl.BlockSpec(memory_space=pl.ANY)] * len(after),
        out_specs=whole((count * rows, width)),
        out_shape=jax.ShapeDtypeStruct((count * rows, width), packed.dtype),
        compiler_params=pltpu.CompilerParams(vmem_limit_bytes=VMEM),
        cost_estimate=LIGHT,
        name="pack",
    )(packed, *after)


def group_stack(query_ref, g, q_half):
    lane = lanes_like((1, 256)) % 128 // 32
    pieces = []
    for i in range(4):
        for r in range(2):
            at = r * q_half + g * 256
            block = query_ref[:, at : at + 256]
            pieces.append(jnp.where(lane == i, block, jnp.zeros_like(block)))
    return jnp.concatenate(pieces, axis=0)


def doubled_values(values, h):
    block = values[:, h // 2 * 128 : h // 2 * 128 + 128]
    swapped = pltpu.roll(block, 64, 1)
    low_half = lanes_like(block.shape) < 64
    return jnp.where(low_half == (h % 2 == 0), block, swapped).astype(bf16)


def group_scores(keys, stack, bias, score_scale):
    scores = product_nt(keys, stack) * score_scale
    return scores + jnp.concatenate([bias] * 8, axis=1)


def rotated(u1, u2, cosine, sine, gain1, gain2, head_size):
    scale = lax.rsqrt(head_sums(u1 * u1 + u2 * u2) / head_size + EPSILON)
    u1 = u1 * scale * gain1
    u2 = u2 * scale * gain2
    return (
        (u1 * cosine - u2 * sine).astype(bf16),
        (u2 * cosine + u1 * sine).astype(bf16),
    )


def front_kernel(
    head_size,
    own_ref,
    one_ref,
    two_ref,
    weights_ref,
    out_weights_ref,
    tail_ref,
    cosine_ref,
    sine_ref,
    gains_ref,
    bias_ref,
    *refs,
):
    micro, rows, width = own_ref.shape
    first, rest = refs[-4 * micro - 5 : -4 * micro], refs[-4 * micro :]
    normed_ref, pre_ref, query_ref, key_value_ref, turned_ref = first
    q_width = query_ref.shape[2]
    kv_width = q_width // 2
    groups = kv_width // 256
    score_scale = 1.0 / math.sqrt(head_size)
    turned = tail_ref[...].astype(f32).T
    turned_ref[...] = turned
    gain = turned[33:34, :]
    low_half = lanes_like((rows, 128)) < 64
    head_gains = [gains_ref[n : n + 1, :] for n in range(4)]

    def norm(x):
        return (x * rms_scale(x) * gain).astype(bf16)

    for m in range(micro):
        attended_ref, middle_ref, moe_ref, peak_ref = rest[4 * m : 4 * m + 4]
        x = own_ref[m].astype(f32)
        normed = norm(x)
        normed_ref[m] = normed
        own = product(normed, weights_ref[...])
        pre_ref[m] = own[:, : q_width + kv_width]
        own_rows = pl.ds(2 * rows, rows)
        for at in range(0, q_width, 256):
            made = rotated(
                own[:, at : at + 128], own[:, at + 128 : at + 256],
                cosine_ref[own_rows, :], sine_ref[own_rows, :],
                head_gains[0], head_gains[1], head_size,
            )
            query_ref[m, :, at : at + 128] = made[0]
            query_ref[m, :, at + 128 : at + 256] = made[1]
        earlier = jnp.concatenate(
            [norm(two_ref[m].astype(f32)), norm(one_ref[m].astype(f32))], axis=0
        )
        earlier = product(earlier, weights_ref[:, q_width:])
        both = jnp.concatenate([earlier, own[:, q_width:]], axis=0)
        key_value_ref[m, :, kv_width:] = both[:, kv_width:].astype(bf16)
        for at in range(0, kv_width, 256):
            made = rotated(
                both[:, at : at + 128], both[:, at + 128 : at + 256],
                cosine_ref[...], sine_ref[...], head_gains[2], head_gains[3], head_size,
            )
            key_value_ref[m, :, at : at + 128] = made[0]
            key_value_ref[m, :, at + 128 : at + 256] = made[1]

        bias = bias_ref[m]
        values = key_value_ref[m, :, kv_width:].astype(f32)
        for g in range(groups):
            keys = key_value_ref[m, :, g * 256 : (g + 1) * 256]
            stack = group_stack(query_ref.at[m], g, q_width // 2)
            scores = group_scores(keys, stack, bias, score_scale)
            peak = jnp.max(scores, axis=0, keepdims=True)
            exps = jnp.exp(scores - peak)
            total = jnp.sum(exps, axis=0, keepdims=True)
            probs = (exps * (1.0 / total)).astype(bf16)
            peak_ref[g : g + 1, :] = peak + jnp.log(total)
            for i in range(4):
                h = 4 * g + i
                mixed = product_tn(probs[:, i * 256 : (i + 1) * 256], doubled_values(values, h))
                attended_ref[:, h * 128 : (h + 1) * 128] = jnp.where(
                    low_half, mixed[:rows], mixed[rows:]
                ).astype(bf16)
        middle = x + product(attended_ref[...], out_weights_ref[...])
        middle_ref[...] = middle
        moe_ref[...] = (middle * rms_scale(middle) * turned[32:33, :]).astype(bf16)


def picked(array, m):
    return pl.BlockSpec(
        (None,) + array.shape[1:], lambda *_: (m,) + (0,) * (len(array.shape) - 1)
    )


def run_front(own, one, two, dense, cosine, sine, gains, bias, head_size, q_width, after):
    micro, rows, width = own.shape
    kv_width = q_width // 2
    shapes = [
        ((micro, rows, width), bf16),
        ((micro, rows, q_width + kv_width), f32),
        ((micro, rows, q_width), bf16),
        ((micro, 3 * rows, 2 * kv_width), bf16),
        ((128, width), f32),
    ] + [
        ((rows, q_width), bf16),
        ((rows, width), f32),
        ((rows, width), bf16),
        ((8, 8 * rows), f32),
    ] * micro
    small = (cosine, sine, gains, bias)
    return pl.pallas_call(
        functools.partial(front_kernel, head_size),
        grid=(1,),
        in_specs=[whole(own.shape)] * 3
        + [
            columns(dense, 0, 2 * q_width),
            columns(dense, 2 * q_width, width),
            columns(dense, 2 * q_width + width, 128),
        ]
        + [whole(a.shape) for a in small]
        + [pl.BlockSpec(memory_space=pl.ANY)] * len(after),
        out_specs=[whole(shape) for shape, _ in shapes],
        out_shape=[jax.ShapeDtypeStruct(shape, kind) for shape, kind in shapes],
        compiler_params=pltpu.CompilerParams(vmem_limit_bytes=VMEM),
        cost_estimate=LIGHT,
        name="front",
    )(own, one, two, dense, dense, dense, *small, *after)


def add_kernel(left_ref, right_ref, *refs):
    total = left_ref[...].astype(f32) + right_ref[...].astype(f32)
    refs[-1][...] = total.astype(bf16)


def total_kernel(parts_ref, *refs):
    total = parts_ref[0].astype(f32)
    for n in range(1, parts_ref.shape[0]):
        total = total + parts_ref[n].astype(f32)
    refs[-1][...] = total.astype(refs[-1].dtype)


def run_total(parts):
    shape = parts.shape[1:]
    return pl.pallas_call(
        total_kernel,
        grid=(1,),
        in_specs=[whole(parts.shape)],
        out_specs=whole(shape),
        out_shape=jax.ShapeDtypeStruct(shape, bf16),
        compiler_params=pltpu.CompilerParams(vmem_limit_bytes=VMEM),
        cost_estimate=LIGHT,
        name="total",
    )(parts)


def owned_kernel(parts_ref, *refs):
    outs = refs[-9:]
    key_ref, value_ref, attn_ref, query_gain_ref, key_gain_ref = outs[:5]
    out_ref, router_ref, ffn_ref, query_ref = outs[5:]
    kv_width, width, q_width = key_ref.shape[1], out_ref.shape[1], query_ref.shape[1]
    experts = router_ref.shape[1]
    rows = parts_ref.shape[1]
    total = parts_ref[0].astype(f32)
    for n in range(1, parts_ref.shape[0]):
        total = total + parts_ref[n].astype(f32)
    run = lanes_like((rows, 128)) // 32

    def gathered(base, sources):
        made = None
        for j, (block, place) in enumerate(sources):
            at = base + block * 128
            piece = total[:, at : at + 128]
            if place != j:
                piece = pltpu.roll(piece, (j - place) % 4 * 32, 1)
            made = piece if made is None else jnp.where(run == j, piece, made)
        return made

    for block in range(kv_width // 128):
        sources = []
        for j in range(4):
            head, half = 2 * block + j // 2, j % 2
            sources.append((head // 4 * 2 + half, head % 4))
        key_ref[:, block * 128 : (block + 1) * 128] = gathered(0, sources)
    at = kv_width
    value_ref[...] = total[:, at : at + kv_width]
    at += kv_width
    extra = total[:, at : at + 128]
    at += 128
    turned = jnp.concatenate([extra, jnp.zeros((128 - rows, 128), f32)], axis=0).T
    attn_ref[...] = turned[0:1, :rows]
    query_gain_ref[...] = extra[0:1, 64:]
    key_gain_ref[...] = extra[1:2, 64:]
    out_ref[...] = total[:, at : at + width]
    at += width
    tail = total[:, at : at + 128]
    at += 128
    router_ref[...] = tail[:, :experts]
    turned = jnp.concatenate([tail, jnp.zeros((128 - rows, 128), f32)], axis=0).T
    ffn_ref[...] = turned[experts : experts + 1, :rows]
    for block in range(q_width // 128):
        sources = []
        for j in range(4):
            r, half = j // 2, j % 2
            sources.append((r * (q_width // 256) + block // 4 * 2 + half, block % 4))
        query_ref[:, block * 128 : (block + 1) * 128] = gathered(at, sources)


def run_owned(parts, width, q_width, head_size, experts, after):
    rows = parts.shape[1]
    kv_width = q_width // 2
    shapes = [
        (rows, kv_width), (rows, kv_width), (1, rows), (1, head_size), (1, head_size),
        (rows, width), (rows, experts), (1, rows), (rows, q_width),
    ]
    return pl.pallas_call(
        owned_kernel,
        grid=(1,),
        in_specs=[whole(parts.shape)] + [pl.BlockSpec(memory_space=pl.ANY)] * len(after),
        out_specs=[whole(shape) for shape in shapes],
        out_shape=[jax.ShapeDtypeStruct(shape, f32) for shape in shapes],
        compiler_params=pltpu.CompilerParams(vmem_limit_bytes=VMEM),
        cost_estimate=LIGHT,
        name="owned",
    )(parts, *after)


def add_low(left, right, each, after=()):
    block = pl.BlockSpec((each,) + left.shape[1:], lambda i: (i,) + (0,) * (left.ndim - 1))
    return pl.pallas_call(
        add_kernel,
        grid=(left.shape[0] // each,),
        in_specs=[block, block] + [pl.BlockSpec(memory_space=pl.ANY)] * len(after),
        out_specs=block,
        out_shape=jax.ShapeDtypeStruct(left.shape, bf16),
        compiler_params=pltpu.CompilerParams(vmem_limit_bytes=VMEM),
        cost_estimate=LIGHT,
        name="add_low",
    )(left, right, *after)


def fetch(sources, targets, sems):
    copies = [
        pltpu.make_async_copy(source, target, sems.at[n])
        for n, (source, target) in enumerate(zip(sources, targets))
    ]
    for copy in copies:
        copy.start()
    return copies


def middle_back_kernel(score_scale, micro, count, passing, *refs):
    sources = refs[:count]
    buffers, sems = refs[-count - 1 : -1], refs[-1]
    outs = refs[-count - 3 - passing - 5 * micro : -count - 1 - passing]
    one_grad_ref, two_grad_ref = outs[5 * micro : 5 * micro + 2]
    dense = sources[0]
    width = dense.shape[0]
    out_columns = dense.at[:, pl.ds(2 * width, width)]
    copies = fetch((out_columns,) + tuple(sources[1:]), buffers, sems)
    out_weights_ref, turned_ref, member_ref, seed_ref, query_ref, key_value_ref, bias_ref = buffers[:7]
    _, rows, q_width = query_ref.shape
    kv_width = key_value_ref.shape[2] // 2
    groups = kv_width // 256
    experts = member_ref.shape[1]
    low_half = lanes_like((rows, 128)) < 64
    low_rows = lanes_like((3 * rows, 128)) < 64
    lane = lanes_like((1, 256)) % 128 // 32
    q_half = q_width // 2
    for n in (1, 2, 3):
        copies[n].wait()
    router = turned_ref[:experts, :].astype(bf16)
    for m in range(micro):
        parts_ref, moe_ref, middle_ref, peak_ref = buffers[7 + 4 * m : 11 + 4 * m]
        mid_grad_ref, branch_ref, router_grad_ref, query_grad_ref, own_grad_ref = outs[
            5 * m : 5 * m + 5
        ]
        for n in range(7 + 4 * m, 11 + 4 * m):
            copies[n].wait()
        senders = parts_ref.shape[0]
        moe_in = moe_ref[...]
        member = member_ref[m] > 0.5
        shown = jnp.where(member, product_nt(router, moe_in), -1e30)
        exps = jnp.where(member, jnp.exp(shown - jnp.max(shown, axis=0, keepdims=True)), 0.0)
        gates = exps / jnp.sum(exps, axis=0, keepdims=True)
        gate_grad = []
        for s in range(senders):
            row = parts_ref[s, rows:, :].astype(f32)
            row = row[0:1] + row[1:2]
            for j in range(experts // senders):
                gate_grad.append(row[:, j * rows : (j + 1) * rows])
        gate_grad = jnp.concatenate(gate_grad, axis=0)
        logit_grad = gates * (gate_grad - jnp.sum(gates * gate_grad, axis=0, keepdims=True))
        logit_grad = logit_grad.astype(bf16)
        moe_grad = product_tn(logit_grad, router)
        for s in range(senders):
            moe_grad = moe_grad + parts_ref[s, :rows, :].astype(f32)
        middle = middle_ref[...]
        scale = rms_scale(middle)
        router_grad_ref[:experts, :] = product(logit_grad, moe_in)
        router_grad_ref[experts : experts + 1, :] = jnp.sum(
            moe_grad * middle * scale, axis=0, keepdims=True
        )
        mid_grad = seed_ref[m].astype(f32) + norm_back(
            moe_grad * turned_ref[32:33, :], middle, scale
        )
        mid_grad_ref[...] = mid_grad
        branch = mid_grad.astype(bf16)
        branch_ref[...] = branch
        if m == 0:
            for n in (0, 4, 5, 6):
                copies[n].wait()
        attended_grad = product_nt(branch, out_weights_ref[...]).astype(bf16)

        bias = bias_ref[m]
        values = key_value_ref[m, :, kv_width:].astype(f32)

        def store(columns, gradient):
            two_grad_ref[m, :, columns] = gradient[:rows].astype(bf16)
            one_grad_ref[m, :, columns] = gradient[rows : 2 * rows].astype(bf16)
            own_grad_ref[:, columns] = gradient[2 * rows :]

        for g in range(groups):
            keys = key_value_ref[m, :, g * 256 : (g + 1) * 256]
            stack = group_stack(query_ref.at[m], g, q_half)
            scores = group_scores(keys, stack, bias, score_scale)
            probs = jnp.exp(scores - peak_ref[g : g + 1, :])
            probs_low = probs.astype(bf16)
            prob_grads, value_grads = [], []
            for i in range(4):
                h = 4 * g + i
                block = attended_grad[:, h * 128 : (h + 1) * 128]
                zero = jnp.zeros_like(block)
                masked = jnp.concatenate(
                    [jnp.where(low_half, block, zero), jnp.where(low_half, zero, block)], axis=0
                )
                prob_grads.append(product_nt(doubled_values(values, h), masked))
                both = product(probs_low[:, i * 256 : (i + 1) * 256], masked)
                value_grads.append(both + pltpu.roll(both, 64, 1))
            prob_grad = jnp.concatenate(prob_grads, axis=1)
            inner = jnp.sum(probs * prob_grad, axis=0, keepdims=True)
            score_low = (score_scale * probs * (prob_grad - inner)).astype(bf16)
            for pair in range(2):
                merged = jnp.where(low_rows, value_grads[2 * pair], value_grads[2 * pair + 1])
                at = kv_width + (2 * g + pair) * 128
                store(slice(at, at + 128), merged)
            store(slice(g * 256, (g + 1) * 256), product(score_low, stack))
            spread_grad = product_tn(score_low, keys)
            for r in range(2):
                total = jnp.zeros((rows, 256), f32)
                for i in range(4):
                    at = (2 * i + r) * rows
                    total = jnp.where(lane == i, spread_grad[at : at + rows], total)
                at = r * q_half + g * 256
                query_grad_ref[:, at : at + 256] = total


def run_middle_back(
    parts, member, seeds, query, key_value, bias, moe_in, middle, peak, dense, turned,
    score_scale, after, passed,
):
    micro, rows, width = seeds.shape
    q_width = query.shape[2]
    shapes = [
        ((rows, width), f32),
        ((rows, width), bf16),
        ((40, width), f32),
        ((rows, q_width), f32),
        ((rows, q_width), f32),
    ] * micro + [((micro, rows, q_width), bf16)] * 2
    ins = (dense, turned, member, seeds, query, key_value, bias)
    for m in range(micro):
        ins = ins + (parts[m], moe_in[m], middle[m], peak[m])
    held = [pltpu.VMEM((width, width), bf16)] + [pltpu.VMEM(a.shape, a.dtype) for a in ins[1:]]
    count = len(ins)
    return pl.pallas_call(
        functools.partial(middle_back_kernel, score_scale, micro, count, len(passed)),
        grid=(1,),
        in_specs=[pl.BlockSpec(memory_space=pl.ANY)] * (count + len(after) + len(passed)),
        out_specs=[whole(shape) for shape, _ in shapes]
        + [pl.BlockSpec(memory_space=pl.ANY)] * len(passed),
        out_shape=[jax.ShapeDtypeStruct(shape, kind) for shape, kind in shapes]
        + [jax.ShapeDtypeStruct(a.shape, a.dtype) for a in passed],
        input_output_aliases={
            count + len(after) + n: len(shapes) + n for n in range(len(passed))
        },
        scratch_shapes=held + [pltpu.SemaphoreType.DMA((count,))],
        compiler_params=pltpu.CompilerParams(vmem_limit_bytes=VMEM),
        cost_estimate=LIGHT,
        name="middle_back",
    )(*ins, *after, *passed)


def by_core(core_ref, values, kept_ref, sent_ref, at):
    halves, depth = kept_ref.shape[0], kept_ref.shape[1]
    pairs = values.reshape(halves, 2, depth, values.shape[1])
    columns = pl.ds(at, values.shape[1])

    @pl.when(core_ref[0] == 0)
    def even():
        kept_ref[:, :, columns] = pairs[:, 0]
        sent_ref[:, :, columns] = pairs[:, 1]

    @pl.when(core_ref[0] == 1)
    def odd():
        kept_ref[:, :, columns] = pairs[:, 1]
        sent_ref[:, :, columns] = pairs[:, 0]


def head_back(u1, u2, up1, up2, cosine, sine, gain1, gain2, head_size):
    back1 = up1 * cosine + up2 * sine
    back2 = up2 * cosine - up1 * sine
    scale = lax.rsqrt(head_sums(u1 * u1 + u2 * u2) / head_size + EPSILON)
    sum1 = jnp.sum(back1 * u1 * scale, axis=0, keepdims=True)
    sum2 = jnp.sum(back2 * u2 * scale, axis=0, keepdims=True)
    back1 = back1 * gain1
    back2 = back2 * gain2
    mean = head_sums(back1 * u1 + back2 * u2) / head_size
    cube = scale * scale * scale
    low1 = (scale * back1 - u1 * cube * mean).astype(bf16)
    low2 = (scale * back2 - u2 * cube * mean).astype(bf16)
    return low1, low2, sum1, sum2


def query_back_kernel(
    head_size, micro, core_ref, pre_ref, normed_ref, cosine_ref, sine_ref, gains_ref, weights_ref,
    *refs,
):
    query_grads, attended, branch, router = [refs[n * micro : (n + 1) * micro] for n in range(4)]
    kept_ref, sent_ref, normed_grad_ref, sums_ref, low = refs[-5:]
    _, rows, width = normed_ref.shape
    q_width = query_grads[0].shape[1]
    base = kept_ref.shape[2] - q_width
    first = base - width - 128
    out_grad = sum(product_tn(a[...], b[...]) for a, b in zip(attended, branch))
    by_core(core_ref, out_grad.astype(bf16), kept_ref, sent_ref, first)
    tail = sum(r[...] for r in router)
    tail = jnp.concatenate([tail, jnp.zeros((128 - tail.shape[0], width), f32)], axis=0)
    by_core(core_ref, tail.T.astype(bf16), kept_ref, sent_ref, first + width)
    sums = [jnp.zeros((1, 128), f32) for _ in range(2)]
    for m in range(micro):
        at_rows = pl.ds(m * rows, rows)
        for at in range(0, q_width, 256):
            low1, low2, sum1, sum2 = head_back(
                pre_ref[m, :, at : at + 128], pre_ref[m, :, at + 128 : at + 256],
                query_grads[m][:, at : at + 128], query_grads[m][:, at + 128 : at + 256],
                cosine_ref[...], sine_ref[...], gains_ref[0:1, :], gains_ref[1:2, :], head_size,
            )
            low[at_rows, at : at + 128] = low1
            low[at_rows, at + 128 : at + 256] = low2
            sums = [sums[0] + sum1, sums[1] + sum2]
    sums_ref[...] = jnp.concatenate(sums + [jnp.zeros((6, 128), f32)], axis=0)
    normed = jnp.concatenate([normed_ref[m] for m in range(micro)], axis=0)
    for at in range(0, q_width, 512):
        grad = product_tn(normed, low[:, at : at + 512]).astype(bf16)
        by_core(core_ref, grad, kept_ref, sent_ref, base + at)
    normed_grad_ref[...] = product_nt(low[...], weights_ref[...])


def last_rows(array, rows):
    block = array.shape[0] // rows - 1
    return pl.BlockSpec((rows, array.shape[1]), lambda *_: (block, 0))


def run_query_back(
    core, owners, pre, normed, cosine, sine, gains, dense, query_grads, attended, branch, router,
    head_size, after,
):
    micro, rows, width = normed.shape
    q_width = query_grads[0].shape[1]
    shape = (owners // 2, width // owners, q_width + 128 + width + 128 + q_width)
    out = jax.ShapeDtypeStruct(shape, bf16)
    ins = (pre, normed, cosine, sine, gains)
    rest = (*query_grads, *attended, *branch, *router)
    return pl.pallas_call(
        functools.partial(query_back_kernel, head_size, micro),
        grid=(1,),
        in_specs=[pl.BlockSpec(memory_space=pltpu.SMEM)]
        + [whole(pre.shape), whole(normed.shape), last_rows(cosine, rows), last_rows(sine, rows)]
        + [whole(gains.shape)]
        + [columns(dense, 0, q_width)]
        + [whole(a.shape) for a in rest]
        + [pl.BlockSpec(memory_space=pl.ANY)] * len(after),
        out_specs=[whole(shape), whole(shape), whole((micro * rows, width)), whole((8, 128))],
        out_shape=[
            out,
            out,
            jax.ShapeDtypeStruct((micro * rows, width), f32),
            jax.ShapeDtypeStruct((8, 128), f32),
        ],
        scratch_shapes=[pltpu.VMEM((micro * rows, q_width), bf16)],
        compiler_params=pltpu.CompilerParams(vmem_limit_bytes=VMEM),
        cost_estimate=LIGHT,
        name="query_back",
    )(core, *ins, dense, *rest, *after)


def tokens_back_kernel(
    head_size, micro, core_ref, pre_ref, normed_ref, tokens_ref, cosine_ref, sine_ref, gains_ref,
    weights_ref, turned_ref, normed_grad_ref, sums_ref, *refs,
):
    kept_ref, sent_ref, tokens_grad_ref, low = refs[-4:]
    own_grads, mid_grads = refs[:micro], refs[micro : 2 * micro]
    ones, twos = refs[2 * micro], refs[2 * micro + 1]
    _, rows, width = normed_ref.shape
    kv_width = own_grads[0].shape[1] // 2
    q_width = pre_ref.shape[2] - kv_width
    sums = [jnp.zeros((1, 128), f32) for _ in range(2)]
    for m in range(micro):
        at_rows = pl.ds(m * rows, rows)

        def upstream(start, size):
            columns = pl.ds(start, size)
            return (
                own_grads[m][:, columns]
                + ones[m, :, columns].astype(f32)
                + twos[m, :, columns].astype(f32)
            )

        low[at_rows, kv_width:] = upstream(kv_width, kv_width).astype(bf16)
        for at in range(0, kv_width, 256):
            from_pre = q_width + at
            low1, low2, sum1, sum2 = head_back(
                pre_ref[m, :, from_pre : from_pre + 128],
                pre_ref[m, :, from_pre + 128 : from_pre + 256],
                upstream(at, 128), upstream(at + 128, 128),
                cosine_ref[...], sine_ref[...], gains_ref[2:3, :], gains_ref[3:4, :], head_size,
            )
            low[at_rows, at : at + 128] = low1
            low[at_rows, at + 128 : at + 256] = low2
            sums = [sums[0] + sum1, sums[1] + sum2]
    normed = jnp.concatenate([normed_ref[m] for m in range(micro)], axis=0)
    for at in range(0, low.shape[1], 512):
        grad = product_tn(normed, low[:, at : at + 512]).astype(bf16)
        by_core(core_ref, grad, kept_ref, sent_ref, at)
    normed_grad = normed_grad_ref[...] + product_nt(low[...], weights_ref[...])
    gain = turned_ref[33:34, :]
    gain_grad = jnp.zeros((1, width), f32)
    for m in range(micro):
        x = tokens_ref[m].astype(f32)
        scale = rms_scale(x)
        part = normed_grad[m * rows : (m + 1) * rows]
        gain_grad = gain_grad + jnp.sum(part * x * scale, axis=0, keepdims=True)
        tokens_grad_ref[m] = (mid_grads[m][...] + norm_back(part * gain, x, scale)).astype(bf16)
    folded = []
    for total in [sums_ref[0:1, :], sums_ref[1:2, :]] + sums:
        total = total + pltpu.roll(total, 64, 1)
        folded.append(total + pltpu.roll(total, 32, 1))
    lane = lanes_like((1, 128))
    query_row = jnp.where(lane < 96, folded[0], folded[1])
    key_row = jnp.where(lane < 96, folded[2], folded[3])
    column = jnp.concatenate([gain_grad, jnp.zeros((127, width), f32)], axis=0).T
    row = lax.broadcasted_iota(jnp.int32, (width, 128), 0)
    extra = jnp.where(
        lanes_like((width, 128)) < 64, column, jnp.where(row % 2 == 0, query_row, key_row)
    )
    by_core(core_ref, extra.astype(bf16), kept_ref, sent_ref, low.shape[1])


def run_tokens_back(
    core, pre, normed, tokens, cosine, sine, gains, dense, turned, normed_grad, sums,
    own_grads, mid_grads, ones, twos, kept, sent, head_size, after,
):
    micro, rows, width = tokens.shape
    wide = own_grads[0].shape[1]
    shape = kept.shape[:2] + (wide + 128,)
    ins = (pre, normed, tokens, cosine, sine, gains)
    rest = (turned, normed_grad, sums, *own_grads, *mid_grads, ones, twos)
    return pl.pallas_call(
        functools.partial(tokens_back_kernel, head_size, micro),
        grid=(1,),
        in_specs=[pl.BlockSpec(memory_space=pltpu.SMEM)]
        + [whole(pre.shape), whole(normed.shape), whole(tokens.shape)]
        + [last_rows(cosine, rows), last_rows(sine, rows), whole(gains.shape)]
        + [columns(dense, wide, wide)]
        + [whole(a.shape) for a in rest]
        + [pl.BlockSpec(memory_space=pl.ANY)] * (2 + len(after)),
        out_specs=[whole(shape), whole(shape), whole(tokens.shape)],
        out_shape=[
            jax.ShapeDtypeStruct(kept.shape, bf16),
            jax.ShapeDtypeStruct(kept.shape, bf16),
            jax.ShapeDtypeStruct(tokens.shape, bf16),
        ],
        input_output_aliases={2 + len(ins) + len(rest): 0, 3 + len(ins) + len(rest): 1},
        scratch_shapes=[pltpu.VMEM((micro * rows, wide), bf16)],
        compiler_params=pltpu.CompilerParams(vmem_limit_bytes=VMEM),
        cost_estimate=LIGHT,
        name="tokens_back",
    )(core, *ins, dense, *rest, kept, sent, *after)


def body(
    tokens,
    cotangent,
    routes,
    doc_lengths,
    valid,
    attn_gain,
    w_query,
    w_key,
    w_value,
    query_gain,
    key_gain,
    w_out,
    ffn_gain,
    w_router,
    w_gate,
    w_up,
    w_down,
):
    micro = tokens.shape[0]
    rows = tokens.shape[2]
    width = tokens.shape[3]
    head_size = query_gain.shape[0]
    q_width = w_query.shape[1]
    kv_width = w_key.shape[1]
    kv_heads = kv_width // head_size
    q_heads = q_width // head_size
    group_size = q_heads // kv_heads
    experts = w_router.shape[1]
    local = w_gate.shape[0]
    hidden_width = w_gate.shape[2]
    upper = w_gate.shape[1]
    expert_devices = lax.axis_size("expert")
    dp_devices = lax.axis_size("dp")
    own_rows = w_query.shape[0]
    reach_back = (WINDOW + rows - 2) // rows
    key_rows = rows * (reach_back + 1)
    score_scale = 1.0 / math.sqrt(head_size)
    q_gain = query_gain.astype(f32)
    k_gain = key_gain.astype(f32)
    all_rows = micro * rows
    qkv_width = q_width + 2 * kv_width

    tiles = 128 // (head_size // 2)
    halves = dp_devices // 2
    core = lax.axis_index("dp") % 2
    core_flag = core[None].astype(jnp.int32)
    expert_index = lax.axis_index("expert")
    across, depth = expert_index % 2, expert_index // 2
    across_flag, depth_flag = across[None].astype(jnp.int32), depth[None].astype(jnp.int32)
    other_core = [(i, i ^ 1) for i in range(dp_devices)]
    other_across = [(i, i ^ 1) for i in range(expert_devices)]
    along_depth = [[2 * z + x for z in range(expert_devices // 2)] for x in range(2)]

    groups = kv_heads // 4
    half_size = head_size // 2
    query_cols = w_query.reshape(own_rows, groups, 4, group_size, 2, half_size)
    query_cols = query_cols.transpose(0, 3, 1, 4, 2, 5).reshape(own_rows, q_width)
    key_cols = w_key.reshape(own_rows, groups, 4, 2, half_size)
    key_cols = key_cols.transpose(0, 1, 3, 2, 4).reshape(own_rows, kv_width)
    tail = jnp.concatenate(
        [
            w_router,
            ffn_gain[:, None],
            attn_gain[:, None],
            jnp.zeros((own_rows, 128 - experts - 2), bf16),
        ],
        axis=1,
    )
    route_cols = routes[:, 0].astype(bf16).reshape(own_rows, -1)
    packed = jnp.concatenate([query_cols, key_cols, w_value, w_out, tail, route_cols], axis=1)
    packed = spread(packed, "expert")
    dense_width = packed.shape[2] - route_cols.shape[1]
    routes_all = packed[:, :, dense_width:].astype(jnp.int32)
    routes_all = routes_all.reshape((expert_devices,) + routes.shape[:1] + routes.shape[2:])
    seed_low = cotangent[:, 0] * valid[:, 0][:, :, None].astype(bf16)
    seed_other = lax.ppermute(seed_low, "expert", other_across)
    x_low = tokens[:, 0]
    one = passed_along(x_low, "expert", 1)
    two = passed_along(x_low, "expert", 2)
    weights = jnp.concatenate([jnp.concatenate([w_gate, w_up], axis=2), w_down], axis=1)
    weights = lax.all_gather(weights, "dp", axis=1)
    dense = run_pack(packed, dense_width, (seed_other,))
    dense = lax.all_gather(dense, "dp", axis=0, tiled=True)

    def by_depth(values, other, after=()):
        pair = run_pair(across_flag, values, other, expert_devices // 2, after)
        return lax.all_to_all(pair, "expert", 0, 0, axis_index_groups=along_depth)

    seed_all = by_depth(seed_low, seed_other, (one, two))
    expert_ids = jnp.arange(experts, dtype=jnp.int32)
    member_all = jnp.any(routes_all[..., None] == expert_ids, axis=3)
    member_turned = jnp.roll(member_all, -expert_index * local, axis=3).transpose(1, 0, 3, 2)
    member = member_turned[:, :, :local]
    earlier = (
        jnp.arange(rows, dtype=jnp.int32)[:, None] < jnp.arange(rows, dtype=jnp.int32)[None, :]
    ).astype(bf16)
    rank = einsum("mbjt,tu->mbju", member.astype(bf16), earlier).astype(jnp.int32)
    slots = jnp.where(member, rank, -1)
    turned_slots = slots.transpose(0, 1, 3, 2)
    member_turned = member_turned.astype(f32)
    own_member = jnp.any(routes[:, 0, :, :, None] == expert_ids, axis=2)
    own_member = own_member.transpose(0, 2, 1).astype(f32)

    q_pos = expert_index * rows + jnp.arange(rows, dtype=jnp.int32)
    k_pos = (expert_index - reach_back) * rows + jnp.arange(key_rows, dtype=jnp.int32)
    cosine, sine = rope_tables(k_pos, head_size)
    cosine = jnp.tile(cosine[:, :half_size], (1, tiles))
    sine = jnp.tile(sine[:, :half_size], (1, tiles))
    bounds = jnp.cumsum(doc_lengths[:, 0], axis=1)
    q_doc = jnp.sum((q_pos[None, :, None] >= bounds[:, None, :]).astype(jnp.int32), axis=2)
    k_doc = jnp.sum((k_pos[None, :, None] >= bounds[:, None, :]).astype(jnp.int32), axis=2)
    offset = q_pos[None, :] - k_pos[:, None]
    visible = (
        (k_pos[None, :, None] >= 0)
        & (q_doc[:, None, :] == k_doc[:, :, None])
        & (offset >= 0)[None]
        & (offset < WINDOW)[None]
    )
    bias = jnp.where(visible, 0.0, -1e30).astype(f32)
    head_gains = jnp.stack(
        [
            jnp.tile(part, tiles)
            for part in (
                q_gain[:half_size],
                q_gain[half_size:],
                k_gain[:half_size],
                k_gain[half_size:],
            )
        ]
        + [jnp.zeros((128,), f32)] * 4
    )

    result = run_front(
        x_low, one, two, dense, cosine, sine, head_gains, bias, head_size, q_width, ()
    )
    normed, pre, query, key_value, turned = result[:5]
    attended, middle, moe_in, peak = [result[5 + n :: 4] for n in range(4)]

    router_turned = jnp.roll(turned[:experts], -expert_index * local, axis=0).astype(bf16)
    saved, backs, mixed = [], [], []
    moe_all = [
        by_depth(
            moe_in[m],
            lax.ppermute(moe_in[m], "expert", other_across),
            (slots, turned_slots, member_turned, own_member, router_turned) if m == 0 else (),
        ).reshape(expert_devices, rows, width)
        for m in range(micro)
    ]
    for m in range(micro):
        back_part, arrived, out_rows, hidden, pre_low, mixed_rows = run_experts(
            m, moe_all[m], seed_all, slots, turned_slots, member_turned, router_turned, weights,
            tuple(mixed),
        )
        saved.append((arrived, out_rows, hidden, pre_low))
        backs.append(lax.all_to_all(back_part, "expert", 0, 0))
        mixed.append(mixed_rows)
    sent = weight_grads(core_flag, dp_devices, saved, (), ())
    received = [lax.ppermute(piece, "dp", other_core) for piece in sent]
    combined = run_combine(depth_flag, mixed, turned_slots, (sent[0], backs[0]), ())
    core_sum = weight_grads(core_flag, dp_devices, saved, received, (combined[0],))

    core_sum = pass_on(core_sum, tuple(backs))

    result = run_middle_back(
        backs, own_member, seed_low, query, key_value, bias, moe_in, middle, peak, dense, turned,
        score_scale, (), (),
    )
    mid_grads, branches, router_grads, query_grads, own_grads = [
        result[n : 5 * micro : 5] for n in range(5)
    ]
    ones = passed_along(result[5 * micro], "expert", -1)
    twos = passed_along(result[5 * micro + 1], "expert", -2)
    across_low = lax.axis_index("dp") // 2 % 2
    place_flag = across_low[None].astype(jnp.int32)
    along_y = [[4 * y + place for y in range(dp_devices // 4)] for place in range(4)]
    over_y = lax.psum_scatter(
        core_sum.reshape((dp_devices // 4, 2, 2) + core_sum.shape[1:]),
        "dp",
        scatter_dimension=0,
        axis_index_groups=along_y,
    )
    over_y = over_y.reshape(over_y.shape[-5:])
    pieces = run_choose(place_flag, core_flag, over_y)
    exchanged = [
        lax.ppermute(piece, "dp", [(i, i ^ step) for i in range(dp_devices)])
        for piece, step in zip(pieces, (2, 1, 3))
    ]
    gate_owned, up_owned, down_owned = run_expert_owned(
        place_flag, core_flag, over_y, exchanged, upper, hidden_width
    )

    out_parts = [combined[0]]
    for ahead in range(1, expert_devices // 2):
        pairs = [(i, (i + 2 * ahead) % expert_devices) for i in range(expert_devices)]
        out_parts.append(lax.ppermute(combined[ahead], "expert", pairs))

    kept_in, sent_in, normed_grad, gain_sums = run_query_back(
        core_flag, dp_devices, pre, normed, cosine, sine, head_gains, dense, query_grads, attended,
        branches, router_grads, head_size, (out_parts[1], out_parts[3]),
    )
    kept_in, sent_in, token_grad = run_tokens_back(
        core_flag, pre, normed, x_low, cosine, sine, head_gains, dense, turned, normed_grad,
        gain_sums, own_grads, mid_grads, ones, twos, kept_in, sent_in, head_size,
        (),
    )
    both = add_low(kept_in, lax.ppermute(sent_in, "dp", other_core), 4)
    parts = both.reshape(dp_devices // 4, 2 * both.shape[1], both.shape[2])
    parts = lax.all_to_all(parts, "dp", 0, 0, axis_index_groups=along_y)

    out_kept, out_sent = run_fold(across_flag, middle, out_parts, (both, *exchanged))
    out_other = lax.ppermute(out_sent, "expert", other_across)

    total = run_total(parts)
    output = add_low(out_kept, out_other, micro, (total,))
    parts = total.reshape(2 * expert_devices, own_rows, -1)
    same_y = [
        [
            ((2 * y + place) * 2 + c) * expert_devices + e
            for place in range(2)
            for e in range(expert_devices)
        ]
        for y in range(dp_devices // 4)
        for c in range(2)
    ]
    parts = lax.all_to_all(parts, ("dp", "expert"), 0, 0, axis_index_groups=same_y)
    (
        key_owned, value_owned, attn_gain_owned, query_gain_owned, key_gain_owned,
        out_owned, router_owned, ffn_gain_owned, query_owned,
    ) = run_owned(parts, width, q_width, head_size, experts, (exchanged[0],))
    return (
        output.reshape(micro, 1, rows, width),
        token_grad.reshape(micro, 1, rows, width),
        attn_gain_owned.reshape(own_rows),
        query_owned,
        key_owned,
        value_owned,
        query_gain_owned.reshape(head_size),
        key_gain_owned.reshape(head_size),
        out_owned,
        ffn_gain_owned.reshape(own_rows),
        router_owned,
        gate_owned,
        up_owned,
        down_owned,
    )


def solution(mesh):
    rows_spec = P(("dp", "expert"), None)
    gain_spec = P(("dp", "expert"))
    token_spec = P(None, "dp", "expert", None)
    expert_spec = P("expert", "dp", None)
    return jax.shard_map(
        body,
        mesh=mesh,
        in_specs=(
            token_spec,
            token_spec,
            token_spec,
            P(None, "dp", None),
            P(None, "dp", "expert"),
            gain_spec,
            rows_spec,
            rows_spec,
            rows_spec,
            P(),
            P(),
            rows_spec,
            gain_spec,
            rows_spec,
            expert_spec,
            expert_spec,
            expert_spec,
        ),
        out_specs=(
            token_spec,
            token_spec,
            gain_spec,
            rows_spec,
            rows_spec,
            rows_spec,
            P(),
            P(),
            rows_spec,
            gain_spec,
            rows_spec,
            expert_spec,
            expert_spec,
            expert_spec,
        ),
        check_vma=False,
    )
```

```python
import functools
import math

import jax
import jax.numpy as jnp
from jax import lax
from jax.experimental import pallas as pl
from jax.experimental.pallas import tpu as pltpu
from jax.sharding import PartitionSpec as P

WINDOW = 256
EPSILON = 1e-06
ROPE_BASE = 10000.0
CAP = 48
EXTRA = 16
VMEM = 60 << 20
PIECES = 2
LIGHT = pl.CostEstimate(flops=1, bytes_accessed=1, transcendentals=0)

bf16 = jnp.bfloat16
f32 = jnp.float32


def rms_scale(values):
    return lax.rsqrt(jnp.mean(values * values, axis=-1, keepdims=True) + EPSILON)


def rope_tables(positions, head_size):
    half_size = head_size // 2
    frequency = jnp.exp(
        -math.log(ROPE_BASE) * (2.0 * jnp.arange(half_size, dtype=f32) / head_size)
    )
    angles = positions.astype(f32)[:, None] * frequency[None, :]
    angles = jnp.concatenate([angles, angles], axis=-1)
    return (jnp.cos(angles), jnp.sin(angles))


def norm_back(upstream, values, scaling):
    return scaling * upstream - values * (scaling * scaling * scaling) * jnp.mean(
        upstream * values, axis=-1, keepdims=True
    )


def product(left_side, right_side):
    return jnp.dot(left_side, right_side, preferred_element_type=f32)


def product_tn(left_side, right_side):
    return lax.dot_general(
        left_side, right_side, (((0,), (0,)), ((), ())), preferred_element_type=f32
    )


def product_nt(left_side, right_side):
    return lax.dot_general(
        left_side, right_side, (((1,), (1,)), ((), ())), preferred_element_type=f32
    )


def einsum(spec, left_side, right_side):
    return jnp.einsum(spec, left_side, right_side, preferred_element_type=f32)


def spread(values, axis):
    count = lax.axis_size(axis)
    return lax.all_to_all(jnp.broadcast_to(values[None], (count,) + values.shape), axis, 0, 0)


def passed_along(value, axis, steps):
    count = lax.axis_size(axis)
    initial, last = (max(0, -steps), min(count, count - steps))
    return lax.ppermute(value, axis, [(source, source + steps) for source in range(initial, last)])


def whole(shape):
    return pl.BlockSpec(shape, lambda *_: (0,) * len(shape))


def once(shape):
    return pl.BlockSpec(shape, lambda *_: (0,) * len(shape), pipeline_mode=pl.Buffered(1))


def put_back(turned, pieces):
    column = lax.broadcasted_iota(jnp.int32, (turned.shape[0], CAP), 1)
    hot = [(turned[:, j : j + 1] == column).astype(f32) for j in range(len(pieces))]
    hot = jnp.concatenate(hot, axis=1).astype(bf16)
    return product(hot, jnp.concatenate(pieces, axis=0)).astype(bf16)


def experts_kernel(
    moe_ref,
    seed_ref,
    slots_ref,
    turned_ref,
    member_ref,
    router_ref,
    weights_ref,
    *refs,
):
    back_ref, arrived_ref, out_rows_ref, hidden_ref, pre_ref, mixed_ref = refs[-11:-5]
    taken, seeds, backs, row_gates, row_grads = refs[-5:]
    step = pl.program_id(0)
    blocks, rows, width = moe_ref.shape
    local = taken.shape[0]
    hidden_width = hidden_ref.shape[2]

    def picks(b, j):
        index = lax.broadcasted_iota(jnp.int32, (CAP, rows), 0)
        return slots_ref[b, j : j + 1, :] == index

    @pl.when(step == 0)
    def dispatch():
        for b in range(blocks):
            tokens = moe_ref[b]
            logits = product_nt(router_ref[...], tokens)
            member = member_ref[b] > 0.5
            shown = jnp.where(member, logits, -1e30)
            exps = jnp.where(member, jnp.exp(shown - jnp.max(shown, axis=0, keepdims=True)), 0.0)
            gates = exps / jnp.sum(exps, axis=0, keepdims=True)
            masks = [picks(b, j) for j in range(local)]
            pick = jnp.concatenate([m.astype(f32) for m in masks], axis=0).astype(bf16)
            arrived = product(pick, tokens).astype(bf16)
            seeded = product(pick, seed_ref[b // 2, b % 2, 0]).astype(bf16)
            for j in range(local):
                at = pl.ds(b * CAP, CAP)
                taken[j, at, :] = arrived[j * CAP : (j + 1) * CAP]
                seeds[j, at, :] = seeded[j * CAP : (j + 1) * CAP]
                row_gates[j, at, :] = jnp.sum(
                    jnp.where(masks[j], gates[j : j + 1, :], 0.0), axis=1, keepdims=True
                )

    def expert():
        upper = width // weights_ref.shape[1]
        gate_up_weights = weights_ref[0, :, :upper, :].reshape(width, 2 * hidden_width)
        down_weights = weights_ref[0, :, upper:, :].reshape(hidden_width, width)
        arrived_ref[0] = taken[step]
        pre = product(taken[step], gate_up_weights)
        gate_pre = pre[:, :hidden_width]
        up_pre = pre[:, hidden_width:]
        sigma = 1.0 / (1.0 + jnp.exp(-gate_pre))
        gate_act = gate_pre * sigma
        hidden = (gate_act * up_pre).astype(bf16)
        hidden_ref[0] = hidden
        expert_out = product(hidden, down_weights).astype(bf16).astype(f32)
        seed_rows = seeds[step].astype(f32)
        gate_column = row_gates[step]
        row_grads[step] = jnp.sum(expert_out * seed_rows, axis=1, keepdims=True)
        mixed_ref[0] = (gate_column * expert_out).astype(bf16)
        out_rows = (gate_column * seed_rows).astype(bf16)
        out_rows_ref[0] = out_rows
        hidden_grad = product_nt(out_rows, down_weights)
        gate_low = (hidden_grad * up_pre * sigma * (1.0 + gate_pre * (1.0 - sigma))).astype(bf16)
        up_low = (hidden_grad * gate_act).astype(bf16)
        pre_ref[0, :, :hidden_width] = gate_low
        pre_ref[0, :, hidden_width:] = up_low
        backs[step] = product_nt(pre_ref[0], gate_up_weights).astype(bf16)

    expert()

    @pl.when(step == local - 1)
    def combine():
        for b in range(blocks):
            at = pl.ds(b * CAP, CAP)
            back_ref[b, :rows, :] = put_back(
                turned_ref[b], [backs[j, at, :] for j in range(local)]
            )
            gate_grads = [
                jnp.sum(jnp.where(picks(b, j), row_grads[j, at, :], 0.0), axis=0, keepdims=True)
                for j in range(local)
            ]
            gate_grads = jnp.concatenate(
                gate_grads + [jnp.zeros((1, width - local * rows), f32)], axis=1
            )
            high = gate_grads.astype(bf16).astype(f32)
            row = lax.broadcasted_iota(jnp.int32, (EXTRA, width), 0)
            back_ref[b, rows:, :] = jnp.where(
                row == 0, high, jnp.where(row == 1, gate_grads - high, 0.0)
            ).astype(bf16)


def run_experts(m, tokens, seeds, slots, turned, member, router, weights, after):
    blocks, rows, width = tokens.shape
    local, owners, each, wide = weights.shape
    hidden_width = wide // 2
    held = blocks * CAP
    shapes = [
        ((blocks, rows + EXTRA, width), bf16),
        ((local, held, width), bf16),
        ((local, held, width), bf16),
        ((local, held, hidden_width), bf16),
        ((local, held, wide), bf16),
        ((local, held, width), bf16),
    ]
    return pl.pallas_call(
        experts_kernel,
        grid=(local,),
        in_specs=[
            once(tokens.shape),
            pl.BlockSpec(
                seeds.shape[:2] + (1,) + seeds.shape[3:],
                lambda j: (0, 0, m, 0, 0),
                pipeline_mode=pl.Buffered(1),
            ),
            picked(slots, m),
            picked(turned, m),
            picked(member, m),
            once(router.shape),
            pl.BlockSpec((1, owners, each, wide), lambda j: (j, 0, 0, 0)),
        ]
        + [pl.BlockSpec(memory_space=pl.ANY)] * len(after),
        out_specs=[once(shapes[0][0])]
        + [pl.BlockSpec((1,) + shape[1:], lambda j: (j, 0, 0)) for shape, _ in shapes[1:]],
        out_shape=[jax.ShapeDtypeStruct(shape, kind) for shape, kind in shapes],
        scratch_shapes=[
            pltpu.VMEM((local, held, width), bf16),
            pltpu.VMEM((local, held, width), bf16),
            pltpu.VMEM((local, held, width), bf16),
            pltpu.VMEM((local, held, 1), f32),
            pltpu.VMEM((local, held, 1), f32),
        ],
        compiler_params=pltpu.CompilerParams(vmem_limit_bytes=VMEM),
        cost_estimate=LIGHT,
        name="experts",
    )(tokens, seeds, slots, turned, member, router, weights, *after)


def weight_grads_kernel(micro, adding, core_ref, *refs):
    del core_ref
    parts = [refs[4 * m : 4 * m + 4] for m in range(micro)]
    gate_up = sum(product_tn(p[0][0], p[3][0]) for p in parts)
    down = sum(product_tn(p[2][0], p[1][0]) for p in parts)
    outs = refs[-1:] if adding else refs[-PIECES:]
    owners = sum(ref.shape[0] for ref in outs)
    upper = gate_up.shape[0] // owners
    gate_up = gate_up.reshape(owners, upper, gate_up.shape[1])
    down = down.reshape(owners, down.shape[0] // owners, down.shape[1])
    each = owners // PIECES
    for n in range(PIECES):
        part = slice(n * each, (n + 1) * each)
        above, below = gate_up[part], down[part]
        if adding:
            received_ref = refs[4 * micro + n]
            above = above + received_ref[:, 0, :upper, :].astype(f32)
            below = below + received_ref[:, 0, upper:, :].astype(f32)
            outs[0][part, 0, :upper, :] = above.astype(bf16)
            outs[0][part, 0, upper:, :] = below.astype(bf16)
        else:
            outs[n][:, 0, :upper, :] = above.astype(bf16)
            outs[n][:, 0, upper:, :] = below.astype(bf16)


def combine_kernel(micro, depth_ref, *refs):
    mixed, turned = refs[:micro], refs[micro]
    own_ref, next_ref, low_ref, high_ref, last_ref = refs[-5:]
    local = mixed[0].shape[0]
    for ahead in range(4):
        target = lax.rem(depth_ref[0] + ahead, 4)
        for x in range(2):
            b = 2 * target + x
            at = pl.ds(pl.multiple_of(b * CAP, CAP), CAP)
            for m in range(micro):
                made = put_back(turned[m, b], [mixed[m][j, at, :] for j in range(local)])
                if ahead == 2:
                    (low_ref, high_ref)[x][m] = made
                else:
                    (own_ref, next_ref, None, last_ref)[ahead][x, m] = made


def run_combine(depth, mixed, turned, after):
    micro, _, rows, _ = turned.shape
    width = mixed[0].shape[2]
    pair, half = (2, micro, rows, width), (micro, rows, width)
    shapes = [pair, pair, half, half, pair]
    return pl.pallas_call(
        functools.partial(combine_kernel, micro),
        grid=(1,),
        in_specs=[pl.BlockSpec(memory_space=pltpu.SMEM)]
        + [whole(a.shape) for a in (*mixed, turned)]
        + [pl.BlockSpec(memory_space=pl.ANY)] * len(after),
        out_specs=[whole(shape) for shape in shapes],
        out_shape=[jax.ShapeDtypeStruct(shape, bf16) for shape in shapes],
        compiler_params=pltpu.CompilerParams(vmem_limit_bytes=VMEM),
        cost_estimate=LIGHT,
        name="combine",
    )(depth, *mixed, turned, *after)


def merge_kernel(next_ref, last_ref, low_ref, high_ref, *refs):
    next_out, last_out = refs[-2:]
    next_out[0] = (next_ref[0].astype(f32) + low_ref[...].astype(f32)).astype(bf16)
    next_out[1] = next_ref[1]
    last_out[0] = last_ref[0]
    last_out[1] = (last_ref[1].astype(f32) + high_ref[...].astype(f32)).astype(bf16)


def run_merge(parts, after):
    shape = parts[0].shape
    return pl.pallas_call(
        merge_kernel,
        grid=(1,),
        in_specs=[whole(a.shape) for a in parts]
        + [pl.BlockSpec(memory_space=pl.ANY)] * len(after),
        out_specs=[whole(shape)] * 2,
        out_shape=[jax.ShapeDtypeStruct(shape, bf16)] * 2,
        compiler_params=pltpu.CompilerParams(vmem_limit_bytes=16 << 20),
        cost_estimate=LIGHT,
        name="merge",
    )(*parts, *after)


def fold_kernel(micro, across_ref, *refs):
    kept_ref, sent_ref = refs[-2:]
    middles, parts = refs[:micro], refs[micro : micro + 3]

    def place(kept, sent):
        for m in range(micro):
            total = middles[m][...]
            for part in parts:
                total = total + part[kept, m].astype(f32)
            kept_ref[m] = total
            total = parts[0][sent, m].astype(f32)
            for part in parts[1:]:
                total = total + part[sent, m].astype(f32)
            sent_ref[m] = total.astype(bf16)

    @pl.when(across_ref[0] == 0)
    def low_x():
        place(0, 1)

    @pl.when(across_ref[0] == 1)
    def high_x():
        place(1, 0)


def run_fold(across, middles, parts, after):
    micro = len(middles)
    shape = (micro,) + middles[0].shape
    return pl.pallas_call(
        functools.partial(fold_kernel, micro),
        grid=(1,),
        in_specs=[pl.BlockSpec(memory_space=pltpu.SMEM)]
        + [whole(a.shape) for a in (*middles, *parts)]
        + [pl.BlockSpec(memory_space=pl.ANY)] * len(after),
        out_specs=[whole(shape)] * 2,
        out_shape=[jax.ShapeDtypeStruct(shape, f32), jax.ShapeDtypeStruct(shape, bf16)],
        compiler_params=pltpu.CompilerParams(vmem_limit_bytes=16 << 20),
        cost_estimate=LIGHT,
        name="fold",
    )(across, *middles, *parts, *after)


def weight_grads(core, owners, saved, received, after):
    local, held, width = saved[0][0].shape
    hidden_width = saved[0][2].shape[2]
    depth = (width + hidden_width) // owners
    micro, count = len(saved), local // 2
    own = bool(received)

    def expert(j, core_ref):
        side = core_ref[0] if own else 1 - core_ref[0]
        return (side * count + j, 0, 0)

    piece = (owners // PIECES, count, depth, width)
    each = (owners // PIECES, 1, depth, width)
    pieces = [pl.BlockSpec(each, lambda j, core_ref: (0, j, 0, 0))] * PIECES
    flat = [a for group in saved for a in group]
    return pl.pallas_call(
        functools.partial(weight_grads_kernel, micro, own),
        grid_spec=pltpu.PrefetchScalarGridSpec(
            num_scalar_prefetch=1,
            grid=(count,),
            in_specs=[pl.BlockSpec((1,) + a.shape[1:], expert) for a in flat]
            + pieces[: len(received)]
            + [pl.BlockSpec(memory_space=pl.ANY)] * len(after),
            out_specs=pl.BlockSpec((owners, 1, depth, width), lambda j, core_ref: (0, j, 0, 0))
            if own
            else pieces,
        ),
        out_shape=jax.ShapeDtypeStruct((owners, count, depth, width), bf16)
        if own
        else [jax.ShapeDtypeStruct(piece, bf16)] * PIECES,
        compiler_params=pltpu.CompilerParams(vmem_limit_bytes=VMEM),
        cost_estimate=LIGHT,
        name="weight_grads",
    )(core, *flat, *received, *after)


def pass_kernel(*refs):
    del refs


def pass_on(value, after):
    return pl.pallas_call(
        pass_kernel,
        in_specs=[pl.BlockSpec(memory_space=pl.ANY)] * (1 + len(after)),
        out_specs=pl.BlockSpec(memory_space=pl.ANY),
        out_shape=jax.ShapeDtypeStruct(value.shape, value.dtype),
        input_output_aliases={0: 0},
        compiler_params=pltpu.CompilerParams(vmem_limit_bytes=VMEM),
        cost_estimate=LIGHT,
        name="pass_on",
    )(value, *after)


def choose_kernel(place_ref, core_ref, parts_ref, *refs):
    place, core = place_ref[0], core_ref[0]
    refs[0][...] = parts_ref[1 - place, core]
    refs[1][...] = parts_ref[place, 1 - core]
    refs[2][...] = parts_ref[1 - place, 1 - core]


def run_choose(place, core, parts):
    shape = parts.shape[2:]
    return pl.pallas_call(
        choose_kernel,
        grid=(1,),
        in_specs=[pl.BlockSpec(memory_space=pltpu.SMEM)] * 2 + [whole(parts.shape)],
        out_specs=[whole(shape)] * 3,
        out_shape=[jax.ShapeDtypeStruct(shape, bf16)] * 3,
        compiler_params=pltpu.CompilerParams(vmem_limit_bytes=12 << 20),
        cost_estimate=LIGHT,
        name="choose",
    )(place, core, parts)


def expert_owned_kernel(place_ref, core_ref, parts_ref, across_ref, other_ref, both_ref, *refs):
    gate_ref, up_ref, down_ref = refs
    upper, half = gate_ref.shape[1], gate_ref.shape[2]
    place, core = place_ref[0], core_ref[0]
    count = across_ref.shape[0]

    def put(at, total):
        gate_ref[at] = total[:upper, :half]
        up_ref[at] = total[:upper, half:]
        down_ref[at] = total[upper:]

    for n in range(count):
        own = parts_ref[place, core, n].astype(f32) + across_ref[n].astype(f32)
        put(core * count + n, own)
        put((1 - core) * count + n, other_ref[n].astype(f32) + both_ref[n].astype(f32))


def run_expert_owned(place, core, parts, received, upper, half):
    count, depth, width = received[0].shape
    count = 2 * count
    shapes = [(count, upper, half), (count, upper, half), (count, depth - upper, width)]
    return pl.pallas_call(
        expert_owned_kernel,
        grid=(1,),
        in_specs=[pl.BlockSpec(memory_space=pltpu.SMEM)] * 2
        + [whole(a.shape) for a in (parts, *received)],
        out_specs=[whole(shape) for shape in shapes],
        out_shape=[jax.ShapeDtypeStruct(shape, f32) for shape in shapes],
        compiler_params=pltpu.CompilerParams(vmem_limit_bytes=12 << 20),
        cost_estimate=LIGHT,
        name="expert_owned",
    )(place, core, parts, *received)


def lanes_like(shape):
    return lax.broadcasted_iota(jnp.int32, shape, len(shape) - 1)


def head_sums(values):
    left = lax.broadcasted_iota(jnp.int32, (128, 128), 0) // 32
    right = lax.broadcasted_iota(jnp.int32, (128, 128), 1) // 32
    ones = (left == right).astype(f32).astype(bf16)
    high = values.astype(bf16)
    rest = (values - high.astype(f32)).astype(bf16)
    return product(high, ones) + product(rest, ones)


def columns(dense, start, size):
    return pl.BlockSpec((dense.shape[0], size), lambda *_: (0, start // size))


def pair_kernel(across_ref, own_ref, other_ref, *refs):
    out_ref = refs[-1]

    @pl.when(across_ref[0] == 0)
    def low_x():
        out_ref[0, 0] = own_ref[...]
        out_ref[0, 1] = other_ref[...]

    @pl.when(across_ref[0] == 1)
    def high_x():
        out_ref[0, 0] = other_ref[...]
        out_ref[0, 1] = own_ref[...]


def run_pair(across, own, other, count, after):
    shape = (count, 2) + own.shape
    zeros = (0,) * own.ndim
    return pl.pallas_call(
        pair_kernel,
        grid=(count,),
        in_specs=[pl.BlockSpec(memory_space=pltpu.SMEM), whole(own.shape), whole(other.shape)]
        + [pl.BlockSpec(memory_space=pl.ANY)] * len(after),
        out_specs=pl.BlockSpec((1, 2) + own.shape, lambda i: (i, 0) + zeros),
        out_shape=jax.ShapeDtypeStruct(shape, own.dtype),
        compiler_params=pltpu.CompilerParams(vmem_limit_bytes=16 << 20),
        cost_estimate=LIGHT,
        name="pair",
    )(across, own, other, *after)


def pack_kernel(packed_ref, *refs):
    width = refs[-1].shape[1]
    for n in range(packed_ref.shape[0]):
        rows = packed_ref.shape[1]
        refs[-1][n * rows : (n + 1) * rows, :] = packed_ref[n, :, :width]


def run_pack(packed, width, after):
    count, rows, _ = packed.shape
    return pl.pallas_call(
        pack_kernel,
        grid=(1,),
        in_specs=[whole(packed.shape)] + [pl.BlockSpec(memory_space=pl.ANY)] * len(after),
        out_specs=whole((count * rows, width)),
        out_shape=jax.ShapeDtypeStruct((count * rows, width), packed.dtype),
        compiler_params=pltpu.CompilerParams(vmem_limit_bytes=8 << 20),
        cost_estimate=LIGHT,
        name="pack",
    )(packed, *after)


def group_stack(query_ref, g, q_half):
    lane = lanes_like((1, 256)) % 128 // 32
    pieces = []
    for i in range(4):
        for r in range(2):
            at = r * q_half + g * 256
            block = query_ref[:, at : at + 256]
            pieces.append(jnp.where(lane == i, block, jnp.zeros_like(block)))
    return jnp.concatenate(pieces, axis=0)


def doubled_values(values, h):
    block = values[:, h // 2 * 128 : h // 2 * 128 + 128]
    swapped = pltpu.roll(block, 64, 1)
    low_half = lanes_like(block.shape) < 64
    return jnp.where(low_half == (h % 2 == 0), block, swapped).astype(bf16)


def group_scores(keys, stack, bias, score_scale):
    scores = product_nt(keys, stack) * score_scale
    return scores + jnp.concatenate([bias] * 8, axis=1)


def rotated(u1, u2, cosine, sine, gain1, gain2, head_size):
    scale = lax.rsqrt(head_sums(u1 * u1 + u2 * u2) / head_size + EPSILON)
    u1 = u1 * scale * gain1
    u2 = u2 * scale * gain2
    return (
        (u1 * cosine - u2 * sine).astype(bf16),
        (u2 * cosine + u1 * sine).astype(bf16),
    )


def front_kernel(
    head_size,
    own_ref,
    one_ref,
    two_ref,
    weights_ref,
    out_weights_ref,
    tail_ref,
    cosine_ref,
    sine_ref,
    gains_ref,
    bias_ref,
    *refs,
):
    micro, rows, width = own_ref.shape
    first, rest = refs[-4 * micro - 5 : -4 * micro], refs[-4 * micro :]
    normed_ref, pre_ref, query_ref, key_value_ref, turned_ref = first
    q_width = query_ref.shape[2]
    kv_width = q_width // 2
    groups = kv_width // 256
    score_scale = 1.0 / math.sqrt(head_size)
    turned = tail_ref[...].astype(f32).T
    turned_ref[...] = turned
    gain = turned[33:34, :]
    low_half = lanes_like((rows, 128)) < 64
    head_gains = [gains_ref[n : n + 1, :] for n in range(4)]

    def norm(x):
        return (x * rms_scale(x) * gain).astype(bf16)

    for m in range(micro):
        attended_ref, middle_ref, moe_ref, peak_ref = rest[4 * m : 4 * m + 4]
        x = own_ref[m].astype(f32)
        normed = norm(x)
        normed_ref[m] = normed
        own = product(normed, weights_ref[...])
        pre_ref[m] = own[:, : q_width + kv_width]
        own_rows = pl.ds(2 * rows, rows)
        for at in range(0, q_width, 256):
            made = rotated(
                own[:, at : at + 128], own[:, at + 128 : at + 256],
                cosine_ref[own_rows, :], sine_ref[own_rows, :],
                head_gains[0], head_gains[1], head_size,
            )
            query_ref[m, :, at : at + 128] = made[0]
            query_ref[m, :, at + 128 : at + 256] = made[1]
        earlier = jnp.concatenate(
            [norm(two_ref[m].astype(f32)), norm(one_ref[m].astype(f32))], axis=0
        )
        earlier = product(earlier, weights_ref[:, q_width:])
        both = jnp.concatenate([earlier, own[:, q_width:]], axis=0)
        key_value_ref[m, :, kv_width:] = both[:, kv_width:].astype(bf16)
        for at in range(0, kv_width, 256):
            made = rotated(
                both[:, at : at + 128], both[:, at + 128 : at + 256],
                cosine_ref[...], sine_ref[...], head_gains[2], head_gains[3], head_size,
            )
            key_value_ref[m, :, at : at + 128] = made[0]
            key_value_ref[m, :, at + 128 : at + 256] = made[1]

        bias = bias_ref[m]
        values = key_value_ref[m, :, kv_width:].astype(f32)
        for g in range(groups):
            keys = key_value_ref[m, :, g * 256 : (g + 1) * 256]
            stack = group_stack(query_ref.at[m], g, q_width // 2)
            scores = group_scores(keys, stack, bias, score_scale)
            peak = jnp.max(scores, axis=0, keepdims=True)
            exps = jnp.exp(scores - peak)
            total = jnp.sum(exps, axis=0, keepdims=True)
            probs = (exps * (1.0 / total)).astype(bf16)
            peak_ref[g : g + 1, :] = peak + jnp.log(total)
            for i in range(4):
                h = 4 * g + i
                mixed = product_tn(probs[:, i * 256 : (i + 1) * 256], doubled_values(values, h))
                attended_ref[:, h * 128 : (h + 1) * 128] = jnp.where(
                    low_half, mixed[:rows], mixed[rows:]
                ).astype(bf16)
        middle = x + product(attended_ref[...], out_weights_ref[...])
        middle_ref[...] = middle
        moe_ref[...] = (middle * rms_scale(middle) * turned[32:33, :]).astype(bf16)


def picked(array, m):
    return pl.BlockSpec(
        (None,) + array.shape[1:], lambda *_: (m,) + (0,) * (len(array.shape) - 1)
    )


def run_front(own, one, two, dense, cosine, sine, gains, bias, head_size, q_width, after):
    micro, rows, width = own.shape
    kv_width = q_width // 2
    shapes = [
        ((micro, rows, width), bf16),
        ((micro, rows, q_width + kv_width), f32),
        ((micro, rows, q_width), bf16),
        ((micro, 3 * rows, 2 * kv_width), bf16),
        ((128, width), f32),
    ] + [
        ((rows, q_width), bf16),
        ((rows, width), f32),
        ((rows, width), bf16),
        ((8, 8 * rows), f32),
    ] * micro
    small = (cosine, sine, gains, bias)
    return pl.pallas_call(
        functools.partial(front_kernel, head_size),
        grid=(1,),
        in_specs=[whole(own.shape)] * 3
        + [
            columns(dense, 0, 2 * q_width),
            columns(dense, 2 * q_width, width),
            columns(dense, 2 * q_width + width, 128),
        ]
        + [whole(a.shape) for a in small]
        + [pl.BlockSpec(memory_space=pl.ANY)] * len(after),
        out_specs=[whole(shape) for shape, _ in shapes],
        out_shape=[jax.ShapeDtypeStruct(shape, kind) for shape, kind in shapes],
        compiler_params=pltpu.CompilerParams(vmem_limit_bytes=VMEM),
        cost_estimate=LIGHT,
        name="front",
    )(own, one, two, dense, dense, dense, *small, *after)


def add_kernel(left_ref, right_ref, *refs):
    total = left_ref[...].astype(f32) + right_ref[...].astype(f32)
    refs[-1][...] = total.astype(bf16)


def total_kernel(parts_ref, *refs):
    total = parts_ref[0].astype(f32)
    for n in range(1, parts_ref.shape[0]):
        total = total + parts_ref[n].astype(f32)
    refs[-1][...] = total.astype(refs[-1].dtype)


def run_total(parts, after):
    shape = parts.shape[1:]
    return pl.pallas_call(
        total_kernel,
        grid=(1,),
        in_specs=[whole(parts.shape)] + [pl.BlockSpec(memory_space=pl.ANY)] * len(after),
        out_specs=whole(shape),
        out_shape=jax.ShapeDtypeStruct(shape, bf16),
        compiler_params=pltpu.CompilerParams(vmem_limit_bytes=16 << 20),
        cost_estimate=LIGHT,
        name="total",
    )(parts, *after)


def owned_kernel(parts_ref, *refs):
    outs = refs[-9:]
    key_ref, value_ref, attn_ref, query_gain_ref, key_gain_ref = outs[:5]
    out_ref, router_ref, ffn_ref, query_ref = outs[5:]
    kv_width, width, q_width = key_ref.shape[1], out_ref.shape[1], query_ref.shape[1]
    experts = router_ref.shape[1]
    rows = parts_ref.shape[1]
    total = parts_ref[0].astype(f32)
    for n in range(1, parts_ref.shape[0]):
        total = total + parts_ref[n].astype(f32)
    run = lanes_like((rows, 128)) // 32

    def gathered(base, sources):
        made = None
        for j, (block, place) in enumerate(sources):
            at = base + block * 128
            piece = total[:, at : at + 128]
            if place != j:
                piece = pltpu.roll(piece, (j - place) % 4 * 32, 1)
            made = piece if made is None else jnp.where(run == j, piece, made)
        return made

    for block in range(kv_width // 128):
        sources = []
        for j in range(4):
            head, half = 2 * block + j // 2, j % 2
            sources.append((head // 4 * 2 + half, head % 4))
        key_ref[:, block * 128 : (block + 1) * 128] = gathered(0, sources)
    at = kv_width
    value_ref[...] = total[:, at : at + kv_width]
    at += kv_width
    extra = total[:, at : at + 128]
    at += 128
    turned = jnp.concatenate([extra, jnp.zeros((128 - rows, 128), f32)], axis=0).T
    attn_ref[...] = turned[0:1, :rows]
    query_gain_ref[...] = extra[0:1, 64:]
    key_gain_ref[...] = extra[1:2, 64:]
    out_ref[...] = total[:, at : at + width]
    at += width
    tail = total[:, at : at + 128]
    at += 128
    router_ref[...] = tail[:, :experts]
    turned = jnp.concatenate([tail, jnp.zeros((128 - rows, 128), f32)], axis=0).T
    ffn_ref[...] = turned[experts : experts + 1, :rows]
    for block in range(q_width // 128):
        sources = []
        for j in range(4):
            r, half = j // 2, j % 2
            sources.append((r * (q_width // 256) + block // 4 * 2 + half, block % 4))
        query_ref[:, block * 128 : (block + 1) * 128] = gathered(at, sources)


def run_owned(parts, width, q_width, head_size, experts, after):
    rows = parts.shape[1]
    kv_width = q_width // 2
    shapes = [
        (rows, kv_width), (rows, kv_width), (1, rows), (1, head_size), (1, head_size),
        (rows, width), (rows, experts), (1, rows), (rows, q_width),
    ]
    return pl.pallas_call(
        owned_kernel,
        grid=(1,),
        in_specs=[whole(parts.shape)] + [pl.BlockSpec(memory_space=pl.ANY)] * len(after),
        out_specs=[whole(shape) for shape in shapes],
        out_shape=[jax.ShapeDtypeStruct(shape, f32) for shape in shapes],
        compiler_params=pltpu.CompilerParams(vmem_limit_bytes=8 << 20),
        cost_estimate=LIGHT,
        name="owned",
    )(parts, *after)


def add_low(left, right, each, after=()):
    block = pl.BlockSpec((each,) + left.shape[1:], lambda i: (i,) + (0,) * (left.ndim - 1))
    return pl.pallas_call(
        add_kernel,
        grid=(left.shape[0] // each,),
        in_specs=[block, block] + [pl.BlockSpec(memory_space=pl.ANY)] * len(after),
        out_specs=block,
        out_shape=jax.ShapeDtypeStruct(left.shape, bf16),
        compiler_params=pltpu.CompilerParams(vmem_limit_bytes=16 << 20),
        cost_estimate=LIGHT,
        name="add_low",
    )(left, right, *after)


def fetch(sources, targets, sems):
    copies = [
        pltpu.make_async_copy(source, target, sems.at[n])
        for n, (source, target) in enumerate(zip(sources, targets))
    ]
    for copy in copies:
        copy.start()
    return copies


def middle_back_kernel(score_scale, m, count, passing, *refs):
    sources = refs[:count]
    buffers, sems = refs[-count - 1 : -1], refs[-1]
    outs = refs[-count - 8 - passing : -count - 1 - passing]
    mid_grad_ref, branch_ref, router_grad_ref, query_grad_ref, own_grad_ref = outs[:5]
    one_grad_ref, two_grad_ref = outs[5:]
    dense = sources[0]
    width = dense.shape[0]
    out_columns = dense.at[:, pl.ds(2 * width, width)]
    by_micro = tuple(source.at[m] for source in sources[2:7])
    copies = fetch((out_columns, sources[1], *by_micro, *sources[7:]), buffers, sems)
    out_weights_ref, turned_ref, member_ref, seed_ref, query_ref, key_value_ref, bias_ref = buffers[:7]
    parts_ref, moe_ref, middle_ref, peak_ref = buffers[7:11]
    rows, q_width = query_ref.shape
    kv_width = key_value_ref.shape[1] // 2
    groups = kv_width // 256
    experts = member_ref.shape[0]
    low_half = lanes_like((rows, 128)) < 64
    low_rows = lanes_like((3 * rows, 128)) < 64
    lane = lanes_like((1, 256)) % 128 // 32
    q_half = q_width // 2
    for n in (1, 2, 3, 7, 8, 9, 10):
        copies[n].wait()
    router = turned_ref[:experts, :].astype(bf16)
    senders = parts_ref.shape[0]
    moe_in = moe_ref[...]
    member = member_ref[...] > 0.5
    shown = jnp.where(member, product_nt(router, moe_in), -1e30)
    exps = jnp.where(member, jnp.exp(shown - jnp.max(shown, axis=0, keepdims=True)), 0.0)
    gates = exps / jnp.sum(exps, axis=0, keepdims=True)
    gate_grad = []
    for s in range(senders):
        row = parts_ref[s, rows:, :].astype(f32)
        row = row[0:1] + row[1:2]
        for j in range(experts // senders):
            gate_grad.append(row[:, j * rows : (j + 1) * rows])
    gate_grad = jnp.concatenate(gate_grad, axis=0)
    logit_grad = gates * (gate_grad - jnp.sum(gates * gate_grad, axis=0, keepdims=True))
    logit_grad = logit_grad.astype(bf16)
    moe_grad = product_tn(logit_grad, router)
    for s in range(senders):
        moe_grad = moe_grad + parts_ref[s, :rows, :].astype(f32)
    middle = middle_ref[...]
    scale = rms_scale(middle)
    router_grad_ref[:experts, :] = product(logit_grad, moe_in)
    router_grad_ref[experts : experts + 1, :] = jnp.sum(
        moe_grad * middle * scale, axis=0, keepdims=True
    )
    mid_grad = seed_ref[...].astype(f32) + norm_back(
        moe_grad * turned_ref[32:33, :], middle, scale
    )
    mid_grad_ref[...] = mid_grad
    branch = mid_grad.astype(bf16)
    branch_ref[...] = branch
    for n in (0, 4, 5, 6):
        copies[n].wait()
    attended_grad = product_nt(branch, out_weights_ref[...]).astype(bf16)

    bias = bias_ref[...]
    values = key_value_ref[:, kv_width:].astype(f32)

    def store(columns, gradient):
        two_grad_ref[:, columns] = gradient[:rows].astype(bf16)
        one_grad_ref[:, columns] = gradient[rows : 2 * rows].astype(bf16)
        own_grad_ref[:, columns] = gradient[2 * rows :]

    for g in range(groups):
        keys = key_value_ref[:, g * 256 : (g + 1) * 256]
        stack = group_stack(query_ref, g, q_half)
        scores = group_scores(keys, stack, bias, score_scale)
        probs = jnp.exp(scores - peak_ref[g : g + 1, :])
        probs_low = probs.astype(bf16)
        prob_grads, value_grads = [], []
        for i in range(4):
            h = 4 * g + i
            block = attended_grad[:, h * 128 : (h + 1) * 128]
            zero = jnp.zeros_like(block)
            masked = jnp.concatenate(
                [jnp.where(low_half, block, zero), jnp.where(low_half, zero, block)], axis=0
            )
            prob_grads.append(product_nt(doubled_values(values, h), masked))
            both = product(probs_low[:, i * 256 : (i + 1) * 256], masked)
            value_grads.append(both + pltpu.roll(both, 64, 1))
        prob_grad = jnp.concatenate(prob_grads, axis=1)
        inner = jnp.sum(probs * prob_grad, axis=0, keepdims=True)
        score_low = (score_scale * probs * (prob_grad - inner)).astype(bf16)
        for pair in range(2):
            merged = jnp.where(low_rows, value_grads[2 * pair], value_grads[2 * pair + 1])
            at = kv_width + (2 * g + pair) * 128
            store(slice(at, at + 128), merged)
        store(slice(g * 256, (g + 1) * 256), product(score_low, stack))
        spread_grad = product_tn(score_low, keys)
        for r in range(2):
            total = jnp.zeros((rows, 256), f32)
            for i in range(4):
                at = (2 * i + r) * rows
                total = jnp.where(lane == i, spread_grad[at : at + rows], total)
            at = r * q_half + g * 256
            query_grad_ref[:, at : at + 256] = total


def run_middle_back(
    m, parts, member, seeds, query, key_value, bias, moe_in, middle, peak, dense, turned,
    score_scale, after, passed, joint,
):
    micro, rows, width = seeds.shape
    q_width = query.shape[2]
    shapes = [
        ((rows, width), f32),
        ((rows, width), bf16),
        ((40, width), f32),
        ((rows, q_width), f32),
        ((rows, q_width), f32),
    ]
    halo = (micro, rows, q_width)
    by_micro = (member, seeds, query, key_value, bias)
    ins = (dense, turned, *by_micro, parts, moe_in, middle, peak)
    held = (
        [pltpu.VMEM((width, width), bf16), pltpu.VMEM(turned.shape, f32)]
        + [pltpu.VMEM(a.shape[1:], a.dtype) for a in by_micro]
        + [pltpu.VMEM(a.shape, a.dtype) for a in ins[7:]]
    )
    count = len(ins)
    given = count + len(after)
    aliases = {given + n: 5 + n for n in range(len(joint))}
    aliases.update({given + len(joint) + n: 7 + n for n in range(len(passed))})
    return pl.pallas_call(
        functools.partial(middle_back_kernel, score_scale, m, count, len(passed)),
        grid=(1,),
        in_specs=[pl.BlockSpec(memory_space=pl.ANY)] * (given + len(joint) + len(passed)),
        out_specs=[whole(shape) for shape, _ in shapes]
        + [pl.BlockSpec((None, rows, q_width), lambda *_: (m, 0, 0))] * 2
        + [pl.BlockSpec(memory_space=pl.ANY)] * len(passed),
        out_shape=[jax.ShapeDtypeStruct(shape, kind) for shape, kind in shapes]
        + [jax.ShapeDtypeStruct(halo, bf16)] * 2
        + [jax.ShapeDtypeStruct(a.shape, a.dtype) for a in passed],
        input_output_aliases=aliases,
        scratch_shapes=held + [pltpu.SemaphoreType.DMA((count,))],
        compiler_params=pltpu.CompilerParams(vmem_limit_bytes=VMEM),
        cost_estimate=LIGHT,
        name="middle_back",
    )(*ins, *after, *joint, *passed)


def by_core(core_ref, values, kept_ref, sent_ref, at):
    halves, depth = kept_ref.shape[0], kept_ref.shape[1]
    pairs = values.reshape(halves, 2, depth, values.shape[1])
    columns = pl.ds(at, values.shape[1])

    @pl.when(core_ref[0] == 0)
    def even():
        kept_ref[:, :, columns] = pairs[:, 0]
        sent_ref[:, :, columns] = pairs[:, 1]

    @pl.when(core_ref[0] == 1)
    def odd():
        kept_ref[:, :, columns] = pairs[:, 1]
        sent_ref[:, :, columns] = pairs[:, 0]


def head_back(u1, u2, up1, up2, cosine, sine, gain1, gain2, head_size):
    back1 = up1 * cosine + up2 * sine
    back2 = up2 * cosine - up1 * sine
    scale = lax.rsqrt(head_sums(u1 * u1 + u2 * u2) / head_size + EPSILON)
    sum1 = jnp.sum(back1 * u1 * scale, axis=0, keepdims=True)
    sum2 = jnp.sum(back2 * u2 * scale, axis=0, keepdims=True)
    back1 = back1 * gain1
    back2 = back2 * gain2
    mean = head_sums(back1 * u1 + back2 * u2) / head_size
    cube = scale * scale * scale
    low1 = (scale * back1 - u1 * cube * mean).astype(bf16)
    low2 = (scale * back2 - u2 * cube * mean).astype(bf16)
    return low1, low2, sum1, sum2


def query_back_kernel(
    head_size, micro, core_ref, pre_ref, normed_ref, cosine_ref, sine_ref, gains_ref, weights_ref,
    *refs,
):
    query_grads, attended, branch, router = [refs[n * micro : (n + 1) * micro] for n in range(4)]
    kept_ref, sent_ref, normed_grad_ref, sums_ref, low = refs[-5:]
    _, rows, width = normed_ref.shape
    q_width = query_grads[0].shape[1]
    base = kept_ref.shape[2] - q_width
    first = base - width - 128
    out_grad = sum(product_tn(a[...], b[...]) for a, b in zip(attended, branch))
    by_core(core_ref, out_grad.astype(bf16), kept_ref, sent_ref, first)
    tail = sum(r[...] for r in router)
    tail = jnp.concatenate([tail, jnp.zeros((128 - tail.shape[0], width), f32)], axis=0)
    by_core(core_ref, tail.T.astype(bf16), kept_ref, sent_ref, first + width)
    sums = [jnp.zeros((1, 128), f32) for _ in range(2)]
    for m in range(micro):
        at_rows = pl.ds(m * rows, rows)
        for at in range(0, q_width, 256):
            low1, low2, sum1, sum2 = head_back(
                pre_ref[m, :, at : at + 128], pre_ref[m, :, at + 128 : at + 256],
                query_grads[m][:, at : at + 128], query_grads[m][:, at + 128 : at + 256],
                cosine_ref[...], sine_ref[...], gains_ref[0:1, :], gains_ref[1:2, :], head_size,
            )
            low[at_rows, at : at + 128] = low1
            low[at_rows, at + 128 : at + 256] = low2
            sums = [sums[0] + sum1, sums[1] + sum2]
    sums_ref[...] = jnp.concatenate(sums + [jnp.zeros((6, 128), f32)], axis=0)
    normed = jnp.concatenate([normed_ref[m] for m in range(micro)], axis=0)
    for at in range(0, q_width, 512):
        grad = product_tn(normed, low[:, at : at + 512]).astype(bf16)
        by_core(core_ref, grad, kept_ref, sent_ref, base + at)
    normed_grad_ref[...] = product_nt(low[...], weights_ref[...])


def last_rows(array, rows):
    block = array.shape[0] // rows - 1
    return pl.BlockSpec((rows, array.shape[1]), lambda *_: (block, 0))


def run_query_back(
    core, owners, pre, normed, cosine, sine, gains, dense, query_grads, attended, branch, router,
    head_size, after,
):
    micro, rows, width = normed.shape
    q_width = query_grads[0].shape[1]
    shape = (owners // 2, width // owners, q_width + 128 + width + 128 + q_width)
    out = jax.ShapeDtypeStruct(shape, bf16)
    ins = (pre, normed, cosine, sine, gains)
    rest = (*query_grads, *attended, *branch, *router)
    return pl.pallas_call(
        functools.partial(query_back_kernel, head_size, micro),
        grid=(1,),
        in_specs=[pl.BlockSpec(memory_space=pltpu.SMEM)]
        + [whole(pre.shape), whole(normed.shape), last_rows(cosine, rows), last_rows(sine, rows)]
        + [whole(gains.shape)]
        + [columns(dense, 0, q_width)]
        + [whole(a.shape) for a in rest]
        + [pl.BlockSpec(memory_space=pl.ANY)] * len(after),
        out_specs=[whole(shape), whole(shape), whole((micro * rows, width)), whole((8, 128))],
        out_shape=[
            out,
            out,
            jax.ShapeDtypeStruct((micro * rows, width), f32),
            jax.ShapeDtypeStruct((8, 128), f32),
        ],
        scratch_shapes=[pltpu.VMEM((micro * rows, q_width), bf16)],
        compiler_params=pltpu.CompilerParams(vmem_limit_bytes=VMEM),
        cost_estimate=LIGHT,
        name="query_back",
    )(core, *ins, dense, *rest, *after)


def tokens_back_kernel(
    head_size, micro, core_ref, pre_ref, normed_ref, tokens_ref, cosine_ref, sine_ref, gains_ref,
    weights_ref, turned_ref, normed_grad_ref, sums_ref, *refs,
):
    kept_ref, sent_ref, tokens_grad_ref, low = refs[-4:]
    own_grads, mid_grads = refs[:micro], refs[micro : 2 * micro]
    ones, twos = refs[2 * micro], refs[2 * micro + 1]
    _, rows, width = normed_ref.shape
    kv_width = own_grads[0].shape[1] // 2
    q_width = pre_ref.shape[2] - kv_width
    sums = [jnp.zeros((1, 128), f32) for _ in range(2)]
    for m in range(micro):
        at_rows = pl.ds(m * rows, rows)

        def upstream(start, size):
            columns = pl.ds(start, size)
            return (
                own_grads[m][:, columns]
                + ones[m, :, columns].astype(f32)
                + twos[m, :, columns].astype(f32)
            )

        low[at_rows, kv_width:] = upstream(kv_width, kv_width).astype(bf16)
        for at in range(0, kv_width, 256):
            from_pre = q_width + at
            low1, low2, sum1, sum2 = head_back(
                pre_ref[m, :, from_pre : from_pre + 128],
                pre_ref[m, :, from_pre + 128 : from_pre + 256],
                upstream(at, 128), upstream(at + 128, 128),
                cosine_ref[...], sine_ref[...], gains_ref[2:3, :], gains_ref[3:4, :], head_size,
            )
            low[at_rows, at : at + 128] = low1
            low[at_rows, at + 128 : at + 256] = low2
            sums = [sums[0] + sum1, sums[1] + sum2]
    normed = jnp.concatenate([normed_ref[m] for m in range(micro)], axis=0)
    for at in range(0, low.shape[1], 512):
        grad = product_tn(normed, low[:, at : at + 512]).astype(bf16)
        by_core(core_ref, grad, kept_ref, sent_ref, at)
    normed_grad = normed_grad_ref[...] + product_nt(low[...], weights_ref[...])
    gain = turned_ref[33:34, :]
    gain_grad = jnp.zeros((1, width), f32)
    for m in range(micro):
        x = tokens_ref[m].astype(f32)
        scale = rms_scale(x)
        part = normed_grad[m * rows : (m + 1) * rows]
        gain_grad = gain_grad + jnp.sum(part * x * scale, axis=0, keepdims=True)
        tokens_grad_ref[m] = (mid_grads[m][...] + norm_back(part * gain, x, scale)).astype(bf16)
    folded = []
    for total in [sums_ref[0:1, :], sums_ref[1:2, :]] + sums:
        total = total + pltpu.roll(total, 64, 1)
        folded.append(total + pltpu.roll(total, 32, 1))
    lane = lanes_like((1, 128))
    query_row = jnp.where(lane < 96, folded[0], folded[1])
    key_row = jnp.where(lane < 96, folded[2], folded[3])
    column = jnp.concatenate([gain_grad, jnp.zeros((127, width), f32)], axis=0).T
    row = lax.broadcasted_iota(jnp.int32, (width, 128), 0)
    extra = jnp.where(
        lanes_like((width, 128)) < 64, column, jnp.where(row % 2 == 0, query_row, key_row)
    )
    by_core(core_ref, extra.astype(bf16), kept_ref, sent_ref, low.shape[1])


def run_tokens_back(
    core, pre, normed, tokens, cosine, sine, gains, dense, turned, normed_grad, sums,
    own_grads, mid_grads, ones, twos, kept, sent, head_size, after,
):
    micro, rows, width = tokens.shape
    wide = own_grads[0].shape[1]
    shape = kept.shape[:2] + (wide + 128,)
    ins = (pre, normed, tokens, cosine, sine, gains)
    rest = (turned, normed_grad, sums, *own_grads, *mid_grads, ones, twos)
    return pl.pallas_call(
        functools.partial(tokens_back_kernel, head_size, micro),
        grid=(1,),
        in_specs=[pl.BlockSpec(memory_space=pltpu.SMEM)]
        + [whole(pre.shape), whole(normed.shape), whole(tokens.shape)]
        + [last_rows(cosine, rows), last_rows(sine, rows), whole(gains.shape)]
        + [columns(dense, wide, wide)]
        + [whole(a.shape) for a in rest]
        + [pl.BlockSpec(memory_space=pl.ANY)] * (2 + len(after)),
        out_specs=[whole(shape), whole(shape), whole(tokens.shape)],
        out_shape=[
            jax.ShapeDtypeStruct(kept.shape, bf16),
            jax.ShapeDtypeStruct(kept.shape, bf16),
            jax.ShapeDtypeStruct(tokens.shape, bf16),
        ],
        input_output_aliases={2 + len(ins) + len(rest): 0, 3 + len(ins) + len(rest): 1},
        scratch_shapes=[pltpu.VMEM((micro * rows, wide), bf16)],
        compiler_params=pltpu.CompilerParams(vmem_limit_bytes=VMEM),
        cost_estimate=LIGHT,
        name="tokens_back",
    )(core, *ins, dense, *rest, kept, sent, *after)


def body(
    tokens,
    cotangent,
    routes,
    doc_lengths,
    valid,
    attn_gain,
    w_query,
    w_key,
    w_value,
    query_gain,
    key_gain,
    w_out,
    ffn_gain,
    w_router,
    w_gate,
    w_up,
    w_down,
):
    micro = tokens.shape[0]
    rows = tokens.shape[2]
    width = tokens.shape[3]
    head_size = query_gain.shape[0]
    q_width = w_query.shape[1]
    kv_width = w_key.shape[1]
    kv_heads = kv_width // head_size
    q_heads = q_width // head_size
    group_size = q_heads // kv_heads
    experts = w_router.shape[1]
    local = w_gate.shape[0]
    hidden_width = w_gate.shape[2]
    upper = w_gate.shape[1]
    expert_devices = lax.axis_size("expert")
    dp_devices = lax.axis_size("dp")
    own_rows = w_query.shape[0]
    reach_back = (WINDOW + rows - 2) // rows
    key_rows = rows * (reach_back + 1)
    score_scale = 1.0 / math.sqrt(head_size)
    q_gain = query_gain.astype(f32)
    k_gain = key_gain.astype(f32)
    all_rows = micro * rows
    qkv_width = q_width + 2 * kv_width

    tiles = 128 // (head_size // 2)
    halves = dp_devices // 2
    core = lax.axis_index("dp") % 2
    core_flag = core[None].astype(jnp.int32)
    expert_index = lax.axis_index("expert")
    across, depth = expert_index % 2, expert_index // 2
    across_flag, depth_flag = across[None].astype(jnp.int32), depth[None].astype(jnp.int32)
    other_core = [(i, i ^ 1) for i in range(dp_devices)]
    other_across = [(i, i ^ 1) for i in range(expert_devices)]
    along_depth = [[2 * z + x for z in range(expert_devices // 2)] for x in range(2)]

    groups = kv_heads // 4
    half_size = head_size // 2
    query_cols = w_query.reshape(own_rows, groups, 4, group_size, 2, half_size)
    query_cols = query_cols.transpose(0, 3, 1, 4, 2, 5).reshape(own_rows, q_width)
    key_cols = w_key.reshape(own_rows, groups, 4, 2, half_size)
    key_cols = key_cols.transpose(0, 1, 3, 2, 4).reshape(own_rows, kv_width)
    tail = jnp.concatenate(
        [
            w_router,
            ffn_gain[:, None],
            attn_gain[:, None],
            jnp.zeros((own_rows, 128 - experts - 2), bf16),
        ],
        axis=1,
    )
    route_cols = routes[:, 0].astype(bf16).reshape(own_rows, -1)
    packed = jnp.concatenate([query_cols, key_cols, w_value, w_out, tail, route_cols], axis=1)
    packed = spread(packed, "expert")
    dense_width = packed.shape[2] - route_cols.shape[1]
    routes_all = packed[:, :, dense_width:].astype(jnp.int32)
    routes_all = routes_all.reshape((expert_devices,) + routes.shape[:1] + routes.shape[2:])
    seed_low = cotangent[:, 0] * valid[:, 0][:, :, None].astype(bf16)
    seed_other = lax.ppermute(seed_low, "expert", other_across)
    x_low = tokens[:, 0]
    one = passed_along(x_low, "expert", 1)
    two = passed_along(x_low, "expert", 2)
    weights = jnp.concatenate([jnp.concatenate([w_gate, w_up], axis=2), w_down], axis=1)
    weights = lax.all_gather(weights, "dp", axis=1)
    dense = run_pack(packed, dense_width, (seed_other,))
    dense = lax.all_gather(dense, "dp", axis=0, tiled=True)

    def by_depth(values, other, after=()):
        pair = run_pair(across_flag, values, other, expert_devices // 2, after)
        return lax.all_to_all(pair, "expert", 0, 0, axis_index_groups=along_depth)

    seed_all = by_depth(seed_low, seed_other, (one, two))
    expert_ids = jnp.arange(experts, dtype=jnp.int32)
    member_all = jnp.any(routes_all[..., None] == expert_ids, axis=3)
    member_turned = jnp.roll(member_all, -expert_index * local, axis=3).transpose(1, 0, 3, 2)
    member = member_turned[:, :, :local]
    earlier = (
        jnp.arange(rows, dtype=jnp.int32)[:, None] < jnp.arange(rows, dtype=jnp.int32)[None, :]
    ).astype(bf16)
    rank = einsum("mbjt,tu->mbju", member.astype(bf16), earlier).astype(jnp.int32)
    slots = jnp.where(member, rank, -1)
    turned_slots = slots.transpose(0, 1, 3, 2)
    member_turned = member_turned.astype(f32)
    own_member = jnp.any(routes[:, 0, :, :, None] == expert_ids, axis=2)
    own_member = own_member.transpose(0, 2, 1).astype(f32)

    q_pos = expert_index * rows + jnp.arange(rows, dtype=jnp.int32)
    k_pos = (expert_index - reach_back) * rows + jnp.arange(key_rows, dtype=jnp.int32)
    cosine, sine = rope_tables(k_pos, head_size)
    cosine = jnp.tile(cosine[:, :half_size], (1, tiles))
    sine = jnp.tile(sine[:, :half_size], (1, tiles))
    bounds = jnp.cumsum(doc_lengths[:, 0], axis=1)
    q_doc = jnp.sum((q_pos[None, :, None] >= bounds[:, None, :]).astype(jnp.int32), axis=2)
    k_doc = jnp.sum((k_pos[None, :, None] >= bounds[:, None, :]).astype(jnp.int32), axis=2)
    offset = q_pos[None, :] - k_pos[:, None]
    visible = (
        (k_pos[None, :, None] >= 0)
        & (q_doc[:, None, :] == k_doc[:, :, None])
        & (offset >= 0)[None]
        & (offset < WINDOW)[None]
    )
    bias = jnp.where(visible, 0.0, -1e30).astype(f32)
    head_gains = jnp.stack(
        [
            jnp.tile(part, tiles)
            for part in (
                q_gain[:half_size],
                q_gain[half_size:],
                k_gain[:half_size],
                k_gain[half_size:],
            )
        ]
        + [jnp.zeros((128,), f32)] * 4
    )

    result = run_front(
        x_low, one, two, dense, cosine, sine, head_gains, bias, head_size, q_width, ()
    )
    normed, pre, query, key_value, turned = result[:5]
    attended, middle, moe_in, peak = [result[5 + n :: 4] for n in range(4)]

    router_turned = jnp.roll(turned[:experts], -expert_index * local, axis=0).astype(bf16)
    saved, backs, mixed = [], [], []
    moe_all = [
        by_depth(
            moe_in[m],
            lax.ppermute(moe_in[m], "expert", other_across),
            (slots, turned_slots, member_turned, own_member, router_turned) if m == 0 else (),
        ).reshape(expert_devices, rows, width)
        for m in range(micro)
    ]
    for m in range(micro):
        back_part, arrived, out_rows, hidden, pre_low, mixed_rows = run_experts(
            m, moe_all[m], seed_all, slots, turned_slots, member_turned, router_turned, weights,
            tuple(mixed),
        )
        saved.append((arrived, out_rows, hidden, pre_low))
        backs.append(lax.all_to_all(back_part, "expert", 0, 0))
        mixed.append(mixed_rows)
    sent = weight_grads(core_flag, dp_devices, saved, (), ())
    received = [lax.ppermute(piece, "dp", other_core) for piece in sent]
    combined = run_combine(depth_flag, mixed, turned_slots, (sent[0], backs[0]))
    core_sum = weight_grads(core_flag, dp_devices, saved, received, (combined[0],))

    made, joint = [], ()
    for m in range(micro):
        result = run_middle_back(
            m, backs[m], own_member, seed_low, query, key_value, bias, moe_in[m], middle[m],
            peak[m], dense, turned, score_scale, (core_sum,), (), joint,
        )
        if m == 0:
            core_sum = pass_on(core_sum, (*backs, result[0]))
        made.append(result[:5])
        joint = tuple(result[5:7])
    mid_grads, branches, router_grads, query_grads, own_grads = zip(*made)
    ones = passed_along(joint[0], "expert", -1)
    twos = passed_along(joint[1], "expert", -2)
    across_low = lax.axis_index("dp") // 2 % 2
    place_flag = across_low[None].astype(jnp.int32)
    along_y = [[4 * y + place for y in range(dp_devices // 4)] for place in range(4)]
    over_y = lax.psum_scatter(
        core_sum.reshape((dp_devices // 4, 2, 2) + core_sum.shape[1:]),
        "dp",
        scatter_dimension=0,
        axis_index_groups=along_y,
    )
    over_y = over_y.reshape(over_y.shape[-5:])
    pieces = run_choose(place_flag, core_flag, over_y)
    exchanged = [
        lax.ppermute(piece, "dp", [(i, i ^ step) for i in range(dp_devices)])
        for piece, step in zip(pieces, (2, 1, 3))
    ]
    gate_owned, up_owned, down_owned = run_expert_owned(
        place_flag, core_flag, over_y, exchanged, upper, hidden_width
    )

    up = [(i, (i + 2) % expert_devices) for i in range(expert_devices)]
    down = [(i, (i - 2) % expert_devices) for i in range(expert_devices)]
    out_low = lax.ppermute(combined[2], "expert", up)
    out_high = lax.ppermute(combined[3], "expert", down)

    kept_in, sent_in, normed_grad, gain_sums = run_query_back(
        core_flag, dp_devices, pre, normed, cosine, sine, head_gains, dense, query_grads, attended,
        branches, router_grads, head_size, (out_low, out_high),
    )
    kept_in, sent_in, token_grad = run_tokens_back(
        core_flag, pre, normed, x_low, cosine, sine, head_gains, dense, turned, normed_grad,
        gain_sums, own_grads, mid_grads, ones, twos, kept_in, sent_in, head_size,
        (),
    )
    both = add_low(kept_in, lax.ppermute(sent_in, "dp", other_core), 4)
    parts = both.reshape(dp_devices // 4, 2 * both.shape[1], both.shape[2])
    parts = lax.all_to_all(parts, "dp", 0, 0, axis_index_groups=along_y)

    next_part, last_part = run_merge((combined[1], combined[4], out_low, out_high), (both,))
    out_parts = [
        combined[0], lax.ppermute(next_part, "expert", up), lax.ppermute(last_part, "expert", down)
    ]
    out_kept, out_sent = run_fold(across_flag, middle, out_parts, tuple(exchanged))
    out_other = lax.ppermute(out_sent, "expert", other_across)

    total = run_total(parts, (out_other, gate_owned))
    output = add_low(out_kept, out_other, micro, (total,))
    parts = total.reshape(2 * expert_devices, own_rows, -1)
    same_y = [
        [
            ((2 * y + place) * 2 + c) * expert_devices + e
            for place in range(2)
            for e in range(expert_devices)
        ]
        for y in range(dp_devices // 4)
        for c in range(2)
    ]
    parts = lax.all_to_all(parts, ("dp", "expert"), 0, 0, axis_index_groups=same_y)
    (
        key_owned, value_owned, attn_gain_owned, query_gain_owned, key_gain_owned,
        out_owned, router_owned, ffn_gain_owned, query_owned,
    ) = run_owned(parts, width, q_width, head_size, experts, (exchanged[0],))
    return (
        output.reshape(micro, 1, rows, width),
        token_grad.reshape(micro, 1, rows, width),
        attn_gain_owned.reshape(own_rows),
        query_owned,
        key_owned,
        value_owned,
        query_gain_owned.reshape(head_size),
        key_gain_owned.reshape(head_size),
        out_owned,
        ffn_gain_owned.reshape(own_rows),
        router_owned,
        gate_owned,
        up_owned,
        down_owned,
    )


def solution(mesh):
    rows_spec = P(("dp", "expert"), None)
    gain_spec = P(("dp", "expert"))
    token_spec = P(None, "dp", "expert", None)
    expert_spec = P("expert", "dp", None)
    return jax.shard_map(
        body,
        mesh=mesh,
        in_specs=(
            token_spec,
            token_spec,
            token_spec,
            P(None, "dp", None),
            P(None, "dp", "expert"),
            gain_spec,
            rows_spec,
            rows_spec,
            rows_spec,
            P(),
            P(),
            rows_spec,
            gain_spec,
            rows_spec,
            expert_spec,
            expert_spec,
            expert_spec,
        ),
        out_specs=(
            token_spec,
            token_spec,
            gain_spec,
            rows_spec,
            rows_spec,
            rows_spec,
            P(),
            P(),
            rows_spec,
            gain_spec,
            rows_spec,
            expert_spec,
            expert_spec,
            expert_spec,
        ),
        check_vma=False,
    )
```

```python
import functools
import math

import jax
import jax.numpy as jnp
from jax import lax
from jax.experimental import pallas as pl
from jax.experimental.pallas import tpu as pltpu
from jax.sharding import PartitionSpec as P

WINDOW = 256
EPSILON = 1e-06
ROPE_BASE = 10000.0
CAP = 48
EXTRA = 16
VMEM = 60 << 20
PIECES = 2
LIGHT = pl.CostEstimate(flops=1, bytes_accessed=1, transcendentals=0)

bf16 = jnp.bfloat16
f32 = jnp.float32


def rms_scale(values):
    return lax.rsqrt(jnp.mean(values * values, axis=-1, keepdims=True) + EPSILON)


def rope_tables(positions, head_size):
    half_size = head_size // 2
    frequency = jnp.exp(
        -math.log(ROPE_BASE) * (2.0 * jnp.arange(half_size, dtype=f32) / head_size)
    )
    angles = positions.astype(f32)[:, None] * frequency[None, :]
    angles = jnp.concatenate([angles, angles], axis=-1)
    return (jnp.cos(angles), jnp.sin(angles))


def norm_back(upstream, values, scaling):
    return scaling * upstream - values * (scaling * scaling * scaling) * jnp.mean(
        upstream * values, axis=-1, keepdims=True
    )


def product(left_side, right_side):
    return jnp.dot(left_side, right_side, preferred_element_type=f32)


def product_tn(left_side, right_side):
    return lax.dot_general(
        left_side, right_side, (((0,), (0,)), ((), ())), preferred_element_type=f32
    )


def product_nt(left_side, right_side):
    return lax.dot_general(
        left_side, right_side, (((1,), (1,)), ((), ())), preferred_element_type=f32
    )


def einsum(spec, left_side, right_side):
    return jnp.einsum(spec, left_side, right_side, preferred_element_type=f32)


def spread(values, axis):
    count = lax.axis_size(axis)
    return lax.all_to_all(jnp.broadcast_to(values[None], (count,) + values.shape), axis, 0, 0)


def passed_along(value, axis, steps):
    count = lax.axis_size(axis)
    initial, last = (max(0, -steps), min(count, count - steps))
    return lax.ppermute(value, axis, [(source, source + steps) for source in range(initial, last)])


def whole(shape):
    return pl.BlockSpec(shape, lambda *_: (0,) * len(shape))


def once(shape):
    return pl.BlockSpec(shape, lambda *_: (0,) * len(shape), pipeline_mode=pl.Buffered(1))


def put_back(turned, pieces):
    column = lax.broadcasted_iota(jnp.int32, (turned.shape[0], CAP), 1)
    hot = [(turned[:, j : j + 1] == column).astype(f32) for j in range(len(pieces))]
    hot = jnp.concatenate(hot, axis=1).astype(bf16)
    return product(hot, jnp.concatenate(pieces, axis=0)).astype(bf16)


def experts_kernel(
    moe_ref,
    seed_ref,
    slots_ref,
    turned_ref,
    member_ref,
    router_ref,
    weights_ref,
    *refs,
):
    back_ref, arrived_ref, out_rows_ref, hidden_ref, pre_ref, mixed_ref = refs[-11:-5]
    taken, seeds, backs, row_gates, row_grads = refs[-5:]
    step = pl.program_id(0)
    blocks, rows, width = moe_ref.shape
    local = taken.shape[0]
    hidden_width = hidden_ref.shape[2]

    def picks(b, j):
        index = lax.broadcasted_iota(jnp.int32, (CAP, rows), 0)
        return slots_ref[b, j : j + 1, :] == index

    @pl.when(step == 0)
    def dispatch():
        for b in range(blocks):
            tokens = moe_ref[b]
            logits = product_nt(router_ref[...], tokens)
            member = member_ref[b] > 0.5
            shown = jnp.where(member, logits, -1e30)
            exps = jnp.where(member, jnp.exp(shown - jnp.max(shown, axis=0, keepdims=True)), 0.0)
            gates = exps / jnp.sum(exps, axis=0, keepdims=True)
            masks = [picks(b, j) for j in range(local)]
            pick = jnp.concatenate([m.astype(f32) for m in masks], axis=0).astype(bf16)
            arrived = product(pick, tokens).astype(bf16)
            seeded = product(pick, seed_ref[b // 2, b % 2, 0]).astype(bf16)
            for j in range(local):
                at = pl.ds(b * CAP, CAP)
                taken[j, at, :] = arrived[j * CAP : (j + 1) * CAP]
                seeds[j, at, :] = seeded[j * CAP : (j + 1) * CAP]
                row_gates[j, at, :] = jnp.sum(
                    jnp.where(masks[j], gates[j : j + 1, :], 0.0), axis=1, keepdims=True
                )

    def expert():
        upper = width // weights_ref.shape[1]
        gate_up_weights = weights_ref[0, :, :upper, :].reshape(width, 2 * hidden_width)
        down_weights = weights_ref[0, :, upper:, :].reshape(hidden_width, width)
        arrived_ref[0] = taken[step]
        pre = product(taken[step], gate_up_weights)
        gate_pre = pre[:, :hidden_width]
        up_pre = pre[:, hidden_width:]
        sigma = 1.0 / (1.0 + jnp.exp(-gate_pre))
        gate_act = gate_pre * sigma
        hidden = (gate_act * up_pre).astype(bf16)
        hidden_ref[0] = hidden
        expert_out = product(hidden, down_weights).astype(bf16).astype(f32)
        seed_rows = seeds[step].astype(f32)
        gate_column = row_gates[step]
        row_grads[step] = jnp.sum(expert_out * seed_rows, axis=1, keepdims=True)
        mixed_ref[0] = (gate_column * expert_out).astype(bf16)
        out_rows = (gate_column * seed_rows).astype(bf16)
        out_rows_ref[0] = out_rows
        hidden_grad = product_nt(out_rows, down_weights)
        gate_low = (hidden_grad * up_pre * sigma * (1.0 + gate_pre * (1.0 - sigma))).astype(bf16)
        up_low = (hidden_grad * gate_act).astype(bf16)
        pre_ref[0, :, :hidden_width] = gate_low
        pre_ref[0, :, hidden_width:] = up_low
        backs[step] = product_nt(pre_ref[0], gate_up_weights).astype(bf16)

    expert()

    @pl.when(step == local - 1)
    def combine():
        for b in range(blocks):
            at = pl.ds(b * CAP, CAP)
            back_ref[b, :rows, :] = put_back(
                turned_ref[b], [backs[j, at, :] for j in range(local)]
            )
            gate_grads = [
                jnp.sum(jnp.where(picks(b, j), row_grads[j, at, :], 0.0), axis=0, keepdims=True)
                for j in range(local)
            ]
            gate_grads = jnp.concatenate(
                gate_grads + [jnp.zeros((1, width - local * rows), f32)], axis=1
            )
            high = gate_grads.astype(bf16).astype(f32)
            row = lax.broadcasted_iota(jnp.int32, (EXTRA, width), 0)
            back_ref[b, rows:, :] = jnp.where(
                row == 0, high, jnp.where(row == 1, gate_grads - high, 0.0)
            ).astype(bf16)


def run_experts(m, tokens, seeds, slots, turned, member, router, weights, after):
    blocks, rows, width = tokens.shape
    local, owners, each, wide = weights.shape
    hidden_width = wide // 2
    held = blocks * CAP
    shapes = [
        ((blocks, rows + EXTRA, width), bf16),
        ((local, held, width), bf16),
        ((local, held, width), bf16),
        ((local, held, hidden_width), bf16),
        ((local, held, wide), bf16),
        ((local, held, width), bf16),
    ]
    return pl.pallas_call(
        experts_kernel,
        grid=(local,),
        in_specs=[
            once(tokens.shape),
            pl.BlockSpec(
                seeds.shape[:2] + (1,) + seeds.shape[3:],
                lambda j: (0, 0, m, 0, 0),
                pipeline_mode=pl.Buffered(1),
            ),
            picked(slots, m),
            picked(turned, m),
            picked(member, m),
            once(router.shape),
            pl.BlockSpec((1, owners, each, wide), lambda j: (j, 0, 0, 0)),
        ]
        + [pl.BlockSpec(memory_space=pl.ANY)] * len(after),
        out_specs=[once(shapes[0][0])]
        + [pl.BlockSpec((1,) + shape[1:], lambda j: (j, 0, 0)) for shape, _ in shapes[1:]],
        out_shape=[jax.ShapeDtypeStruct(shape, kind) for shape, kind in shapes],
        scratch_shapes=[
            pltpu.VMEM((local, held, width), bf16),
            pltpu.VMEM((local, held, width), bf16),
            pltpu.VMEM((local, held, width), bf16),
            pltpu.VMEM((local, held, 1), f32),
            pltpu.VMEM((local, held, 1), f32),
        ],
        compiler_params=pltpu.CompilerParams(vmem_limit_bytes=VMEM),
        cost_estimate=LIGHT,
        name="experts",
    )(tokens, seeds, slots, turned, member, router, weights, *after)


def weight_grads_kernel(micro, adding, core_ref, *refs):
    del core_ref
    parts = [refs[4 * m : 4 * m + 4] for m in range(micro)]
    gate_up = sum(product_tn(p[0][0], p[3][0]) for p in parts)
    down = sum(product_tn(p[2][0], p[1][0]) for p in parts)
    outs = refs[-1:] if adding else refs[-PIECES:]
    owners = sum(ref.shape[0] for ref in outs)
    upper = gate_up.shape[0] // owners
    gate_up = gate_up.reshape(owners, upper, gate_up.shape[1])
    down = down.reshape(owners, down.shape[0] // owners, down.shape[1])
    each = owners // PIECES
    for n in range(PIECES):
        part = slice(n * each, (n + 1) * each)
        above, below = gate_up[part], down[part]
        if adding:
            received_ref = refs[4 * micro + n]
            above = above + received_ref[:, 0, :upper, :].astype(f32)
            below = below + received_ref[:, 0, upper:, :].astype(f32)
            outs[0][part, 0, :upper, :] = above.astype(bf16)
            outs[0][part, 0, upper:, :] = below.astype(bf16)
        else:
            outs[n][:, 0, :upper, :] = above.astype(bf16)
            outs[n][:, 0, upper:, :] = below.astype(bf16)


def combine_kernel(micro, depth_ref, *refs):
    mixed, turned = refs[:micro], refs[micro]
    own_ref, next_ref, low_ref, high_ref, last_ref = refs[-5:]
    local = mixed[0].shape[0]
    for ahead in range(4):
        target = lax.rem(depth_ref[0] + ahead, 4)
        for x in range(2):
            b = 2 * target + x
            at = pl.ds(pl.multiple_of(b * CAP, CAP), CAP)
            for m in range(micro):
                made = put_back(turned[m, b], [mixed[m][j, at, :] for j in range(local)])
                if ahead == 2:
                    (low_ref, high_ref)[x][m] = made
                else:
                    (own_ref, next_ref, None, last_ref)[ahead][x, m] = made


def run_combine(depth, mixed, turned, after):
    micro, _, rows, _ = turned.shape
    width = mixed[0].shape[2]
    pair, half = (2, micro, rows, width), (micro, rows, width)
    shapes = [pair, pair, half, half, pair]
    return pl.pallas_call(
        functools.partial(combine_kernel, micro),
        grid=(1,),
        in_specs=[pl.BlockSpec(memory_space=pltpu.SMEM)]
        + [whole(a.shape) for a in (*mixed, turned)]
        + [pl.BlockSpec(memory_space=pl.ANY)] * len(after),
        out_specs=[whole(shape) for shape in shapes],
        out_shape=[jax.ShapeDtypeStruct(shape, bf16) for shape in shapes],
        compiler_params=pltpu.CompilerParams(vmem_limit_bytes=VMEM),
        cost_estimate=LIGHT,
        name="combine",
    )(depth, *mixed, turned, *after)


def merge_kernel(next_ref, low_ref, high_ref, *refs):
    refs[-1][0] = (next_ref[0].astype(f32) + low_ref[...].astype(f32)).astype(bf16)
    refs[-1][1] = (next_ref[1].astype(f32) + high_ref[...].astype(f32)).astype(bf16)


def run_merge(parts, after):
    shape = parts[0].shape
    return pl.pallas_call(
        merge_kernel,
        grid=(1,),
        in_specs=[whole(a.shape) for a in parts]
        + [pl.BlockSpec(memory_space=pl.ANY)] * len(after),
        out_specs=whole(shape),
        out_shape=jax.ShapeDtypeStruct(shape, bf16),
        compiler_params=pltpu.CompilerParams(vmem_limit_bytes=16 << 20),
        cost_estimate=LIGHT,
        name="merge",
    )(*parts, *after)


def fold_kernel(micro, across_ref, *refs):
    kept_ref, sent_ref = refs[-2:]
    middles, parts = refs[:micro], refs[micro : micro + 3]

    def place(kept, sent):
        for m in range(micro):
            total = middles[m][...]
            for part in parts:
                total = total + part[kept, m].astype(f32)
            kept_ref[m] = total
            total = parts[0][sent, m].astype(f32)
            for part in parts[1:]:
                total = total + part[sent, m].astype(f32)
            sent_ref[m] = total.astype(bf16)

    @pl.when(across_ref[0] == 0)
    def low_x():
        place(0, 1)

    @pl.when(across_ref[0] == 1)
    def high_x():
        place(1, 0)


def run_fold(across, middles, parts, after):
    micro = len(middles)
    shape = (micro,) + middles[0].shape
    return pl.pallas_call(
        functools.partial(fold_kernel, micro),
        grid=(1,),
        in_specs=[pl.BlockSpec(memory_space=pltpu.SMEM)]
        + [whole(a.shape) for a in (*middles, *parts)]
        + [pl.BlockSpec(memory_space=pl.ANY)] * len(after),
        out_specs=[whole(shape)] * 2,
        out_shape=[jax.ShapeDtypeStruct(shape, f32), jax.ShapeDtypeStruct(shape, bf16)],
        compiler_params=pltpu.CompilerParams(vmem_limit_bytes=16 << 20),
        cost_estimate=LIGHT,
        name="fold",
    )(across, *middles, *parts, *after)


def weight_grads(core, owners, saved, received, after):
    local, held, width = saved[0][0].shape
    hidden_width = saved[0][2].shape[2]
    depth = (width + hidden_width) // owners
    micro, count = len(saved), local // 2
    own = bool(received)

    def expert(j, core_ref):
        side = core_ref[0] if own else 1 - core_ref[0]
        return (side * count + j, 0, 0)

    piece = (owners // PIECES, count, depth, width)
    each = (owners // PIECES, 1, depth, width)
    pieces = [pl.BlockSpec(each, lambda j, core_ref: (0, j, 0, 0))] * PIECES
    flat = [a for group in saved for a in group]
    return pl.pallas_call(
        functools.partial(weight_grads_kernel, micro, own),
        grid_spec=pltpu.PrefetchScalarGridSpec(
            num_scalar_prefetch=1,
            grid=(count,),
            in_specs=[pl.BlockSpec((1,) + a.shape[1:], expert) for a in flat]
            + pieces[: len(received)]
            + [pl.BlockSpec(memory_space=pl.ANY)] * len(after),
            out_specs=pl.BlockSpec((owners, 1, depth, width), lambda j, core_ref: (0, j, 0, 0))
            if own
            else pieces,
        ),
        out_shape=jax.ShapeDtypeStruct((owners, count, depth, width), bf16)
        if own
        else [jax.ShapeDtypeStruct(piece, bf16)] * PIECES,
        compiler_params=pltpu.CompilerParams(vmem_limit_bytes=VMEM),
        cost_estimate=LIGHT,
        name="weight_grads",
    )(core, *flat, *received, *after)


def pass_kernel(*refs):
    del refs


def pass_on(value, after):
    return pl.pallas_call(
        pass_kernel,
        in_specs=[pl.BlockSpec(memory_space=pl.ANY)] * (1 + len(after)),
        out_specs=pl.BlockSpec(memory_space=pl.ANY),
        out_shape=jax.ShapeDtypeStruct(value.shape, value.dtype),
        input_output_aliases={0: 0},
        compiler_params=pltpu.CompilerParams(vmem_limit_bytes=VMEM),
        cost_estimate=LIGHT,
        name="pass_on",
    )(value, *after)


def choose_kernel(place_ref, core_ref, parts_ref, *refs):
    place, core = place_ref[0], core_ref[0]
    refs[0][...] = parts_ref[1 - place, core]
    refs[1][...] = parts_ref[place, 1 - core]
    refs[2][...] = parts_ref[1 - place, 1 - core]


def run_choose(place, core, parts):
    shape = parts.shape[2:]
    return pl.pallas_call(
        choose_kernel,
        grid=(1,),
        in_specs=[pl.BlockSpec(memory_space=pltpu.SMEM)] * 2 + [whole(parts.shape)],
        out_specs=[whole(shape)] * 3,
        out_shape=[jax.ShapeDtypeStruct(shape, bf16)] * 3,
        compiler_params=pltpu.CompilerParams(vmem_limit_bytes=12 << 20),
        cost_estimate=LIGHT,
        name="choose",
    )(place, core, parts)


def expert_owned_kernel(place_ref, core_ref, parts_ref, across_ref, other_ref, both_ref, *refs):
    gate_ref, up_ref, down_ref = refs
    upper, half = gate_ref.shape[1], gate_ref.shape[2]
    place, core = place_ref[0], core_ref[0]
    count = across_ref.shape[0]

    def put(at, total):
        gate_ref[at] = total[:upper, :half]
        up_ref[at] = total[:upper, half:]
        down_ref[at] = total[upper:]

    for n in range(count):
        own = parts_ref[place, core, n].astype(f32) + across_ref[n].astype(f32)
        put(core * count + n, own)
        put((1 - core) * count + n, other_ref[n].astype(f32) + both_ref[n].astype(f32))


def run_expert_owned(place, core, parts, received, upper, half):
    count, depth, width = received[0].shape
    count = 2 * count
    shapes = [(count, upper, half), (count, upper, half), (count, depth - upper, width)]
    return pl.pallas_call(
        expert_owned_kernel,
        grid=(1,),
        in_specs=[pl.BlockSpec(memory_space=pltpu.SMEM)] * 2
        + [whole(a.shape) for a in (parts, *received)],
        out_specs=[whole(shape) for shape in shapes],
        out_shape=[jax.ShapeDtypeStruct(shape, f32) for shape in shapes],
        compiler_params=pltpu.CompilerParams(vmem_limit_bytes=12 << 20),
        cost_estimate=LIGHT,
        name="expert_owned",
    )(place, core, parts, *received)


def lanes_like(shape):
    return lax.broadcasted_iota(jnp.int32, shape, len(shape) - 1)


def head_sums(values):
    left = lax.broadcasted_iota(jnp.int32, (128, 128), 0) // 32
    right = lax.broadcasted_iota(jnp.int32, (128, 128), 1) // 32
    ones = (left == right).astype(f32).astype(bf16)
    high = values.astype(bf16)
    rest = (values - high.astype(f32)).astype(bf16)
    return product(high, ones) + product(rest, ones)


def columns(dense, start, size):
    return pl.BlockSpec((dense.shape[0], size), lambda *_: (0, start // size))


def pair_kernel(across_ref, own_ref, other_ref, *refs):
    out_ref = refs[-1]

    @pl.when(across_ref[0] == 0)
    def low_x():
        out_ref[0, 0] = own_ref[...]
        out_ref[0, 1] = other_ref[...]

    @pl.when(across_ref[0] == 1)
    def high_x():
        out_ref[0, 0] = other_ref[...]
        out_ref[0, 1] = own_ref[...]


def run_pair(across, own, other, count, after):
    shape = (count, 2) + own.shape
    zeros = (0,) * own.ndim
    return pl.pallas_call(
        pair_kernel,
        grid=(count,),
        in_specs=[pl.BlockSpec(memory_space=pltpu.SMEM), whole(own.shape), whole(other.shape)]
        + [pl.BlockSpec(memory_space=pl.ANY)] * len(after),
        out_specs=pl.BlockSpec((1, 2) + own.shape, lambda i: (i, 0) + zeros),
        out_shape=jax.ShapeDtypeStruct(shape, own.dtype),
        compiler_params=pltpu.CompilerParams(vmem_limit_bytes=16 << 20),
        cost_estimate=LIGHT,
        name="pair",
    )(across, own, other, *after)


def pack_kernel(packed_ref, *refs):
    width = refs[-1].shape[1]
    for n in range(packed_ref.shape[0]):
        rows = packed_ref.shape[1]
        refs[-1][n * rows : (n + 1) * rows, :] = packed_ref[n, :, :width]


def run_pack(packed, width, after):
    count, rows, _ = packed.shape
    return pl.pallas_call(
        pack_kernel,
        grid=(1,),
        in_specs=[whole(packed.shape)] + [pl.BlockSpec(memory_space=pl.ANY)] * len(after),
        out_specs=whole((count * rows, width)),
        out_shape=jax.ShapeDtypeStruct((count * rows, width), packed.dtype),
        compiler_params=pltpu.CompilerParams(vmem_limit_bytes=8 << 20),
        cost_estimate=LIGHT,
        name="pack",
    )(packed, *after)


def group_stack(query_ref, g, q_half):
    lane = lanes_like((1, 256)) % 128 // 32
    pieces = []
    for i in range(4):
        for r in range(2):
            at = r * q_half + g * 256
            block = query_ref[:, at : at + 256]
            pieces.append(jnp.where(lane == i, block, jnp.zeros_like(block)))
    return jnp.concatenate(pieces, axis=0)


def doubled_values(values, h):
    block = values[:, h // 2 * 128 : h // 2 * 128 + 128]
    swapped = pltpu.roll(block, 64, 1)
    low_half = lanes_like(block.shape) < 64
    return jnp.where(low_half == (h % 2 == 0), block, swapped).astype(bf16)


def group_scores(keys, stack, bias, score_scale):
    scores = product_nt(keys, stack) * score_scale
    return scores + jnp.concatenate([bias] * 8, axis=1)


def rotated(u1, u2, cosine, sine, gain1, gain2, head_size):
    scale = lax.rsqrt(head_sums(u1 * u1 + u2 * u2) / head_size + EPSILON)
    u1 = u1 * scale * gain1
    u2 = u2 * scale * gain2
    return (
        (u1 * cosine - u2 * sine).astype(bf16),
        (u2 * cosine + u1 * sine).astype(bf16),
    )


def front_kernel(
    head_size,
    own_ref,
    one_ref,
    two_ref,
    weights_ref,
    out_weights_ref,
    tail_ref,
    cosine_ref,
    sine_ref,
    gains_ref,
    bias_ref,
    *refs,
):
    micro, rows, width = own_ref.shape
    first, rest = refs[-4 * micro - 5 : -4 * micro], refs[-4 * micro :]
    normed_ref, pre_ref, query_ref, key_value_ref, turned_ref = first
    q_width = query_ref.shape[2]
    kv_width = q_width // 2
    groups = kv_width // 256
    score_scale = 1.0 / math.sqrt(head_size)
    turned = tail_ref[...].astype(f32).T
    turned_ref[...] = turned
    gain = turned[33:34, :]
    low_half = lanes_like((rows, 128)) < 64
    head_gains = [gains_ref[n : n + 1, :] for n in range(4)]

    def norm(x):
        return (x * rms_scale(x) * gain).astype(bf16)

    for m in range(micro):
        attended_ref, middle_ref, moe_ref, peak_ref = rest[4 * m : 4 * m + 4]
        x = own_ref[m].astype(f32)
        normed = norm(x)
        normed_ref[m] = normed
        own = product(normed, weights_ref[...])
        pre_ref[m] = own[:, : q_width + kv_width]
        own_rows = pl.ds(2 * rows, rows)
        for at in range(0, q_width, 256):
            made = rotated(
                own[:, at : at + 128], own[:, at + 128 : at + 256],
                cosine_ref[own_rows, :], sine_ref[own_rows, :],
                head_gains[0], head_gains[1], head_size,
            )
            query_ref[m, :, at : at + 128] = made[0]
            query_ref[m, :, at + 128 : at + 256] = made[1]
        earlier = jnp.concatenate(
            [norm(two_ref[m].astype(f32)), norm(one_ref[m].astype(f32))], axis=0
        )
        earlier = product(earlier, weights_ref[:, q_width:])
        both = jnp.concatenate([earlier, own[:, q_width:]], axis=0)
        key_value_ref[m, :, kv_width:] = both[:, kv_width:].astype(bf16)
        for at in range(0, kv_width, 256):
            made = rotated(
                both[:, at : at + 128], both[:, at + 128 : at + 256],
                cosine_ref[...], sine_ref[...], head_gains[2], head_gains[3], head_size,
            )
            key_value_ref[m, :, at : at + 128] = made[0]
            key_value_ref[m, :, at + 128 : at + 256] = made[1]

        bias = bias_ref[m]
        values = key_value_ref[m, :, kv_width:].astype(f32)
        for g in range(groups):
            keys = key_value_ref[m, :, g * 256 : (g + 1) * 256]
            stack = group_stack(query_ref.at[m], g, q_width // 2)
            scores = group_scores(keys, stack, bias, score_scale)
            peak = jnp.max(scores, axis=0, keepdims=True)
            exps = jnp.exp(scores - peak)
            total = jnp.sum(exps, axis=0, keepdims=True)
            probs = (exps * (1.0 / total)).astype(bf16)
            peak_ref[g : g + 1, :] = peak + jnp.log(total)
            for i in range(4):
                h = 4 * g + i
                mixed = product_tn(probs[:, i * 256 : (i + 1) * 256], doubled_values(values, h))
                attended_ref[:, h * 128 : (h + 1) * 128] = jnp.where(
                    low_half, mixed[:rows], mixed[rows:]
                ).astype(bf16)
        middle = x + product(attended_ref[...], out_weights_ref[...])
        middle_ref[...] = middle
        moe_ref[...] = (middle * rms_scale(middle) * turned[32:33, :]).astype(bf16)


def picked(array, m):
    return pl.BlockSpec(
        (None,) + array.shape[1:], lambda *_: (m,) + (0,) * (len(array.shape) - 1)
    )


def run_front(own, one, two, dense, cosine, sine, gains, bias, head_size, q_width, after):
    micro, rows, width = own.shape
    kv_width = q_width // 2
    shapes = [
        ((micro, rows, width), bf16),
        ((micro, rows, q_width + kv_width), f32),
        ((micro, rows, q_width), bf16),
        ((micro, 3 * rows, 2 * kv_width), bf16),
        ((128, width), f32),
    ] + [
        ((rows, q_width), bf16),
        ((rows, width), f32),
        ((rows, width), bf16),
        ((8, 8 * rows), f32),
    ] * micro
    small = (cosine, sine, gains, bias)
    return pl.pallas_call(
        functools.partial(front_kernel, head_size),
        grid=(1,),
        in_specs=[whole(own.shape)] * 3
        + [
            columns(dense, 0, 2 * q_width),
            columns(dense, 2 * q_width, width),
            columns(dense, 2 * q_width + width, 128),
        ]
        + [whole(a.shape) for a in small]
        + [pl.BlockSpec(memory_space=pl.ANY)] * len(after),
        out_specs=[whole(shape) for shape, _ in shapes],
        out_shape=[jax.ShapeDtypeStruct(shape, kind) for shape, kind in shapes],
        compiler_params=pltpu.CompilerParams(vmem_limit_bytes=VMEM),
        cost_estimate=LIGHT,
        name="front",
    )(own, one, two, dense, dense, dense, *small, *after)


def add_kernel(left_ref, right_ref, *refs):
    total = left_ref[...].astype(f32) + right_ref[...].astype(f32)
    refs[-1][...] = total.astype(bf16)


def total_kernel(parts_ref, *refs):
    total = parts_ref[0].astype(f32)
    for n in range(1, parts_ref.shape[0]):
        total = total + parts_ref[n].astype(f32)
    refs[-1][...] = total.astype(refs[-1].dtype)


def run_total(parts, after):
    shape = parts.shape[1:]
    return pl.pallas_call(
        total_kernel,
        grid=(1,),
        in_specs=[whole(parts.shape)] + [pl.BlockSpec(memory_space=pl.ANY)] * len(after),
        out_specs=whole(shape),
        out_shape=jax.ShapeDtypeStruct(shape, bf16),
        compiler_params=pltpu.CompilerParams(vmem_limit_bytes=16 << 20),
        cost_estimate=LIGHT,
        name="total",
    )(parts, *after)


def owned_kernel(parts_ref, *refs):
    outs = refs[-9:]
    key_ref, value_ref, attn_ref, query_gain_ref, key_gain_ref = outs[:5]
    out_ref, router_ref, ffn_ref, query_ref = outs[5:]
    kv_width, width, q_width = key_ref.shape[1], out_ref.shape[1], query_ref.shape[1]
    experts = router_ref.shape[1]
    rows = parts_ref.shape[1]
    total = parts_ref[0].astype(f32)
    for n in range(1, parts_ref.shape[0]):
        total = total + parts_ref[n].astype(f32)
    run = lanes_like((rows, 128)) // 32

    def gathered(base, sources):
        made = None
        for j, (block, place) in enumerate(sources):
            at = base + block * 128
            piece = total[:, at : at + 128]
            if place != j:
                piece = pltpu.roll(piece, (j - place) % 4 * 32, 1)
            made = piece if made is None else jnp.where(run == j, piece, made)
        return made

    for block in range(kv_width // 128):
        sources = []
        for j in range(4):
            head, half = 2 * block + j // 2, j % 2
            sources.append((head // 4 * 2 + half, head % 4))
        key_ref[:, block * 128 : (block + 1) * 128] = gathered(0, sources)
    at = kv_width
    value_ref[...] = total[:, at : at + kv_width]
    at += kv_width
    extra = total[:, at : at + 128]
    at += 128
    turned = jnp.concatenate([extra, jnp.zeros((128 - rows, 128), f32)], axis=0).T
    attn_ref[...] = turned[0:1, :rows]
    query_gain_ref[...] = extra[0:1, 64:]
    key_gain_ref[...] = extra[1:2, 64:]
    out_ref[...] = total[:, at : at + width]
    at += width
    tail = total[:, at : at + 128]
    at += 128
    router_ref[...] = tail[:, :experts]
    turned = jnp.concatenate([tail, jnp.zeros((128 - rows, 128), f32)], axis=0).T
    ffn_ref[...] = turned[experts : experts + 1, :rows]
    for block in range(q_width // 128):
        sources = []
        for j in range(4):
            r, half = j // 2, j % 2
            sources.append((r * (q_width // 256) + block // 4 * 2 + half, block % 4))
        query_ref[:, block * 128 : (block + 1) * 128] = gathered(at, sources)


def run_owned(parts, width, q_width, head_size, experts, after):
    rows = parts.shape[1]
    kv_width = q_width // 2
    shapes = [
        (rows, kv_width), (rows, kv_width), (1, rows), (1, head_size), (1, head_size),
        (rows, width), (rows, experts), (1, rows), (rows, q_width),
    ]
    return pl.pallas_call(
        owned_kernel,
        grid=(1,),
        in_specs=[whole(parts.shape)] + [pl.BlockSpec(memory_space=pl.ANY)] * len(after),
        out_specs=[whole(shape) for shape in shapes],
        out_shape=[jax.ShapeDtypeStruct(shape, f32) for shape in shapes],
        compiler_params=pltpu.CompilerParams(vmem_limit_bytes=8 << 20),
        cost_estimate=LIGHT,
        name="owned",
    )(parts, *after)


def add_low(left, right, each, after=()):
    block = pl.BlockSpec((each,) + left.shape[1:], lambda i: (i,) + (0,) * (left.ndim - 1))
    return pl.pallas_call(
        add_kernel,
        grid=(left.shape[0] // each,),
        in_specs=[block, block] + [pl.BlockSpec(memory_space=pl.ANY)] * len(after),
        out_specs=block,
        out_shape=jax.ShapeDtypeStruct(left.shape, bf16),
        compiler_params=pltpu.CompilerParams(vmem_limit_bytes=16 << 20),
        cost_estimate=LIGHT,
        name="add_low",
    )(left, right, *after)


def fetch(sources, targets, sems):
    copies = [
        pltpu.make_async_copy(source, target, sems.at[n])
        for n, (source, target) in enumerate(zip(sources, targets))
    ]
    for copy in copies:
        copy.start()
    return copies


def middle_back_kernel(score_scale, m, count, *refs):
    sources = refs[:count]
    buffers, sems = refs[-count - 1 : -1], refs[-1]
    outs = refs[-count - 8 : -count - 1]
    mid_grad_ref, branch_ref, router_grad_ref, query_grad_ref, own_grad_ref = outs[:5]
    one_grad_ref, two_grad_ref = outs[5:]
    dense = sources[0]
    width = dense.shape[0]
    out_columns = dense.at[:, pl.ds(2 * width, width)]
    by_micro = tuple(source.at[m] for source in sources[2:7])
    copies = fetch((out_columns, sources[1], *by_micro, *sources[7:]), buffers, sems)
    out_weights_ref, turned_ref, member_ref, seed_ref, query_ref, key_value_ref, bias_ref = buffers[:7]
    parts_ref, moe_ref, middle_ref, peak_ref = buffers[7:11]
    rows, q_width = query_ref.shape
    kv_width = key_value_ref.shape[1] // 2
    groups = kv_width // 256
    experts = member_ref.shape[0]
    low_half = lanes_like((rows, 128)) < 64
    low_rows = lanes_like((3 * rows, 128)) < 64
    lane = lanes_like((1, 256)) % 128 // 32
    q_half = q_width // 2
    for n in (1, 2, 3, 7, 8, 9, 10):
        copies[n].wait()
    router = turned_ref[:experts, :].astype(bf16)
    senders = parts_ref.shape[0]
    moe_in = moe_ref[...]
    member = member_ref[...] > 0.5
    shown = jnp.where(member, product_nt(router, moe_in), -1e30)
    exps = jnp.where(member, jnp.exp(shown - jnp.max(shown, axis=0, keepdims=True)), 0.0)
    gates = exps / jnp.sum(exps, axis=0, keepdims=True)
    gate_grad = []
    for s in range(senders):
        row = parts_ref[s, rows:, :].astype(f32)
        row = row[0:1] + row[1:2]
        for j in range(experts // senders):
            gate_grad.append(row[:, j * rows : (j + 1) * rows])
    gate_grad = jnp.concatenate(gate_grad, axis=0)
    logit_grad = gates * (gate_grad - jnp.sum(gates * gate_grad, axis=0, keepdims=True))
    logit_grad = logit_grad.astype(bf16)
    moe_grad = product_tn(logit_grad, router)
    for s in range(senders):
        moe_grad = moe_grad + parts_ref[s, :rows, :].astype(f32)
    middle = middle_ref[...]
    scale = rms_scale(middle)
    router_grad_ref[:experts, :] = product(logit_grad, moe_in)
    router_grad_ref[experts : experts + 1, :] = jnp.sum(
        moe_grad * middle * scale, axis=0, keepdims=True
    )
    mid_grad = seed_ref[...].astype(f32) + norm_back(
        moe_grad * turned_ref[32:33, :], middle, scale
    )
    mid_grad_ref[...] = mid_grad
    branch = mid_grad.astype(bf16)
    branch_ref[...] = branch
    for n in (0, 4, 5, 6):
        copies[n].wait()
    attended_grad = product_nt(branch, out_weights_ref[...]).astype(bf16)

    bias = bias_ref[...]
    values = key_value_ref[:, kv_width:].astype(f32)

    def store(columns, gradient):
        two_grad_ref[:, columns] = gradient[:rows].astype(bf16)
        one_grad_ref[:, columns] = gradient[rows : 2 * rows].astype(bf16)
        own_grad_ref[:, columns] = gradient[2 * rows :]

    for g in range(groups):
        keys = key_value_ref[:, g * 256 : (g + 1) * 256]
        stack = group_stack(query_ref, g, q_half)
        scores = group_scores(keys, stack, bias, score_scale)
        probs = jnp.exp(scores - peak_ref[g : g + 1, :])
        probs_low = probs.astype(bf16)
        prob_grads, value_grads = [], []
        for i in range(4):
            h = 4 * g + i
            block = attended_grad[:, h * 128 : (h + 1) * 128]
            zero = jnp.zeros_like(block)
            masked = jnp.concatenate(
                [jnp.where(low_half, block, zero), jnp.where(low_half, zero, block)], axis=0
            )
            prob_grads.append(product_nt(doubled_values(values, h), masked))
            both = product(probs_low[:, i * 256 : (i + 1) * 256], masked)
            value_grads.append(both + pltpu.roll(both, 64, 1))
        prob_grad = jnp.concatenate(prob_grads, axis=1)
        inner = jnp.sum(probs * prob_grad, axis=0, keepdims=True)
        score_low = (score_scale * probs * (prob_grad - inner)).astype(bf16)
        for pair in range(2):
            merged = jnp.where(low_rows, value_grads[2 * pair], value_grads[2 * pair + 1])
            at = kv_width + (2 * g + pair) * 128
            store(slice(at, at + 128), merged)
        store(slice(g * 256, (g + 1) * 256), product(score_low, stack))
        spread_grad = product_tn(score_low, keys)
        for r in range(2):
            total = jnp.zeros((rows, 256), f32)
            for i in range(4):
                at = (2 * i + r) * rows
                total = jnp.where(lane == i, spread_grad[at : at + rows], total)
            at = r * q_half + g * 256
            query_grad_ref[:, at : at + 256] = total


def run_middle_back(
    m, parts, member, seeds, query, key_value, bias, moe_in, middle, peak, dense, turned,
    score_scale, after,
):
    micro, rows, width = seeds.shape
    q_width = query.shape[2]
    shapes = [
        ((rows, width), f32),
        ((rows, width), bf16),
        ((40, width), f32),
        ((rows, q_width), f32),
        ((rows, q_width), f32),
        ((rows, q_width), bf16),
        ((rows, q_width), bf16),
    ]
    by_micro = (member, seeds, query, key_value, bias)
    ins = (dense, turned, *by_micro, parts, moe_in, middle, peak)
    held = (
        [pltpu.VMEM((width, width), bf16), pltpu.VMEM(turned.shape, f32)]
        + [pltpu.VMEM(a.shape[1:], a.dtype) for a in by_micro]
        + [pltpu.VMEM(a.shape, a.dtype) for a in ins[7:]]
    )
    count = len(ins)
    return pl.pallas_call(
        functools.partial(middle_back_kernel, score_scale, m, count),
        grid=(1,),
        in_specs=[pl.BlockSpec(memory_space=pl.ANY)] * (count + len(after)),
        out_specs=[whole(shape) for shape, _ in shapes],
        out_shape=[jax.ShapeDtypeStruct(shape, kind) for shape, kind in shapes],
        scratch_shapes=held + [pltpu.SemaphoreType.DMA((count,))],
        compiler_params=pltpu.CompilerParams(vmem_limit_bytes=VMEM),
        cost_estimate=LIGHT,
        name="middle_back",
    )(*ins, *after)


def by_core(core_ref, values, kept_ref, sent_ref, at):
    halves, depth = kept_ref.shape[0], kept_ref.shape[1]
    pairs = values.reshape(halves, 2, depth, values.shape[1])
    columns = pl.ds(at, values.shape[1])

    @pl.when(core_ref[0] == 0)
    def even():
        kept_ref[:, :, columns] = pairs[:, 0]
        sent_ref[:, :, columns] = pairs[:, 1]

    @pl.when(core_ref[0] == 1)
    def odd():
        kept_ref[:, :, columns] = pairs[:, 1]
        sent_ref[:, :, columns] = pairs[:, 0]


def head_back(u1, u2, up1, up2, cosine, sine, gain1, gain2, head_size):
    back1 = up1 * cosine + up2 * sine
    back2 = up2 * cosine - up1 * sine
    scale = lax.rsqrt(head_sums(u1 * u1 + u2 * u2) / head_size + EPSILON)
    sum1 = jnp.sum(back1 * u1 * scale, axis=0, keepdims=True)
    sum2 = jnp.sum(back2 * u2 * scale, axis=0, keepdims=True)
    back1 = back1 * gain1
    back2 = back2 * gain2
    mean = head_sums(back1 * u1 + back2 * u2) / head_size
    cube = scale * scale * scale
    low1 = (scale * back1 - u1 * cube * mean).astype(bf16)
    low2 = (scale * back2 - u2 * cube * mean).astype(bf16)
    return low1, low2, sum1, sum2


def query_back_kernel(
    head_size, micro, core_ref, pre_ref, normed_ref, cosine_ref, sine_ref, gains_ref, weights_ref,
    *refs,
):
    query_grads, attended, branch, router = [refs[n * micro : (n + 1) * micro] for n in range(4)]
    kept_ref, sent_ref, normed_grad_ref, sums_ref, low = refs[-5:]
    _, rows, width = normed_ref.shape
    q_width = query_grads[0].shape[1]
    base = kept_ref.shape[2] - q_width
    first = base - width - 128
    out_grad = sum(product_tn(a[...], b[...]) for a, b in zip(attended, branch))
    by_core(core_ref, out_grad.astype(bf16), kept_ref, sent_ref, first)
    tail = sum(r[...] for r in router)
    tail = jnp.concatenate([tail, jnp.zeros((128 - tail.shape[0], width), f32)], axis=0)
    by_core(core_ref, tail.T.astype(bf16), kept_ref, sent_ref, first + width)
    sums = [jnp.zeros((1, 128), f32) for _ in range(2)]
    for m in range(micro):
        at_rows = pl.ds(m * rows, rows)
        for at in range(0, q_width, 256):
            low1, low2, sum1, sum2 = head_back(
                pre_ref[m, :, at : at + 128], pre_ref[m, :, at + 128 : at + 256],
                query_grads[m][:, at : at + 128], query_grads[m][:, at + 128 : at + 256],
                cosine_ref[...], sine_ref[...], gains_ref[0:1, :], gains_ref[1:2, :], head_size,
            )
            low[at_rows, at : at + 128] = low1
            low[at_rows, at + 128 : at + 256] = low2
            sums = [sums[0] + sum1, sums[1] + sum2]
    sums_ref[...] = jnp.concatenate(sums + [jnp.zeros((6, 128), f32)], axis=0)
    normed = jnp.concatenate([normed_ref[m] for m in range(micro)], axis=0)
    for at in range(0, q_width, 512):
        grad = product_tn(normed, low[:, at : at + 512]).astype(bf16)
        by_core(core_ref, grad, kept_ref, sent_ref, base + at)
    normed_grad_ref[...] = product_nt(low[...], weights_ref[...])


def last_rows(array, rows):
    block = array.shape[0] // rows - 1
    return pl.BlockSpec((rows, array.shape[1]), lambda *_: (block, 0))


def run_query_back(
    core, owners, pre, normed, cosine, sine, gains, dense, query_grads, attended, branch, router,
    head_size, after,
):
    micro, rows, width = normed.shape
    q_width = query_grads[0].shape[1]
    shape = (owners // 2, width // owners, q_width + 128 + width + 128 + q_width)
    out = jax.ShapeDtypeStruct(shape, bf16)
    ins = (pre, normed, cosine, sine, gains)
    rest = (*query_grads, *attended, *branch, *router)
    return pl.pallas_call(
        functools.partial(query_back_kernel, head_size, micro),
        grid=(1,),
        in_specs=[pl.BlockSpec(memory_space=pltpu.SMEM)]
        + [whole(pre.shape), whole(normed.shape), last_rows(cosine, rows), last_rows(sine, rows)]
        + [whole(gains.shape)]
        + [columns(dense, 0, q_width)]
        + [whole(a.shape) for a in rest]
        + [pl.BlockSpec(memory_space=pl.ANY)] * len(after),
        out_specs=[whole(shape), whole(shape), whole((micro * rows, width)), whole((8, 128))],
        out_shape=[
            out,
            out,
            jax.ShapeDtypeStruct((micro * rows, width), f32),
            jax.ShapeDtypeStruct((8, 128), f32),
        ],
        scratch_shapes=[pltpu.VMEM((micro * rows, q_width), bf16)],
        compiler_params=pltpu.CompilerParams(vmem_limit_bytes=VMEM),
        cost_estimate=LIGHT,
        name="query_back",
    )(core, *ins, dense, *rest, *after)


def tokens_back_kernel(
    head_size, micro, core_ref, pre_ref, normed_ref, tokens_ref, cosine_ref, sine_ref, gains_ref,
    weights_ref, turned_ref, normed_grad_ref, sums_ref, *refs,
):
    kept_ref, sent_ref, tokens_grad_ref, low = refs[-4:]
    own_grads, mid_grads = refs[:micro], refs[micro : 2 * micro]
    ones, twos = refs[2 * micro : 3 * micro], refs[3 * micro : 4 * micro]
    _, rows, width = normed_ref.shape
    kv_width = own_grads[0].shape[1] // 2
    q_width = pre_ref.shape[2] - kv_width
    sums = [jnp.zeros((1, 128), f32) for _ in range(2)]
    for m in range(micro):
        at_rows = pl.ds(m * rows, rows)

        def upstream(start, size):
            columns = pl.ds(start, size)
            return (
                own_grads[m][:, columns]
                + ones[m][:, columns].astype(f32)
                + twos[m][:, columns].astype(f32)
            )

        low[at_rows, kv_width:] = upstream(kv_width, kv_width).astype(bf16)
        for at in range(0, kv_width, 256):
            from_pre = q_width + at
            low1, low2, sum1, sum2 = head_back(
                pre_ref[m, :, from_pre : from_pre + 128],
                pre_ref[m, :, from_pre + 128 : from_pre + 256],
                upstream(at, 128), upstream(at + 128, 128),
                cosine_ref[...], sine_ref[...], gains_ref[2:3, :], gains_ref[3:4, :], head_size,
            )
            low[at_rows, at : at + 128] = low1
            low[at_rows, at + 128 : at + 256] = low2
            sums = [sums[0] + sum1, sums[1] + sum2]
    normed = jnp.concatenate([normed_ref[m] for m in range(micro)], axis=0)
    for at in range(0, low.shape[1], 512):
        grad = product_tn(normed, low[:, at : at + 512]).astype(bf16)
        by_core(core_ref, grad, kept_ref, sent_ref, at)
    normed_grad = normed_grad_ref[...] + product_nt(low[...], weights_ref[...])
    gain = turned_ref[33:34, :]
    gain_grad = jnp.zeros((1, width), f32)
    for m in range(micro):
        x = tokens_ref[m].astype(f32)
        scale = rms_scale(x)
        part = normed_grad[m * rows : (m + 1) * rows]
        gain_grad = gain_grad + jnp.sum(part * x * scale, axis=0, keepdims=True)
        tokens_grad_ref[m] = (mid_grads[m][...] + norm_back(part * gain, x, scale)).astype(bf16)
    folded = []
    for total in [sums_ref[0:1, :], sums_ref[1:2, :]] + sums:
        total = total + pltpu.roll(total, 64, 1)
        folded.append(total + pltpu.roll(total, 32, 1))
    lane = lanes_like((1, 128))
    query_row = jnp.where(lane < 96, folded[0], folded[1])
    key_row = jnp.where(lane < 96, folded[2], folded[3])
    column = jnp.concatenate([gain_grad, jnp.zeros((127, width), f32)], axis=0).T
    row = lax.broadcasted_iota(jnp.int32, (width, 128), 0)
    extra = jnp.where(
        lanes_like((width, 128)) < 64, column, jnp.where(row % 2 == 0, query_row, key_row)
    )
    by_core(core_ref, extra.astype(bf16), kept_ref, sent_ref, low.shape[1])


def run_tokens_back(
    core, pre, normed, tokens, cosine, sine, gains, dense, turned, normed_grad, sums,
    own_grads, mid_grads, ones, twos, kept, sent, head_size, after,
):
    micro, rows, width = tokens.shape
    wide = own_grads[0].shape[1]
    shape = kept.shape[:2] + (wide + 128,)
    ins = (pre, normed, tokens, cosine, sine, gains)
    rest = (turned, normed_grad, sums, *own_grads, *mid_grads, *ones, *twos)
    return pl.pallas_call(
        functools.partial(tokens_back_kernel, head_size, micro),
        grid=(1,),
        in_specs=[pl.BlockSpec(memory_space=pltpu.SMEM)]
        + [whole(pre.shape), whole(normed.shape), whole(tokens.shape)]
        + [last_rows(cosine, rows), last_rows(sine, rows), whole(gains.shape)]
        + [columns(dense, wide, wide)]
        + [whole(a.shape) for a in rest]
        + [pl.BlockSpec(memory_space=pl.ANY)] * (2 + len(after)),
        out_specs=[whole(shape), whole(shape), whole(tokens.shape)],
        out_shape=[
            jax.ShapeDtypeStruct(kept.shape, bf16),
            jax.ShapeDtypeStruct(kept.shape, bf16),
            jax.ShapeDtypeStruct(tokens.shape, bf16),
        ],
        input_output_aliases={2 + len(ins) + len(rest): 0, 3 + len(ins) + len(rest): 1},
        scratch_shapes=[pltpu.VMEM((micro * rows, wide), bf16)],
        compiler_params=pltpu.CompilerParams(vmem_limit_bytes=VMEM),
        cost_estimate=LIGHT,
        name="tokens_back",
    )(core, *ins, dense, *rest, kept, sent, *after)


def body(
    tokens,
    cotangent,
    routes,
    doc_lengths,
    valid,
    attn_gain,
    w_query,
    w_key,
    w_value,
    query_gain,
    key_gain,
    w_out,
    ffn_gain,
    w_router,
    w_gate,
    w_up,
    w_down,
):
    micro = tokens.shape[0]
    rows = tokens.shape[2]
    width = tokens.shape[3]
    head_size = query_gain.shape[0]
    q_width = w_query.shape[1]
    kv_width = w_key.shape[1]
    kv_heads = kv_width // head_size
    q_heads = q_width // head_size
    group_size = q_heads // kv_heads
    experts = w_router.shape[1]
    local = w_gate.shape[0]
    hidden_width = w_gate.shape[2]
    upper = w_gate.shape[1]
    expert_devices = lax.axis_size("expert")
    dp_devices = lax.axis_size("dp")
    own_rows = w_query.shape[0]
    reach_back = (WINDOW + rows - 2) // rows
    key_rows = rows * (reach_back + 1)
    score_scale = 1.0 / math.sqrt(head_size)
    q_gain = query_gain.astype(f32)
    k_gain = key_gain.astype(f32)
    all_rows = micro * rows
    qkv_width = q_width + 2 * kv_width

    tiles = 128 // (head_size // 2)
    halves = dp_devices // 2
    core = lax.axis_index("dp") % 2
    core_flag = core[None].astype(jnp.int32)
    expert_index = lax.axis_index("expert")
    across, depth = expert_index % 2, expert_index // 2
    across_flag, depth_flag = across[None].astype(jnp.int32), depth[None].astype(jnp.int32)
    other_core = [(i, i ^ 1) for i in range(dp_devices)]
    other_across = [(i, i ^ 1) for i in range(expert_devices)]
    along_depth = [[2 * z + x for z in range(expert_devices // 2)] for x in range(2)]

    groups = kv_heads // 4
    half_size = head_size // 2
    query_cols = w_query.reshape(own_rows, groups, 4, group_size, 2, half_size)
    query_cols = query_cols.transpose(0, 3, 1, 4, 2, 5).reshape(own_rows, q_width)
    key_cols = w_key.reshape(own_rows, groups, 4, 2, half_size)
    key_cols = key_cols.transpose(0, 1, 3, 2, 4).reshape(own_rows, kv_width)
    tail = jnp.concatenate(
        [
            w_router,
            ffn_gain[:, None],
            attn_gain[:, None],
            jnp.zeros((own_rows, 128 - experts - 2), bf16),
        ],
        axis=1,
    )
    route_cols = routes[:, 0].astype(bf16).reshape(own_rows, -1)
    packed = jnp.concatenate([query_cols, key_cols, w_value, w_out, tail, route_cols], axis=1)
    packed = spread(packed, "expert")
    dense_width = packed.shape[2] - route_cols.shape[1]
    routes_all = packed[:, :, dense_width:].astype(jnp.int32)
    routes_all = routes_all.reshape((expert_devices,) + routes.shape[:1] + routes.shape[2:])
    seed_low = cotangent[:, 0] * valid[:, 0][:, :, None].astype(bf16)
    seed_other = lax.ppermute(seed_low, "expert", other_across)
    x_low = tokens[:, 0]
    one = passed_along(x_low, "expert", 1)
    two = passed_along(x_low, "expert", 2)
    weights = jnp.concatenate([jnp.concatenate([w_gate, w_up], axis=2), w_down], axis=1)
    weights = lax.all_gather(weights, "dp", axis=1)
    dense = run_pack(packed, dense_width, (seed_other,))
    dense = lax.all_gather(dense, "dp", axis=0, tiled=True)

    def by_depth(values, other, after=()):
        pair = run_pair(across_flag, values, other, expert_devices // 2, after)
        return lax.all_to_all(pair, "expert", 0, 0, axis_index_groups=along_depth)

    seed_all = by_depth(seed_low, seed_other, (one, two))
    expert_ids = jnp.arange(experts, dtype=jnp.int32)
    member_all = jnp.any(routes_all[..., None] == expert_ids, axis=3)
    member_turned = jnp.roll(member_all, -expert_index * local, axis=3).transpose(1, 0, 3, 2)
    member = member_turned[:, :, :local]
    earlier = (
        jnp.arange(rows, dtype=jnp.int32)[:, None] < jnp.arange(rows, dtype=jnp.int32)[None, :]
    ).astype(bf16)
    rank = einsum("mbjt,tu->mbju", member.astype(bf16), earlier).astype(jnp.int32)
    slots = jnp.where(member, rank, -1)
    turned_slots = slots.transpose(0, 1, 3, 2)
    member_turned = member_turned.astype(f32)
    own_member = jnp.any(routes[:, 0, :, :, None] == expert_ids, axis=2)
    own_member = own_member.transpose(0, 2, 1).astype(f32)

    q_pos = expert_index * rows + jnp.arange(rows, dtype=jnp.int32)
    k_pos = (expert_index - reach_back) * rows + jnp.arange(key_rows, dtype=jnp.int32)
    cosine, sine = rope_tables(k_pos, head_size)
    cosine = jnp.tile(cosine[:, :half_size], (1, tiles))
    sine = jnp.tile(sine[:, :half_size], (1, tiles))
    bounds = jnp.cumsum(doc_lengths[:, 0], axis=1)
    q_doc = jnp.sum((q_pos[None, :, None] >= bounds[:, None, :]).astype(jnp.int32), axis=2)
    k_doc = jnp.sum((k_pos[None, :, None] >= bounds[:, None, :]).astype(jnp.int32), axis=2)
    offset = q_pos[None, :] - k_pos[:, None]
    visible = (
        (k_pos[None, :, None] >= 0)
        & (q_doc[:, None, :] == k_doc[:, :, None])
        & (offset >= 0)[None]
        & (offset < WINDOW)[None]
    )
    bias = jnp.where(visible, 0.0, -1e30).astype(f32)
    head_gains = jnp.stack(
        [
            jnp.tile(part, tiles)
            for part in (
                q_gain[:half_size],
                q_gain[half_size:],
                k_gain[:half_size],
                k_gain[half_size:],
            )
        ]
        + [jnp.zeros((128,), f32)] * 4
    )

    result = run_front(
        x_low, one, two, dense, cosine, sine, head_gains, bias, head_size, q_width, ()
    )
    normed, pre, query, key_value, turned = result[:5]
    attended, middle, moe_in, peak = [result[5 + n :: 4] for n in range(4)]

    router_turned = jnp.roll(turned[:experts], -expert_index * local, axis=0).astype(bf16)
    saved, backs, mixed = [], [], []
    moe_all = [
        by_depth(
            moe_in[m],
            lax.ppermute(moe_in[m], "expert", other_across),
            (slots, turned_slots, member_turned, own_member, router_turned) if m == 0 else (),
        ).reshape(expert_devices, rows, width)
        for m in range(micro)
    ]
    for m in range(micro):
        back_part, arrived, out_rows, hidden, pre_low, mixed_rows = run_experts(
            m, moe_all[m], seed_all, slots, turned_slots, member_turned, router_turned, weights,
            tuple(mixed),
        )
        saved.append((arrived, out_rows, hidden, pre_low))
        backs.append(lax.all_to_all(back_part, "expert", 0, 0))
        mixed.append(mixed_rows)
    sent = weight_grads(core_flag, dp_devices, saved, (), ())
    received = [lax.ppermute(piece, "dp", other_core) for piece in sent]
    combined = run_combine(depth_flag, mixed, turned_slots, (sent[0], backs[0]))
    core_sum = weight_grads(core_flag, dp_devices, saved, received, (combined[0],))

    made, ones, twos = [], [], []
    for m in range(micro):
        result = run_middle_back(
            m, backs[m], own_member, seed_low, query, key_value, bias, moe_in[m], middle[m],
            peak[m], dense, turned, score_scale, (core_sum,),
        )
        if m == 0:
            core_sum = pass_on(core_sum, (*backs, result[0]))
        made.append(result[:5])
        ones.append(passed_along(result[5], "expert", -1))
        twos.append(passed_along(result[6], "expert", -2))
    mid_grads, branches, router_grads, query_grads, own_grads = zip(*made)
    across_low = lax.axis_index("dp") // 2 % 2
    place_flag = across_low[None].astype(jnp.int32)
    along_y = [[4 * y + place for y in range(dp_devices // 4)] for place in range(4)]
    over_y = lax.psum_scatter(
        core_sum.reshape((dp_devices // 4, 2, 2) + core_sum.shape[1:]),
        "dp",
        scatter_dimension=0,
        axis_index_groups=along_y,
    )
    over_y = over_y.reshape(over_y.shape[-5:])
    pieces = run_choose(place_flag, core_flag, over_y)
    exchanged = [
        lax.ppermute(piece, "dp", [(i, i ^ step) for i in range(dp_devices)])
        for piece, step in zip(pieces, (2, 1, 3))
    ]
    gate_owned, up_owned, down_owned = run_expert_owned(
        place_flag, core_flag, over_y, exchanged, upper, hidden_width
    )

    up = [(i, (i + 2) % expert_devices) for i in range(expert_devices)]
    down = [(i, (i - 2) % expert_devices) for i in range(expert_devices)]
    out_low = lax.ppermute(combined[2], "expert", up)
    out_high = lax.ppermute(combined[3], "expert", up)

    kept_in, sent_in, normed_grad, gain_sums = run_query_back(
        core_flag, dp_devices, pre, normed, cosine, sine, head_gains, dense, query_grads, attended,
        branches, router_grads, head_size, (out_low, ones[0], twos[0]),
    )
    kept_in, sent_in, token_grad = run_tokens_back(
        core_flag, pre, normed, x_low, cosine, sine, head_gains, dense, turned, normed_grad,
        gain_sums, own_grads, mid_grads, ones, twos, kept_in, sent_in, head_size,
        (out_high,),
    )
    both = add_low(kept_in, lax.ppermute(sent_in, "dp", other_core), 4)
    parts = both.reshape(dp_devices // 4, 2 * both.shape[1], both.shape[2])
    parts = lax.all_to_all(parts, "dp", 0, 0, axis_index_groups=along_y)

    next_part = run_merge((combined[1], out_low, out_high), (both,))
    out_parts = [
        combined[0],
        lax.ppermute(next_part, "expert", up),
        lax.ppermute(combined[4], "expert", down),
    ]
    total = run_total(parts, (gate_owned,))
    out_kept, out_sent = run_fold(across_flag, middle, out_parts, (total,))
    out_other = lax.ppermute(out_sent, "expert", other_across)

    output = add_low(out_kept, out_other, micro, (total,))
    parts = total.reshape(2 * expert_devices, own_rows, -1)
    same_y = [
        [
            ((2 * y + place) * 2 + c) * expert_devices + e
            for place in range(2)
            for e in range(expert_devices)
        ]
        for y in range(dp_devices // 4)
        for c in range(2)
    ]
    parts = lax.all_to_all(parts, ("dp", "expert"), 0, 0, axis_index_groups=same_y)
    (
        key_owned, value_owned, attn_gain_owned, query_gain_owned, key_gain_owned,
        out_owned, router_owned, ffn_gain_owned, query_owned,
    ) = run_owned(parts, width, q_width, head_size, experts, (exchanged[0],))
    return (
        output.reshape(micro, 1, rows, width),
        token_grad.reshape(micro, 1, rows, width),
        attn_gain_owned.reshape(own_rows),
        query_owned,
        key_owned,
        value_owned,
        query_gain_owned.reshape(head_size),
        key_gain_owned.reshape(head_size),
        out_owned,
        ffn_gain_owned.reshape(own_rows),
        router_owned,
        gate_owned,
        up_owned,
        down_owned,
    )


def solution(mesh):
    rows_spec = P(("dp", "expert"), None)
    gain_spec = P(("dp", "expert"))
    token_spec = P(None, "dp", "expert", None)
    expert_spec = P("expert", "dp", None)
    return jax.shard_map(
        body,
        mesh=mesh,
        in_specs=(
            token_spec,
            token_spec,
            token_spec,
            P(None, "dp", None),
            P(None, "dp", "expert"),
            gain_spec,
            rows_spec,
            rows_spec,
            rows_spec,
            P(),
            P(),
            rows_spec,
            gain_spec,
            rows_spec,
            expert_spec,
            expert_spec,
            expert_spec,
        ),
        out_specs=(
            token_spec,
            token_spec,
            gain_spec,
            rows_spec,
            rows_spec,
            rows_spec,
            P(),
            P(),
            rows_spec,
            gain_spec,
            rows_spec,
            expert_spec,
            expert_spec,
            expert_spec,
        ),
        check_vma=False,
    )
```

```python
import functools
import math

import jax
import jax.numpy as jnp
from jax import lax
from jax.experimental import pallas as pl
from jax.experimental.pallas import tpu as pltpu
from jax.sharding import PartitionSpec as P

WINDOW = 256
EPSILON = 1e-06
ROPE_BASE = 10000.0
CAP = 48
EXTRA = 16
VMEM = 60 << 20
PIECES = 2
LIGHT = pl.CostEstimate(flops=1, bytes_accessed=1, transcendentals=0)

bf16 = jnp.bfloat16
f32 = jnp.float32


def rms_scale(values):
    return lax.rsqrt(jnp.mean(values * values, axis=-1, keepdims=True) + EPSILON)


def rope_tables(positions, head_size):
    half_size = head_size // 2
    frequency = jnp.exp(
        -math.log(ROPE_BASE) * (2.0 * jnp.arange(half_size, dtype=f32) / head_size)
    )
    angles = positions.astype(f32)[:, None] * frequency[None, :]
    angles = jnp.concatenate([angles, angles], axis=-1)
    return (jnp.cos(angles), jnp.sin(angles))


def norm_back(upstream, values, scaling):
    return scaling * upstream - values * (scaling * scaling * scaling) * jnp.mean(
        upstream * values, axis=-1, keepdims=True
    )


def product(left_side, right_side):
    return jnp.dot(left_side, right_side, preferred_element_type=f32)


def product_tn(left_side, right_side):
    return lax.dot_general(
        left_side, right_side, (((0,), (0,)), ((), ())), preferred_element_type=f32
    )


def product_nt(left_side, right_side):
    return lax.dot_general(
        left_side, right_side, (((1,), (1,)), ((), ())), preferred_element_type=f32
    )


def einsum(spec, left_side, right_side):
    return jnp.einsum(spec, left_side, right_side, preferred_element_type=f32)


def spread(values, axis):
    count = lax.axis_size(axis)
    return lax.all_to_all(jnp.broadcast_to(values[None], (count,) + values.shape), axis, 0, 0)


def passed_along(value, axis, steps):
    count = lax.axis_size(axis)
    initial, last = (max(0, -steps), min(count, count - steps))
    return lax.ppermute(value, axis, [(source, source + steps) for source in range(initial, last)])


def whole(shape):
    return pl.BlockSpec(shape, lambda *_: (0,) * len(shape))


def once(shape):
    return pl.BlockSpec(shape, lambda *_: (0,) * len(shape), pipeline_mode=pl.Buffered(1))


def put_back(turned, pieces):
    column = lax.broadcasted_iota(jnp.int32, (turned.shape[0], CAP), 1)
    hot = [(turned[:, j : j + 1] == column).astype(f32) for j in range(len(pieces))]
    hot = jnp.concatenate(hot, axis=1).astype(bf16)
    return product(hot, jnp.concatenate(pieces, axis=0)).astype(bf16)


def experts_kernel(
    moe_ref,
    seed_ref,
    slots_ref,
    turned_ref,
    member_ref,
    router_ref,
    weights_ref,
    *refs,
):
    back_ref, arrived_ref, out_rows_ref, hidden_ref, pre_ref, mixed_ref = refs[-11:-5]
    taken, seeds, backs, row_gates, row_grads = refs[-5:]
    step = pl.program_id(0)
    blocks, rows, width = moe_ref.shape
    local = taken.shape[0]
    hidden_width = hidden_ref.shape[2]

    def picks(b, j):
        index = lax.broadcasted_iota(jnp.int32, (CAP, rows), 0)
        return slots_ref[b, j : j + 1, :] == index

    @pl.when(step == 0)
    def dispatch():
        for b in range(blocks):
            tokens = moe_ref[b]
            logits = product_nt(router_ref[...], tokens)
            member = member_ref[b] > 0.5
            shown = jnp.where(member, logits, -1e30)
            exps = jnp.where(member, jnp.exp(shown - jnp.max(shown, axis=0, keepdims=True)), 0.0)
            gates = exps / jnp.sum(exps, axis=0, keepdims=True)
            masks = [picks(b, j) for j in range(local)]
            pick = jnp.concatenate([m.astype(f32) for m in masks], axis=0).astype(bf16)
            arrived = product(pick, tokens).astype(bf16)
            seeded = product(pick, seed_ref[b // 2, b % 2, 0]).astype(bf16)
            for j in range(local):
                at = pl.ds(b * CAP, CAP)
                taken[j, at, :] = arrived[j * CAP : (j + 1) * CAP]
                seeds[j, at, :] = seeded[j * CAP : (j + 1) * CAP]
                row_gates[j, at, :] = jnp.sum(
                    jnp.where(masks[j], gates[j : j + 1, :], 0.0), axis=1, keepdims=True
                )

    def expert():
        upper = width // weights_ref.shape[1]
        gate_up_weights = weights_ref[0, :, :upper, :].reshape(width, 2 * hidden_width)
        down_weights = weights_ref[0, :, upper:, :].reshape(hidden_width, width)
        arrived_ref[0] = taken[step]
        pre = product(taken[step], gate_up_weights)
        gate_pre = pre[:, :hidden_width]
        up_pre = pre[:, hidden_width:]
        sigma = 1.0 / (1.0 + jnp.exp(-gate_pre))
        gate_act = gate_pre * sigma
        hidden = (gate_act * up_pre).astype(bf16)
        hidden_ref[0] = hidden
        expert_out = product(hidden, down_weights).astype(bf16).astype(f32)
        seed_rows = seeds[step].astype(f32)
        gate_column = row_gates[step]
        row_grads[step] = jnp.sum(expert_out * seed_rows, axis=1, keepdims=True)
        mixed_ref[0] = (gate_column * expert_out).astype(bf16)
        out_rows = (gate_column * seed_rows).astype(bf16)
        out_rows_ref[0] = out_rows
        hidden_grad = product_nt(out_rows, down_weights)
        gate_low = (hidden_grad * up_pre * sigma * (1.0 + gate_pre * (1.0 - sigma))).astype(bf16)
        up_low = (hidden_grad * gate_act).astype(bf16)
        pre_ref[0, :, :hidden_width] = gate_low
        pre_ref[0, :, hidden_width:] = up_low
        backs[step] = product_nt(pre_ref[0], gate_up_weights).astype(bf16)

    expert()

    @pl.when(step == local - 1)
    def combine():
        for b in range(blocks):
            at = pl.ds(b * CAP, CAP)
            back_ref[b, :rows, :] = put_back(
                turned_ref[b], [backs[j, at, :] for j in range(local)]
            )
            gate_grads = [
                jnp.sum(jnp.where(picks(b, j), row_grads[j, at, :], 0.0), axis=0, keepdims=True)
                for j in range(local)
            ]
            gate_grads = jnp.concatenate(
                gate_grads + [jnp.zeros((1, width - local * rows), f32)], axis=1
            )
            high = gate_grads.astype(bf16).astype(f32)
            row = lax.broadcasted_iota(jnp.int32, (EXTRA, width), 0)
            back_ref[b, rows:, :] = jnp.where(
                row == 0, high, jnp.where(row == 1, gate_grads - high, 0.0)
            ).astype(bf16)


def run_experts(m, tokens, seeds, slots, turned, member, router, weights, after):
    blocks, rows, width = tokens.shape
    local, owners, each, wide = weights.shape
    hidden_width = wide // 2
    held = blocks * CAP
    shapes = [
        ((blocks, rows + EXTRA, width), bf16),
        ((local, held, width), bf16),
        ((local, held, width), bf16),
        ((local, held, hidden_width), bf16),
        ((local, held, wide), bf16),
        ((local, held, width), bf16),
    ]
    return pl.pallas_call(
        experts_kernel,
        grid=(local,),
        in_specs=[
            once(tokens.shape),
            pl.BlockSpec(
                seeds.shape[:2] + (1,) + seeds.shape[3:],
                lambda j: (0, 0, m, 0, 0),
                pipeline_mode=pl.Buffered(1),
            ),
            picked(slots, m),
            picked(turned, m),
            picked(member, m),
            once(router.shape),
            pl.BlockSpec((1, owners, each, wide), lambda j: (j, 0, 0, 0)),
        ]
        + [pl.BlockSpec(memory_space=pl.ANY)] * len(after),
        out_specs=[once(shapes[0][0])]
        + [pl.BlockSpec((1,) + shape[1:], lambda j: (j, 0, 0)) for shape, _ in shapes[1:]],
        out_shape=[jax.ShapeDtypeStruct(shape, kind) for shape, kind in shapes],
        scratch_shapes=[
            pltpu.VMEM((local, held, width), bf16),
            pltpu.VMEM((local, held, width), bf16),
            pltpu.VMEM((local, held, width), bf16),
            pltpu.VMEM((local, held, 1), f32),
            pltpu.VMEM((local, held, 1), f32),
        ],
        compiler_params=pltpu.CompilerParams(vmem_limit_bytes=VMEM),
        cost_estimate=LIGHT,
        name="experts",
    )(tokens, seeds, slots, turned, member, router, weights, *after)


def weight_grads_kernel(micro, adding, core_ref, *refs):
    del core_ref
    parts = [refs[4 * m : 4 * m + 4] for m in range(micro)]
    gate_up = sum(product_tn(p[0][0], p[3][0]) for p in parts)
    down = sum(product_tn(p[2][0], p[1][0]) for p in parts)
    outs = refs[-1:] if adding else refs[-PIECES:]
    owners = sum(ref.shape[0] for ref in outs)
    upper = gate_up.shape[0] // owners
    gate_up = gate_up.reshape(owners, upper, gate_up.shape[1])
    down = down.reshape(owners, down.shape[0] // owners, down.shape[1])
    each = owners // PIECES
    for n in range(PIECES):
        part = slice(n * each, (n + 1) * each)
        above, below = gate_up[part], down[part]
        if adding:
            received_ref = refs[4 * micro + n]
            above = above + received_ref[:, 0, :upper, :].astype(f32)
            below = below + received_ref[:, 0, upper:, :].astype(f32)
            outs[0][part, 0, :upper, :] = above.astype(bf16)
            outs[0][part, 0, upper:, :] = below.astype(bf16)
        else:
            outs[n][:, 0, :upper, :] = above.astype(bf16)
            outs[n][:, 0, upper:, :] = below.astype(bf16)


def combine_kernel(micro, depth_ref, *refs):
    mixed, turned = refs[:micro], refs[micro]
    own_ref, next_ref, low_ref, high_ref, last_ref = refs[-5:]
    local = mixed[0].shape[0]
    for ahead in range(4):
        target = lax.rem(depth_ref[0] + ahead, 4)
        for x in range(2):
            b = 2 * target + x
            at = pl.ds(pl.multiple_of(b * CAP, CAP), CAP)
            for m in range(micro):
                made = put_back(turned[m, b], [mixed[m][j, at, :] for j in range(local)])
                if ahead == 2:
                    (low_ref, high_ref)[x][m] = made
                else:
                    (own_ref, next_ref, None, last_ref)[ahead][x, m] = made


def run_combine(depth, mixed, turned, after):
    micro, _, rows, _ = turned.shape
    width = mixed[0].shape[2]
    pair, half = (2, micro, rows, width), (micro, rows, width)
    shapes = [pair, pair, half, half, pair]
    return pl.pallas_call(
        functools.partial(combine_kernel, micro),
        grid=(1,),
        in_specs=[pl.BlockSpec(memory_space=pltpu.SMEM)]
        + [whole(a.shape) for a in (*mixed, turned)]
        + [pl.BlockSpec(memory_space=pl.ANY)] * len(after),
        out_specs=[whole(shape) for shape in shapes],
        out_shape=[jax.ShapeDtypeStruct(shape, bf16) for shape in shapes],
        compiler_params=pltpu.CompilerParams(vmem_limit_bytes=VMEM),
        cost_estimate=LIGHT,
        name="combine",
    )(depth, *mixed, turned, *after)


def merge_kernel(next_ref, low_ref, high_ref, *refs):
    refs[-1][0] = (next_ref[0].astype(f32) + low_ref[...].astype(f32)).astype(bf16)
    refs[-1][1] = (next_ref[1].astype(f32) + high_ref[...].astype(f32)).astype(bf16)


def run_merge(parts, after):
    shape = parts[0].shape
    return pl.pallas_call(
        merge_kernel,
        grid=(1,),
        in_specs=[whole(a.shape) for a in parts]
        + [pl.BlockSpec(memory_space=pl.ANY)] * len(after),
        out_specs=whole(shape),
        out_shape=jax.ShapeDtypeStruct(shape, bf16),
        compiler_params=pltpu.CompilerParams(vmem_limit_bytes=16 << 20),
        cost_estimate=LIGHT,
        name="merge",
    )(*parts, *after)


def fold_kernel(micro, across_ref, *refs):
    kept_ref, sent_ref = refs[-2:]
    middles, parts = refs[:micro], refs[micro : micro + 3]

    def place(kept, sent):
        for m in range(micro):
            total = middles[m][...]
            for part in parts:
                total = total + part[kept, m].astype(f32)
            kept_ref[m] = total
            total = parts[0][sent, m].astype(f32)
            for part in parts[1:]:
                total = total + part[sent, m].astype(f32)
            sent_ref[m] = total.astype(bf16)

    @pl.when(across_ref[0] == 0)
    def low_x():
        place(0, 1)

    @pl.when(across_ref[0] == 1)
    def high_x():
        place(1, 0)


def run_fold(across, middles, parts, after):
    micro = len(middles)
    shape = (micro,) + middles[0].shape
    return pl.pallas_call(
        functools.partial(fold_kernel, micro),
        grid=(1,),
        in_specs=[pl.BlockSpec(memory_space=pltpu.SMEM)]
        + [whole(a.shape) for a in (*middles, *parts)]
        + [pl.BlockSpec(memory_space=pl.ANY)] * len(after),
        out_specs=[whole(shape)] * 2,
        out_shape=[jax.ShapeDtypeStruct(shape, f32), jax.ShapeDtypeStruct(shape, bf16)],
        compiler_params=pltpu.CompilerParams(vmem_limit_bytes=16 << 20),
        cost_estimate=LIGHT,
        name="fold",
    )(across, *middles, *parts, *after)


def weight_grads(core, owners, saved, received, after):
    local, held, width = saved[0][0].shape
    hidden_width = saved[0][2].shape[2]
    depth = (width + hidden_width) // owners
    micro, count = len(saved), local // 2
    own = bool(received)

    def expert(j, core_ref):
        side = core_ref[0] if own else 1 - core_ref[0]
        return (side * count + j, 0, 0)

    piece = (owners // PIECES, count, depth, width)
    each = (owners // PIECES, 1, depth, width)
    pieces = [pl.BlockSpec(each, lambda j, core_ref: (0, j, 0, 0))] * PIECES
    flat = [a for group in saved for a in group]
    return pl.pallas_call(
        functools.partial(weight_grads_kernel, micro, own),
        grid_spec=pltpu.PrefetchScalarGridSpec(
            num_scalar_prefetch=1,
            grid=(count,),
            in_specs=[pl.BlockSpec((1,) + a.shape[1:], expert) for a in flat]
            + pieces[: len(received)]
            + [pl.BlockSpec(memory_space=pl.ANY)] * len(after),
            out_specs=pl.BlockSpec((owners, 1, depth, width), lambda j, core_ref: (0, j, 0, 0))
            if own
            else pieces,
        ),
        out_shape=jax.ShapeDtypeStruct((owners, count, depth, width), bf16)
        if own
        else [jax.ShapeDtypeStruct(piece, bf16)] * PIECES,
        compiler_params=pltpu.CompilerParams(vmem_limit_bytes=VMEM),
        cost_estimate=LIGHT,
        name="weight_grads",
    )(core, *flat, *received, *after)


def pass_kernel(*refs):
    del refs


def pass_on(value, after):
    return pl.pallas_call(
        pass_kernel,
        in_specs=[pl.BlockSpec(memory_space=pl.ANY)] * (1 + len(after)),
        out_specs=pl.BlockSpec(memory_space=pl.ANY),
        out_shape=jax.ShapeDtypeStruct(value.shape, value.dtype),
        input_output_aliases={0: 0},
        compiler_params=pltpu.CompilerParams(vmem_limit_bytes=VMEM),
        cost_estimate=LIGHT,
        name="pass_on",
    )(value, *after)


def choose_kernel(place_ref, core_ref, parts_ref, *refs):
    place, core = place_ref[0], core_ref[0]
    refs[0][...] = parts_ref[1 - place, core]
    refs[1][...] = parts_ref[place, 1 - core]
    refs[2][...] = parts_ref[1 - place, 1 - core]


def run_choose(place, core, parts):
    shape = parts.shape[2:]
    return pl.pallas_call(
        choose_kernel,
        grid=(1,),
        in_specs=[pl.BlockSpec(memory_space=pltpu.SMEM)] * 2 + [whole(parts.shape)],
        out_specs=[whole(shape)] * 3,
        out_shape=[jax.ShapeDtypeStruct(shape, bf16)] * 3,
        compiler_params=pltpu.CompilerParams(vmem_limit_bytes=12 << 20),
        cost_estimate=LIGHT,
        name="choose",
    )(place, core, parts)


def expert_owned_kernel(place_ref, core_ref, parts_ref, across_ref, other_ref, both_ref, *refs):
    gate_ref, up_ref, down_ref = refs
    upper, half = gate_ref.shape[1], gate_ref.shape[2]
    place, core = place_ref[0], core_ref[0]
    count = across_ref.shape[0]

    def put(at, total):
        gate_ref[at] = total[:upper, :half]
        up_ref[at] = total[:upper, half:]
        down_ref[at] = total[upper:]

    for n in range(count):
        own = parts_ref[place, core, n].astype(f32) + across_ref[n].astype(f32)
        put(core * count + n, own)
        put((1 - core) * count + n, other_ref[n].astype(f32) + both_ref[n].astype(f32))


def run_expert_owned(place, core, parts, received, upper, half):
    count, depth, width = received[0].shape
    count = 2 * count
    shapes = [(count, upper, half), (count, upper, half), (count, depth - upper, width)]
    return pl.pallas_call(
        expert_owned_kernel,
        grid=(1,),
        in_specs=[pl.BlockSpec(memory_space=pltpu.SMEM)] * 2
        + [whole(a.shape) for a in (parts, *received)],
        out_specs=[whole(shape) for shape in shapes],
        out_shape=[jax.ShapeDtypeStruct(shape, f32) for shape in shapes],
        compiler_params=pltpu.CompilerParams(vmem_limit_bytes=12 << 20),
        cost_estimate=LIGHT,
        name="expert_owned",
    )(place, core, parts, *received)


def lanes_like(shape):
    return lax.broadcasted_iota(jnp.int32, shape, len(shape) - 1)


def head_sums(values):
    left = lax.broadcasted_iota(jnp.int32, (128, 128), 0) // 32
    right = lax.broadcasted_iota(jnp.int32, (128, 128), 1) // 32
    ones = (left == right).astype(f32).astype(bf16)
    high = values.astype(bf16)
    rest = (values - high.astype(f32)).astype(bf16)
    return product(high, ones) + product(rest, ones)


def columns(dense, start, size):
    return pl.BlockSpec((dense.shape[0], size), lambda *_: (0, start // size))


def pair_kernel(across_ref, own_ref, other_ref, *refs):
    out_ref = refs[-1]

    @pl.when(across_ref[0] == 0)
    def low_x():
        out_ref[0, 0] = own_ref[...]
        out_ref[0, 1] = other_ref[...]

    @pl.when(across_ref[0] == 1)
    def high_x():
        out_ref[0, 0] = other_ref[...]
        out_ref[0, 1] = own_ref[...]


def run_pair(across, own, other, count, after):
    shape = (count, 2) + own.shape
    zeros = (0,) * own.ndim
    return pl.pallas_call(
        pair_kernel,
        grid=(count,),
        in_specs=[pl.BlockSpec(memory_space=pltpu.SMEM), whole(own.shape), whole(other.shape)]
        + [pl.BlockSpec(memory_space=pl.ANY)] * len(after),
        out_specs=pl.BlockSpec((1, 2) + own.shape, lambda i: (i, 0) + zeros),
        out_shape=jax.ShapeDtypeStruct(shape, own.dtype),
        compiler_params=pltpu.CompilerParams(vmem_limit_bytes=16 << 20),
        cost_estimate=LIGHT,
        name="pair",
    )(across, own, other, *after)


def pack_kernel(packed_ref, *refs):
    width = refs[-1].shape[1]
    for n in range(packed_ref.shape[0]):
        rows = packed_ref.shape[1]
        refs[-1][n * rows : (n + 1) * rows, :] = packed_ref[n, :, :width]


def run_pack(packed, width, after):
    count, rows, _ = packed.shape
    return pl.pallas_call(
        pack_kernel,
        grid=(1,),
        in_specs=[whole(packed.shape)] + [pl.BlockSpec(memory_space=pl.ANY)] * len(after),
        out_specs=whole((count * rows, width)),
        out_shape=jax.ShapeDtypeStruct((count * rows, width), packed.dtype),
        compiler_params=pltpu.CompilerParams(vmem_limit_bytes=8 << 20),
        cost_estimate=LIGHT,
        name="pack",
    )(packed, *after)


def group_stack(query_ref, g, q_half):
    lane = lanes_like((1, 256)) % 128 // 32
    pieces = []
    for i in range(4):
        for r in range(2):
            at = r * q_half + g * 256
            block = query_ref[:, at : at + 256]
            pieces.append(jnp.where(lane == i, block, jnp.zeros_like(block)))
    return jnp.concatenate(pieces, axis=0)


def doubled_values(values, h):
    block = values[:, h // 2 * 128 : h // 2 * 128 + 128]
    swapped = pltpu.roll(block, 64, 1)
    low_half = lanes_like(block.shape) < 64
    return jnp.where(low_half == (h % 2 == 0), block, swapped).astype(bf16)


def group_scores(keys, stack, bias, score_scale):
    scores = product_nt(keys, stack) * score_scale
    return scores + jnp.concatenate([bias] * 8, axis=1)


def rotated(u1, u2, cosine, sine, gain1, gain2, head_size):
    scale = lax.rsqrt(head_sums(u1 * u1 + u2 * u2) / head_size + EPSILON)
    u1 = u1 * scale * gain1
    u2 = u2 * scale * gain2
    return (
        (u1 * cosine - u2 * sine).astype(bf16),
        (u2 * cosine + u1 * sine).astype(bf16),
    )


def front_kernel(
    head_size,
    own_ref,
    one_ref,
    two_ref,
    weights_ref,
    out_weights_ref,
    tail_ref,
    cosine_ref,
    sine_ref,
    gains_ref,
    bias_ref,
    *refs,
):
    micro, rows, width = own_ref.shape
    first, rest = refs[-4 * micro - 5 : -4 * micro], refs[-4 * micro :]
    normed_ref, pre_ref, query_ref, key_value_ref, turned_ref = first
    q_width = query_ref.shape[2]
    kv_width = q_width // 2
    groups = kv_width // 256
    score_scale = 1.0 / math.sqrt(head_size)
    turned = tail_ref[...].astype(f32).T
    turned_ref[...] = turned
    gain = turned[33:34, :]
    low_half = lanes_like((rows, 128)) < 64
    head_gains = [gains_ref[n : n + 1, :] for n in range(4)]

    def norm(x):
        return (x * rms_scale(x) * gain).astype(bf16)

    for m in range(micro):
        attended_ref, middle_ref, moe_ref, peak_ref = rest[4 * m : 4 * m + 4]
        x = own_ref[m].astype(f32)
        normed = norm(x)
        normed_ref[m] = normed
        own = product(normed, weights_ref[...])
        pre_ref[m] = own[:, : q_width + kv_width]
        own_rows = pl.ds(2 * rows, rows)
        for at in range(0, q_width, 256):
            made = rotated(
                own[:, at : at + 128], own[:, at + 128 : at + 256],
                cosine_ref[own_rows, :], sine_ref[own_rows, :],
                head_gains[0], head_gains[1], head_size,
            )
            query_ref[m, :, at : at + 128] = made[0]
            query_ref[m, :, at + 128 : at + 256] = made[1]
        earlier = jnp.concatenate(
            [norm(two_ref[m].astype(f32)), norm(one_ref[m].astype(f32))], axis=0
        )
        earlier = product(earlier, weights_ref[:, q_width:])
        both = jnp.concatenate([earlier, own[:, q_width:]], axis=0)
        key_value_ref[m, :, kv_width:] = both[:, kv_width:].astype(bf16)
        for at in range(0, kv_width, 256):
            made = rotated(
                both[:, at : at + 128], both[:, at + 128 : at + 256],
                cosine_ref[...], sine_ref[...], head_gains[2], head_gains[3], head_size,
            )
            key_value_ref[m, :, at : at + 128] = made[0]
            key_value_ref[m, :, at + 128 : at + 256] = made[1]

        bias = bias_ref[m]
        values = key_value_ref[m, :, kv_width:].astype(f32)
        for g in range(groups):
            keys = key_value_ref[m, :, g * 256 : (g + 1) * 256]
            stack = group_stack(query_ref.at[m], g, q_width // 2)
            scores = group_scores(keys, stack, bias, score_scale)
            peak = jnp.max(scores, axis=0, keepdims=True)
            exps = jnp.exp(scores - peak)
            total = jnp.sum(exps, axis=0, keepdims=True)
            probs = (exps * (1.0 / total)).astype(bf16)
            peak_ref[g : g + 1, :] = peak + jnp.log(total)
            for i in range(4):
                h = 4 * g + i
                mixed = product_tn(probs[:, i * 256 : (i + 1) * 256], doubled_values(values, h))
                attended_ref[:, h * 128 : (h + 1) * 128] = jnp.where(
                    low_half, mixed[:rows], mixed[rows:]
                ).astype(bf16)
        middle = x + product(attended_ref[...], out_weights_ref[...])
        middle_ref[...] = middle
        moe_ref[...] = (middle * rms_scale(middle) * turned[32:33, :]).astype(bf16)


def picked(array, m):
    return pl.BlockSpec(
        (None,) + array.shape[1:], lambda *_: (m,) + (0,) * (len(array.shape) - 1)
    )


def run_front(own, one, two, dense, cosine, sine, gains, bias, head_size, q_width, after):
    micro, rows, width = own.shape
    kv_width = q_width // 2
    shapes = [
        ((micro, rows, width), bf16),
        ((micro, rows, q_width + kv_width), f32),
        ((micro, rows, q_width), bf16),
        ((micro, 3 * rows, 2 * kv_width), bf16),
        ((128, width), f32),
    ] + [
        ((rows, q_width), bf16),
        ((rows, width), f32),
        ((rows, width), bf16),
        ((8, 8 * rows), f32),
    ] * micro
    small = (cosine, sine, gains, bias)
    return pl.pallas_call(
        functools.partial(front_kernel, head_size),
        grid=(1,),
        in_specs=[whole(own.shape)] * 3
        + [
            columns(dense, 0, 2 * q_width),
            columns(dense, 2 * q_width, width),
            columns(dense, 2 * q_width + width, 128),
        ]
        + [whole(a.shape) for a in small]
        + [pl.BlockSpec(memory_space=pl.ANY)] * len(after),
        out_specs=[whole(shape) for shape, _ in shapes],
        out_shape=[jax.ShapeDtypeStruct(shape, kind) for shape, kind in shapes],
        compiler_params=pltpu.CompilerParams(vmem_limit_bytes=VMEM),
        cost_estimate=LIGHT,
        name="front",
    )(own, one, two, dense, dense, dense, *small, *after)


def add_kernel(left_ref, right_ref, *refs):
    total = left_ref[...].astype(f32) + right_ref[...].astype(f32)
    refs[-1][...] = total.astype(bf16)


def total_kernel(parts_ref, *refs):
    total = parts_ref[0].astype(f32)
    for n in range(1, parts_ref.shape[0]):
        total = total + parts_ref[n].astype(f32)
    refs[-1][...] = total.astype(refs[-1].dtype)


def run_total(parts, after):
    shape = parts.shape[1:]
    return pl.pallas_call(
        total_kernel,
        grid=(1,),
        in_specs=[whole(parts.shape)] + [pl.BlockSpec(memory_space=pl.ANY)] * len(after),
        out_specs=whole(shape),
        out_shape=jax.ShapeDtypeStruct(shape, bf16),
        compiler_params=pltpu.CompilerParams(vmem_limit_bytes=16 << 20),
        cost_estimate=LIGHT,
        name="total",
    )(parts, *after)


def owned_kernel(parts_ref, *refs):
    outs = refs[-9:]
    key_ref, value_ref, attn_ref, query_gain_ref, key_gain_ref = outs[:5]
    out_ref, router_ref, ffn_ref, query_ref = outs[5:]
    kv_width, width, q_width = key_ref.shape[1], out_ref.shape[1], query_ref.shape[1]
    experts = router_ref.shape[1]
    rows = parts_ref.shape[1]
    total = parts_ref[0].astype(f32)
    for n in range(1, parts_ref.shape[0]):
        total = total + parts_ref[n].astype(f32)
    run = lanes_like((rows, 128)) // 32

    def gathered(base, sources):
        made = None
        for j, (block, place) in enumerate(sources):
            at = base + block * 128
            piece = total[:, at : at + 128]
            if place != j:
                piece = pltpu.roll(piece, (j - place) % 4 * 32, 1)
            made = piece if made is None else jnp.where(run == j, piece, made)
        return made

    for block in range(kv_width // 128):
        sources = []
        for j in range(4):
            head, half = 2 * block + j // 2, j % 2
            sources.append((head // 4 * 2 + half, head % 4))
        key_ref[:, block * 128 : (block + 1) * 128] = gathered(0, sources)
    at = kv_width
    value_ref[...] = total[:, at : at + kv_width]
    at += kv_width
    extra = total[:, at : at + 128]
    at += 128
    turned = jnp.concatenate([extra, jnp.zeros((128 - rows, 128), f32)], axis=0).T
    attn_ref[...] = turned[0:1, :rows]
    query_gain_ref[...] = extra[0:1, 64:]
    key_gain_ref[...] = extra[1:2, 64:]
    out_ref[...] = total[:, at : at + width]
    at += width
    tail = total[:, at : at + 128]
    at += 128
    router_ref[...] = tail[:, :experts]
    turned = jnp.concatenate([tail, jnp.zeros((128 - rows, 128), f32)], axis=0).T
    ffn_ref[...] = turned[experts : experts + 1, :rows]
    for block in range(q_width // 128):
        sources = []
        for j in range(4):
            r, half = j // 2, j % 2
            sources.append((r * (q_width // 256) + block // 4 * 2 + half, block % 4))
        query_ref[:, block * 128 : (block + 1) * 128] = gathered(at, sources)


def run_owned(parts, width, q_width, head_size, experts, after):
    rows = parts.shape[1]
    kv_width = q_width // 2
    shapes = [
        (rows, kv_width), (rows, kv_width), (1, rows), (1, head_size), (1, head_size),
        (rows, width), (rows, experts), (1, rows), (rows, q_width),
    ]
    return pl.pallas_call(
        owned_kernel,
        grid=(1,),
        in_specs=[whole(parts.shape)] + [pl.BlockSpec(memory_space=pl.ANY)] * len(after),
        out_specs=[whole(shape) for shape in shapes],
        out_shape=[jax.ShapeDtypeStruct(shape, f32) for shape in shapes],
        compiler_params=pltpu.CompilerParams(vmem_limit_bytes=8 << 20),
        cost_estimate=LIGHT,
        name="owned",
    )(parts, *after)


def add_low(left, right, each, after=()):
    block = pl.BlockSpec((each,) + left.shape[1:], lambda i: (i,) + (0,) * (left.ndim - 1))
    return pl.pallas_call(
        add_kernel,
        grid=(left.shape[0] // each,),
        in_specs=[block, block] + [pl.BlockSpec(memory_space=pl.ANY)] * len(after),
        out_specs=block,
        out_shape=jax.ShapeDtypeStruct(left.shape, bf16),
        compiler_params=pltpu.CompilerParams(vmem_limit_bytes=16 << 20),
        cost_estimate=LIGHT,
        name="add_low",
    )(left, right, *after)


def fetch(sources, targets, sems):
    copies = [
        pltpu.make_async_copy(source, target, sems.at[n])
        for n, (source, target) in enumerate(zip(sources, targets))
    ]
    for copy in copies:
        copy.start()
    return copies


def middle_back_kernel(score_scale, m, count, *refs):
    sources = refs[:count]
    buffers, sems = refs[-count - 1 : -1], refs[-1]
    outs = refs[-count - 8 : -count - 1]
    mid_grad_ref, branch_ref, router_grad_ref, query_grad_ref, own_grad_ref = outs[:5]
    one_grad_ref, two_grad_ref = outs[5:]
    dense = sources[0]
    width = dense.shape[0]
    out_columns = dense.at[:, pl.ds(2 * width, width)]
    by_micro = tuple(source.at[m] for source in sources[2:7])
    copies = fetch((out_columns, sources[1], *by_micro, *sources[7:]), buffers, sems)
    out_weights_ref, turned_ref, member_ref, seed_ref, query_ref, key_value_ref, bias_ref = buffers[:7]
    parts_ref, moe_ref, middle_ref, peak_ref = buffers[7:11]
    rows, q_width = query_ref.shape
    kv_width = key_value_ref.shape[1] // 2
    groups = kv_width // 256
    experts = member_ref.shape[0]
    low_half = lanes_like((rows, 128)) < 64
    low_rows = lanes_like((3 * rows, 128)) < 64
    lane = lanes_like((1, 256)) % 128 // 32
    q_half = q_width // 2
    for n in (1, 2, 3, 7, 8, 9, 10):
        copies[n].wait()
    router = turned_ref[:experts, :].astype(bf16)
    senders = parts_ref.shape[0]
    moe_in = moe_ref[...]
    member = member_ref[...] > 0.5
    shown = jnp.where(member, product_nt(router, moe_in), -1e30)
    exps = jnp.where(member, jnp.exp(shown - jnp.max(shown, axis=0, keepdims=True)), 0.0)
    gates = exps / jnp.sum(exps, axis=0, keepdims=True)
    gate_grad = []
    for s in range(senders):
        row = parts_ref[s, rows:, :].astype(f32)
        row = row[0:1] + row[1:2]
        for j in range(experts // senders):
            gate_grad.append(row[:, j * rows : (j + 1) * rows])
    gate_grad = jnp.concatenate(gate_grad, axis=0)
    logit_grad = gates * (gate_grad - jnp.sum(gates * gate_grad, axis=0, keepdims=True))
    logit_grad = logit_grad.astype(bf16)
    moe_grad = product_tn(logit_grad, router)
    for s in range(senders):
        moe_grad = moe_grad + parts_ref[s, :rows, :].astype(f32)
    middle = middle_ref[...]
    scale = rms_scale(middle)
    router_grad_ref[:experts, :] = product(logit_grad, moe_in)
    router_grad_ref[experts : experts + 1, :] = jnp.sum(
        moe_grad * middle * scale, axis=0, keepdims=True
    )
    mid_grad = seed_ref[...].astype(f32) + norm_back(
        moe_grad * turned_ref[32:33, :], middle, scale
    )
    mid_grad_ref[...] = mid_grad
    branch = mid_grad.astype(bf16)
    branch_ref[...] = branch
    for n in (0, 4, 5, 6):
        copies[n].wait()
    attended_grad = product_nt(branch, out_weights_ref[...]).astype(bf16)

    bias = bias_ref[...]
    values = key_value_ref[:, kv_width:].astype(f32)

    def store(columns, gradient):
        two_grad_ref[:, columns] = gradient[:rows].astype(bf16)
        one_grad_ref[:, columns] = gradient[rows : 2 * rows].astype(bf16)
        own_grad_ref[:, columns] = gradient[2 * rows :]

    for g in range(groups):
        keys = key_value_ref[:, g * 256 : (g + 1) * 256]
        stack = group_stack(query_ref, g, q_half)
        scores = group_scores(keys, stack, bias, score_scale)
        probs = jnp.exp(scores - peak_ref[g : g + 1, :])
        probs_low = probs.astype(bf16)
        prob_grads, value_grads = [], []
        for i in range(4):
            h = 4 * g + i
            block = attended_grad[:, h * 128 : (h + 1) * 128]
            zero = jnp.zeros_like(block)
            masked = jnp.concatenate(
                [jnp.where(low_half, block, zero), jnp.where(low_half, zero, block)], axis=0
            )
            prob_grads.append(product_nt(doubled_values(values, h), masked))
            both = product(probs_low[:, i * 256 : (i + 1) * 256], masked)
            value_grads.append(both + pltpu.roll(both, 64, 1))
        prob_grad = jnp.concatenate(prob_grads, axis=1)
        inner = jnp.sum(probs * prob_grad, axis=0, keepdims=True)
        score_low = (score_scale * probs * (prob_grad - inner)).astype(bf16)
        for pair in range(2):
            merged = jnp.where(low_rows, value_grads[2 * pair], value_grads[2 * pair + 1])
            at = kv_width + (2 * g + pair) * 128
            store(slice(at, at + 128), merged)
        store(slice(g * 256, (g + 1) * 256), product(score_low, stack))
        spread_grad = product_tn(score_low, keys)
        for r in range(2):
            total = jnp.zeros((rows, 256), f32)
            for i in range(4):
                at = (2 * i + r) * rows
                total = jnp.where(lane == i, spread_grad[at : at + rows], total)
            at = r * q_half + g * 256
            query_grad_ref[:, at : at + 256] = total


def run_middle_back(
    m, parts, member, seeds, query, key_value, bias, moe_in, middle, peak, dense, turned,
    score_scale, after,
):
    micro, rows, width = seeds.shape
    q_width = query.shape[2]
    shapes = [
        ((rows, width), f32),
        ((rows, width), bf16),
        ((40, width), f32),
        ((rows, q_width), f32),
        ((rows, q_width), f32),
        ((rows, q_width), bf16),
        ((rows, q_width), bf16),
    ]
    by_micro = (member, seeds, query, key_value, bias)
    ins = (dense, turned, *by_micro, parts, moe_in, middle, peak)
    held = (
        [pltpu.VMEM((width, width), bf16), pltpu.VMEM(turned.shape, f32)]
        + [pltpu.VMEM(a.shape[1:], a.dtype) for a in by_micro]
        + [pltpu.VMEM(a.shape, a.dtype) for a in ins[7:]]
    )
    count = len(ins)
    return pl.pallas_call(
        functools.partial(middle_back_kernel, score_scale, m, count),
        grid=(1,),
        in_specs=[pl.BlockSpec(memory_space=pl.ANY)] * (count + len(after)),
        out_specs=[whole(shape) for shape, _ in shapes],
        out_shape=[jax.ShapeDtypeStruct(shape, kind) for shape, kind in shapes],
        scratch_shapes=held + [pltpu.SemaphoreType.DMA((count,))],
        compiler_params=pltpu.CompilerParams(vmem_limit_bytes=VMEM),
        cost_estimate=LIGHT,
        name="middle_back",
    )(*ins, *after)


def by_core(core_ref, values, kept_ref, sent_ref, at):
    halves, depth = kept_ref.shape[0], kept_ref.shape[1]
    pairs = values.reshape(halves, 2, depth, values.shape[1])
    columns = pl.ds(at, values.shape[1])

    @pl.when(core_ref[0] == 0)
    def even():
        kept_ref[:, :, columns] = pairs[:, 0]
        sent_ref[:, :, columns] = pairs[:, 1]

    @pl.when(core_ref[0] == 1)
    def odd():
        kept_ref[:, :, columns] = pairs[:, 1]
        sent_ref[:, :, columns] = pairs[:, 0]


def head_back(u1, u2, up1, up2, cosine, sine, gain1, gain2, head_size):
    back1 = up1 * cosine + up2 * sine
    back2 = up2 * cosine - up1 * sine
    scale = lax.rsqrt(head_sums(u1 * u1 + u2 * u2) / head_size + EPSILON)
    sum1 = jnp.sum(back1 * u1 * scale, axis=0, keepdims=True)
    sum2 = jnp.sum(back2 * u2 * scale, axis=0, keepdims=True)
    back1 = back1 * gain1
    back2 = back2 * gain2
    mean = head_sums(back1 * u1 + back2 * u2) / head_size
    cube = scale * scale * scale
    low1 = (scale * back1 - u1 * cube * mean).astype(bf16)
    low2 = (scale * back2 - u2 * cube * mean).astype(bf16)
    return low1, low2, sum1, sum2


def query_back_kernel(
    head_size, micro, core_ref, pre_ref, normed_ref, cosine_ref, sine_ref, gains_ref, weights_ref,
    *refs,
):
    query_grads, attended, branch, router = [refs[n * micro : (n + 1) * micro] for n in range(4)]
    kept_ref, sent_ref, normed_grad_ref, sums_ref, low, held_ref, sem = refs[-7:]
    width = held_ref.shape[0]
    taken = weights_ref.at[:, pl.ds(0, held_ref.shape[1])]
    loading = pltpu.make_async_copy(taken, held_ref, sem)
    loading.start()
    _, rows, width = normed_ref.shape
    q_width = query_grads[0].shape[1]
    base = kept_ref.shape[2] - q_width
    first = base - width - 128
    out_grad = sum(product_tn(a[...], b[...]) for a, b in zip(attended, branch))
    by_core(core_ref, out_grad.astype(bf16), kept_ref, sent_ref, first)
    tail = sum(r[...] for r in router)
    tail = jnp.concatenate([tail, jnp.zeros((128 - tail.shape[0], width), f32)], axis=0)
    by_core(core_ref, tail.T.astype(bf16), kept_ref, sent_ref, first + width)
    sums = [jnp.zeros((1, 128), f32) for _ in range(2)]
    for m in range(micro):
        at_rows = pl.ds(m * rows, rows)
        for at in range(0, q_width, 256):
            low1, low2, sum1, sum2 = head_back(
                pre_ref[m, :, at : at + 128], pre_ref[m, :, at + 128 : at + 256],
                query_grads[m][:, at : at + 128], query_grads[m][:, at + 128 : at + 256],
                cosine_ref[...], sine_ref[...], gains_ref[0:1, :], gains_ref[1:2, :], head_size,
            )
            low[at_rows, at : at + 128] = low1
            low[at_rows, at + 128 : at + 256] = low2
            sums = [sums[0] + sum1, sums[1] + sum2]
    sums_ref[...] = jnp.concatenate(sums + [jnp.zeros((6, 128), f32)], axis=0)
    normed = jnp.concatenate([normed_ref[m] for m in range(micro)], axis=0)
    for at in range(0, q_width, 512):
        grad = product_tn(normed, low[:, at : at + 512]).astype(bf16)
        by_core(core_ref, grad, kept_ref, sent_ref, base + at)
    loading.wait()
    normed_grad_ref[...] = product_nt(low[...], held_ref[...])


def last_rows(array, rows):
    block = array.shape[0] // rows - 1
    return pl.BlockSpec((rows, array.shape[1]), lambda *_: (block, 0))


def run_query_back(
    core, owners, pre, normed, cosine, sine, gains, dense, query_grads, attended, branch, router,
    head_size, after,
):
    micro, rows, width = normed.shape
    q_width = query_grads[0].shape[1]
    shape = (owners // 2, width // owners, q_width + 128 + width + 128 + q_width)
    out = jax.ShapeDtypeStruct(shape, bf16)
    ins = (pre, normed, cosine, sine, gains)
    rest = (*query_grads, *attended, *branch, *router)
    return pl.pallas_call(
        functools.partial(query_back_kernel, head_size, micro),
        grid=(1,),
        in_specs=[pl.BlockSpec(memory_space=pltpu.SMEM)]
        + [whole(pre.shape), whole(normed.shape), last_rows(cosine, rows), last_rows(sine, rows)]
        + [whole(gains.shape)]
        + [pl.BlockSpec(memory_space=pl.ANY)]
        + [whole(a.shape) for a in rest]
        + [pl.BlockSpec(memory_space=pl.ANY)] * len(after),
        out_specs=[whole(shape), whole(shape), whole((micro * rows, width)), whole((8, 128))],
        out_shape=[
            out,
            out,
            jax.ShapeDtypeStruct((micro * rows, width), f32),
            jax.ShapeDtypeStruct((8, 128), f32),
        ],
        scratch_shapes=[
            pltpu.VMEM((micro * rows, q_width), bf16),
            pltpu.VMEM((width, q_width), bf16),
            pltpu.SemaphoreType.DMA,
        ],
        compiler_params=pltpu.CompilerParams(vmem_limit_bytes=VMEM),
        cost_estimate=LIGHT,
        name="query_back",
    )(core, *ins, dense, *rest, *after)


def tokens_back_kernel(
    head_size, micro, core_ref, pre_ref, normed_ref, tokens_ref, cosine_ref, sine_ref, gains_ref,
    weights_ref, turned_ref, normed_grad_ref, sums_ref, *refs,
):
    kept_ref, sent_ref, tokens_grad_ref, low, held_ref, sem = refs[-6:]
    wide = held_ref.shape[1]
    loading = pltpu.make_async_copy(weights_ref.at[:, pl.ds(wide, wide)], held_ref, sem)
    loading.start()
    own_grads, mid_grads = refs[:micro], refs[micro : 2 * micro]
    ones, twos = refs[2 * micro : 3 * micro], refs[3 * micro : 4 * micro]
    _, rows, width = normed_ref.shape
    kv_width = own_grads[0].shape[1] // 2
    q_width = pre_ref.shape[2] - kv_width
    sums = [jnp.zeros((1, 128), f32) for _ in range(2)]
    for m in range(micro):
        at_rows = pl.ds(m * rows, rows)

        def upstream(start, size):
            columns = pl.ds(start, size)
            return (
                own_grads[m][:, columns]
                + ones[m][:, columns].astype(f32)
                + twos[m][:, columns].astype(f32)
            )

        low[at_rows, kv_width:] = upstream(kv_width, kv_width).astype(bf16)
        for at in range(0, kv_width, 256):
            from_pre = q_width + at
            low1, low2, sum1, sum2 = head_back(
                pre_ref[m, :, from_pre : from_pre + 128],
                pre_ref[m, :, from_pre + 128 : from_pre + 256],
                upstream(at, 128), upstream(at + 128, 128),
                cosine_ref[...], sine_ref[...], gains_ref[2:3, :], gains_ref[3:4, :], head_size,
            )
            low[at_rows, at : at + 128] = low1
            low[at_rows, at + 128 : at + 256] = low2
            sums = [sums[0] + sum1, sums[1] + sum2]
    normed = jnp.concatenate([normed_ref[m] for m in range(micro)], axis=0)
    for at in range(0, low.shape[1], 512):
        grad = product_tn(normed, low[:, at : at + 512]).astype(bf16)
        by_core(core_ref, grad, kept_ref, sent_ref, at)
    loading.wait()
    normed_grad = normed_grad_ref[...] + product_nt(low[...], held_ref[...])
    gain = turned_ref[33:34, :]
    gain_grad = jnp.zeros((1, width), f32)
    for m in range(micro):
        x = tokens_ref[m].astype(f32)
        scale = rms_scale(x)
        part = normed_grad[m * rows : (m + 1) * rows]
        gain_grad = gain_grad + jnp.sum(part * x * scale, axis=0, keepdims=True)
        tokens_grad_ref[m] = (mid_grads[m][...] + norm_back(part * gain, x, scale)).astype(bf16)
    folded = []
    for total in [sums_ref[0:1, :], sums_ref[1:2, :]] + sums:
        total = total + pltpu.roll(total, 64, 1)
        folded.append(total + pltpu.roll(total, 32, 1))
    lane = lanes_like((1, 128))
    query_row = jnp.where(lane < 96, folded[0], folded[1])
    key_row = jnp.where(lane < 96, folded[2], folded[3])
    column = jnp.concatenate([gain_grad, jnp.zeros((127, width), f32)], axis=0).T
    row = lax.broadcasted_iota(jnp.int32, (width, 128), 0)
    extra = jnp.where(
        lanes_like((width, 128)) < 64, column, jnp.where(row % 2 == 0, query_row, key_row)
    )
    by_core(core_ref, extra.astype(bf16), kept_ref, sent_ref, low.shape[1])


def run_tokens_back(
    core, pre, normed, tokens, cosine, sine, gains, dense, turned, normed_grad, sums,
    own_grads, mid_grads, ones, twos, kept, sent, head_size, after,
):
    micro, rows, width = tokens.shape
    wide = own_grads[0].shape[1]
    shape = kept.shape[:2] + (wide + 128,)
    ins = (pre, normed, tokens, cosine, sine, gains)
    rest = (turned, normed_grad, sums, *own_grads, *mid_grads, *ones, *twos)
    return pl.pallas_call(
        functools.partial(tokens_back_kernel, head_size, micro),
        grid=(1,),
        in_specs=[pl.BlockSpec(memory_space=pltpu.SMEM)]
        + [whole(pre.shape), whole(normed.shape), whole(tokens.shape)]
        + [last_rows(cosine, rows), last_rows(sine, rows), whole(gains.shape)]
        + [pl.BlockSpec(memory_space=pl.ANY)]
        + [whole(a.shape) for a in rest]
        + [pl.BlockSpec(memory_space=pl.ANY)] * (2 + len(after)),
        out_specs=[whole(shape), whole(shape), whole(tokens.shape)],
        out_shape=[
            jax.ShapeDtypeStruct(kept.shape, bf16),
            jax.ShapeDtypeStruct(kept.shape, bf16),
            jax.ShapeDtypeStruct(tokens.shape, bf16),
        ],
        input_output_aliases={2 + len(ins) + len(rest): 0, 3 + len(ins) + len(rest): 1},
        scratch_shapes=[
            pltpu.VMEM((micro * rows, wide), bf16),
            pltpu.VMEM((width, wide), bf16),
            pltpu.SemaphoreType.DMA,
        ],
        compiler_params=pltpu.CompilerParams(vmem_limit_bytes=VMEM),
        cost_estimate=LIGHT,
        name="tokens_back",
    )(core, *ins, dense, *rest, kept, sent, *after)


def body(
    tokens,
    cotangent,
    routes,
    doc_lengths,
    valid,
    attn_gain,
    w_query,
    w_key,
    w_value,
    query_gain,
    key_gain,
    w_out,
    ffn_gain,
    w_router,
    w_gate,
    w_up,
    w_down,
):
    micro = tokens.shape[0]
    rows = tokens.shape[2]
    width = tokens.shape[3]
    head_size = query_gain.shape[0]
    q_width = w_query.shape[1]
    kv_width = w_key.shape[1]
    kv_heads = kv_width // head_size
    q_heads = q_width // head_size
    group_size = q_heads // kv_heads
    experts = w_router.shape[1]
    local = w_gate.shape[0]
    hidden_width = w_gate.shape[2]
    upper = w_gate.shape[1]
    expert_devices = lax.axis_size("expert")
    dp_devices = lax.axis_size("dp")
    own_rows = w_query.shape[0]
    reach_back = (WINDOW + rows - 2) // rows
    key_rows = rows * (reach_back + 1)
    score_scale = 1.0 / math.sqrt(head_size)
    q_gain = query_gain.astype(f32)
    k_gain = key_gain.astype(f32)
    all_rows = micro * rows
    qkv_width = q_width + 2 * kv_width

    tiles = 128 // (head_size // 2)
    halves = dp_devices // 2
    core = lax.axis_index("dp") % 2
    core_flag = core[None].astype(jnp.int32)
    expert_index = lax.axis_index("expert")
    across, depth = expert_index % 2, expert_index // 2
    across_flag, depth_flag = across[None].astype(jnp.int32), depth[None].astype(jnp.int32)
    other_core = [(i, i ^ 1) for i in range(dp_devices)]
    other_across = [(i, i ^ 1) for i in range(expert_devices)]
    along_depth = [[2 * z + x for z in range(expert_devices // 2)] for x in range(2)]

    groups = kv_heads // 4
    half_size = head_size // 2
    query_cols = w_query.reshape(own_rows, groups, 4, group_size, 2, half_size)
    query_cols = query_cols.transpose(0, 3, 1, 4, 2, 5).reshape(own_rows, q_width)
    key_cols = w_key.reshape(own_rows, groups, 4, 2, half_size)
    key_cols = key_cols.transpose(0, 1, 3, 2, 4).reshape(own_rows, kv_width)
    tail = jnp.concatenate(
        [
            w_router,
            ffn_gain[:, None],
            attn_gain[:, None],
            jnp.zeros((own_rows, 128 - experts - 2), bf16),
        ],
        axis=1,
    )
    route_cols = routes[:, 0].astype(bf16).reshape(own_rows, -1)
    packed = jnp.concatenate([query_cols, key_cols, w_value, w_out, tail, route_cols], axis=1)
    packed = spread(packed, "expert")
    dense_width = packed.shape[2] - route_cols.shape[1]
    routes_all = packed[:, :, dense_width:].astype(jnp.int32)
    routes_all = routes_all.reshape((expert_devices,) + routes.shape[:1] + routes.shape[2:])
    seed_low = cotangent[:, 0] * valid[:, 0][:, :, None].astype(bf16)
    seed_other = lax.ppermute(seed_low, "expert", other_across)
    x_low = tokens[:, 0]
    one = passed_along(x_low, "expert", 1)
    two = passed_along(x_low, "expert", 2)
    weights = jnp.concatenate([jnp.concatenate([w_gate, w_up], axis=2), w_down], axis=1)
    weights = lax.all_gather(weights, "dp", axis=1)
    dense = run_pack(packed, dense_width, (seed_other,))
    dense = lax.all_gather(dense, "dp", axis=0, tiled=True)

    def by_depth(values, other, after=()):
        pair = run_pair(across_flag, values, other, expert_devices // 2, after)
        return lax.all_to_all(pair, "expert", 0, 0, axis_index_groups=along_depth)

    seed_all = by_depth(seed_low, seed_other, (one, two))
    expert_ids = jnp.arange(experts, dtype=jnp.int32)
    member_all = jnp.any(routes_all[..., None] == expert_ids, axis=3)
    member_turned = jnp.roll(member_all, -expert_index * local, axis=3).transpose(1, 0, 3, 2)
    member = member_turned[:, :, :local]
    earlier = (
        jnp.arange(rows, dtype=jnp.int32)[:, None] < jnp.arange(rows, dtype=jnp.int32)[None, :]
    ).astype(bf16)
    rank = einsum("mbjt,tu->mbju", member.astype(bf16), earlier).astype(jnp.int32)
    slots = jnp.where(member, rank, -1)
    turned_slots = slots.transpose(0, 1, 3, 2)
    member_turned = member_turned.astype(f32)
    own_member = jnp.any(routes[:, 0, :, :, None] == expert_ids, axis=2)
    own_member = own_member.transpose(0, 2, 1).astype(f32)

    q_pos = expert_index * rows + jnp.arange(rows, dtype=jnp.int32)
    k_pos = (expert_index - reach_back) * rows + jnp.arange(key_rows, dtype=jnp.int32)
    cosine, sine = rope_tables(k_pos, head_size)
    cosine = jnp.tile(cosine[:, :half_size], (1, tiles))
    sine = jnp.tile(sine[:, :half_size], (1, tiles))
    bounds = jnp.cumsum(doc_lengths[:, 0], axis=1)
    q_doc = jnp.sum((q_pos[None, :, None] >= bounds[:, None, :]).astype(jnp.int32), axis=2)
    k_doc = jnp.sum((k_pos[None, :, None] >= bounds[:, None, :]).astype(jnp.int32), axis=2)
    offset = q_pos[None, :] - k_pos[:, None]
    visible = (
        (k_pos[None, :, None] >= 0)
        & (q_doc[:, None, :] == k_doc[:, :, None])
        & (offset >= 0)[None]
        & (offset < WINDOW)[None]
    )
    bias = jnp.where(visible, 0.0, -1e30).astype(f32)
    head_gains = jnp.stack(
        [
            jnp.tile(part, tiles)
            for part in (
                q_gain[:half_size],
                q_gain[half_size:],
                k_gain[:half_size],
                k_gain[half_size:],
            )
        ]
        + [jnp.zeros((128,), f32)] * 4
    )

    result = run_front(
        x_low, one, two, dense, cosine, sine, head_gains, bias, head_size, q_width, ()
    )
    normed, pre, query, key_value, turned = result[:5]
    attended, middle, moe_in, peak = [result[5 + n :: 4] for n in range(4)]

    router_turned = jnp.roll(turned[:experts], -expert_index * local, axis=0).astype(bf16)
    saved, backs, mixed = [], [], []
    moe_all = [
        by_depth(
            moe_in[m],
            lax.ppermute(moe_in[m], "expert", other_across),
            (slots, turned_slots, member_turned, own_member, router_turned) if m == 0 else (),
        ).reshape(expert_devices, rows, width)
        for m in range(micro)
    ]
    for m in range(micro):
        back_part, arrived, out_rows, hidden, pre_low, mixed_rows = run_experts(
            m, moe_all[m], seed_all, slots, turned_slots, member_turned, router_turned, weights,
            tuple(mixed),
        )
        saved.append((arrived, out_rows, hidden, pre_low))
        backs.append(lax.all_to_all(back_part, "expert", 0, 0))
        mixed.append(mixed_rows)
    sent = weight_grads(core_flag, dp_devices, saved, (), ())
    received = [lax.ppermute(piece, "dp", other_core) for piece in sent]
    combined = run_combine(depth_flag, mixed, turned_slots, (sent[0], backs[0]))
    core_sum = weight_grads(core_flag, dp_devices, saved, received, (combined[0],))

    made, ones, twos = [], [], []
    for m in range(micro):
        result = run_middle_back(
            m, backs[m], own_member, seed_low, query, key_value, bias, moe_in[m], middle[m],
            peak[m], dense, turned, score_scale, (core_sum,),
        )
        if m == 0:
            core_sum = pass_on(core_sum, (*backs, result[0]))
        made.append(result[:5])
        ones.append(passed_along(result[5], "expert", -1))
        twos.append(passed_along(result[6], "expert", -2))
    mid_grads, branches, router_grads, query_grads, own_grads = zip(*made)
    across_low = lax.axis_index("dp") // 2 % 2
    place_flag = across_low[None].astype(jnp.int32)
    along_y = [[4 * y + place for y in range(dp_devices // 4)] for place in range(4)]
    over_y = lax.psum_scatter(
        core_sum.reshape((dp_devices // 4, 2, 2) + core_sum.shape[1:]),
        "dp",
        scatter_dimension=0,
        axis_index_groups=along_y,
    )
    over_y = over_y.reshape(over_y.shape[-5:])
    pieces = run_choose(place_flag, core_flag, over_y)
    exchanged = [
        lax.ppermute(piece, "dp", [(i, i ^ step) for i in range(dp_devices)])
        for piece, step in zip(pieces, (2, 1, 3))
    ]
    gate_owned, up_owned, down_owned = run_expert_owned(
        place_flag, core_flag, over_y, exchanged, upper, hidden_width
    )

    up = [(i, (i + 2) % expert_devices) for i in range(expert_devices)]
    down = [(i, (i - 2) % expert_devices) for i in range(expert_devices)]
    out_low = lax.ppermute(combined[2], "expert", up)
    out_high = lax.ppermute(combined[3], "expert", up)

    kept_in, sent_in, normed_grad, gain_sums = run_query_back(
        core_flag, dp_devices, pre, normed, cosine, sine, head_gains, dense, query_grads, attended,
        branches, router_grads, head_size, (out_low, ones[0], twos[0]),
    )
    kept_in, sent_in, token_grad = run_tokens_back(
        core_flag, pre, normed, x_low, cosine, sine, head_gains, dense, turned, normed_grad,
        gain_sums, own_grads, mid_grads, ones, twos, kept_in, sent_in, head_size,
        (out_high,),
    )
    both = add_low(kept_in, lax.ppermute(sent_in, "dp", other_core), 4)
    parts = both.reshape(dp_devices // 4, 2 * both.shape[1], both.shape[2])
    parts = lax.all_to_all(parts, "dp", 0, 0, axis_index_groups=along_y)

    next_part = run_merge((combined[1], out_low, out_high), (both,))
    out_parts = [
        combined[0],
        lax.ppermute(next_part, "expert", up),
        lax.ppermute(combined[4], "expert", down),
    ]
    total = run_total(parts, (gate_owned,))
    out_kept, out_sent = run_fold(across_flag, middle, out_parts, (total,))
    out_other = lax.ppermute(out_sent, "expert", other_across)

    output = add_low(out_kept, out_other, micro, (total,))
    parts = total.reshape(2 * expert_devices, own_rows, -1)
    same_y = [
        [
            ((2 * y + place) * 2 + c) * expert_devices + e
            for place in range(2)
            for e in range(expert_devices)
        ]
        for y in range(dp_devices // 4)
        for c in range(2)
    ]
    parts = lax.all_to_all(parts, ("dp", "expert"), 0, 0, axis_index_groups=same_y)
    (
        key_owned, value_owned, attn_gain_owned, query_gain_owned, key_gain_owned,
        out_owned, router_owned, ffn_gain_owned, query_owned,
    ) = run_owned(parts, width, q_width, head_size, experts, (exchanged[0],))
    return (
        output.reshape(micro, 1, rows, width),
        token_grad.reshape(micro, 1, rows, width),
        attn_gain_owned.reshape(own_rows),
        query_owned,
        key_owned,
        value_owned,
        query_gain_owned.reshape(head_size),
        key_gain_owned.reshape(head_size),
        out_owned,
        ffn_gain_owned.reshape(own_rows),
        router_owned,
        gate_owned,
        up_owned,
        down_owned,
    )


def solution(mesh):
    rows_spec = P(("dp", "expert"), None)
    gain_spec = P(("dp", "expert"))
    token_spec = P(None, "dp", "expert", None)
    expert_spec = P("expert", "dp", None)
    return jax.shard_map(
        body,
        mesh=mesh,
        in_specs=(
            token_spec,
            token_spec,
            token_spec,
            P(None, "dp", None),
            P(None, "dp", "expert"),
            gain_spec,
            rows_spec,
            rows_spec,
            rows_spec,
            P(),
            P(),
            rows_spec,
            gain_spec,
            rows_spec,
            expert_spec,
            expert_spec,
            expert_spec,
        ),
        out_specs=(
            token_spec,
            token_spec,
            gain_spec,
            rows_spec,
            rows_spec,
            rows_spec,
            P(),
            P(),
            rows_spec,
            gain_spec,
            rows_spec,
            expert_spec,
            expert_spec,
            expert_spec,
        ),
        check_vma=False,
    )
```
